32 devices in a mesh: dp: 4 (over y, core), fsdp: 8 (over z, x).
Axes of the slice: x: 2, y: 2, z: 4, core: 2. Of those that a mesh axis runs over, the one named last changes fastest.
Arguments:
- dec_in: bfloat16 [2, 32, 128, 768], P(None, ('dp', 'fsdp')), may hold values from -6 to 6
- enc_out: bfloat16 [2, 32, 512, 768], P(None, ('dp', 'fsdp')), may hold values from -6 to 6
- dec_len: int32 [2, 32], P(None, ('dp', 'fsdp')), may hold values from 1 to 114, as said below
- enc_len: int32 [2, 32], P(None, ('dp', 'fsdp')), may hold values from 32 to 512, as said below
- cotangent: bfloat16 [2, 32, 128, 768], P(None, ('dp', 'fsdp')), may hold values from -6 to 6
- norm_self: bfloat16 [768], P(('dp', 'fsdp')), may hold values from 0.5 to 1.5
- self_q: bfloat16 [768, 768], P(('dp', 'fsdp')), may hold values from -0.109375 to 0.109375
- self_k: bfloat16 [768, 768], P(('dp', 'fsdp')), may hold values from -0.109375 to 0.109375
- self_v: bfloat16 [768, 768], P(('dp', 'fsdp')), may hold values from -0.21875 to 0.21875
- self_o: bfloat16 [768, 768], P(('dp', 'fsdp')), may hold values from -0.625 to 0.625
- rel_bias: bfloat16 [32, 12], P('fsdp'), may hold values from -4 to 4
- norm_cross: bfloat16 [768], P(('dp', 'fsdp')), may hold values from 0.5 to 1.5
- cross_q: bfloat16 [768, 768], P(('dp', 'fsdp')), may hold values from -0.109375 to 0.109375
- cross_k: bfloat16 [768, 768], P(('dp', 'fsdp')), may hold values from -0.109375 to 0.109375
- cross_v: bfloat16 [768, 768], P(('dp', 'fsdp')), may hold values from -0.21875 to 0.21875
- cross_o: bfloat16 [768, 768], P(('dp', 'fsdp')), may hold values from -1.25 to 1.25
- norm_ffn: bfloat16 [768], P(('dp', 'fsdp')), may hold values from 0.5 to 1.5
- ffn_in: bfloat16 [768, 3072], P(('dp', 'fsdp')), may hold values from -0.21875 to 0.21875
- ffn_out: bfloat16 [3072, 768], P(('dp', 'fsdp')), may hold values from -0.15625 to 0.15625
Outputs:
- output: bfloat16 [2, 32, 128, 768], P(None, ('dp', 'fsdp'))
- grad_dec: bfloat16 [2, 32, 128, 768], P(None, ('dp', 'fsdp'))
- grad_enc: bfloat16 [2, 32, 512, 768], P(None, ('dp', 'fsdp'))
- grad_norm_self: float32 [768], P(('dp', 'fsdp'))
- grad_self_q: float32 [768, 768], P(('dp', 'fsdp'))
- grad_self_k: float32 [768, 768], P(('dp', 'fsdp'))
- grad_self_v: float32 [768, 768], P(('dp', 'fsdp'))
- grad_self_o: float32 [768, 768], P(('dp', 'fsdp'))
- grad_rel_bias: float32 [32, 12], P('fsdp')
- grad_norm_cross: float32 [768], P(('dp', 'fsdp'))
- grad_cross_q: float32 [768, 768], P(('dp', 'fsdp'))
- grad_cross_k: float32 [768, 768], P(('dp', 'fsdp'))
- grad_cross_v: float32 [768, 768], P(('dp', 'fsdp'))
- grad_cross_o: float32 [768, 768], P(('dp', 'fsdp'))
- grad_norm_ffn: float32 [768], P(('dp', 'fsdp'))
- grad_ffn_in: float32 [768, 3072], P(('dp', 'fsdp'))
- grad_ffn_out: float32 [3072, 768], P(('dp', 'fsdp'))
The draws below stay inside these ranges and needn't reach their ends.
Inputs may be any that keep to these rules, and one draw needn't show every extreme that they name: `dec_len`: every micro-batch has some target of exactly 114. `enc_len`: every micro-batch has some encoder input of exactly 512.
All inputs are finite; a program needn't handle non-finite values.
Results may differ from the reference program's by a relative error of at most 0.024.
The reference program's roundings to bfloat16 on the way count: a program that leaves them out, or rounds other values in their place, can miss the bound.
Values may be sent and summed in bfloat16 or wider, within the bound.
A program may use at most 256 MiB of HBM per device.

```python
import math
import jax
import jax.numpy as jnp
import numpy as np
from jax import lax

D = 768
H = 12
FF = 3072
NB = 32
TD = 128
DEC_MOST = 114
TE = 512
ENC_LEAST = 32
MB = 2
SEQS = 32


def draw_dec_len(key, part):
    key = jax.random.fold_in(key, 11)
    first_key, second_key, third_key = jax.random.split(key, 3)
    first_len = jax.random.randint(first_key, (MB, SEQS), 1, DEC_MOST + 1)
    second_len = jax.random.randint(second_key, (MB, SEQS), 1, DEC_MOST + 1)
    lengths = jnp.minimum(first_len, second_len)
    chosen = jax.random.randint(third_key, (MB,), 0, SEQS)
    lengths = lengths.at[jnp.arange(MB), chosen].set(DEC_MOST)
    return lengths.astype(jnp.int32)


def draw_enc_len(key, part):
    key = jax.random.fold_in(key, 23)
    first_key, second_key, third_key = jax.random.split(key, 3)
    first_len = jax.random.randint(first_key, (MB, SEQS), ENC_LEAST, TE + 1)
    second_len = jax.random.randint(second_key, (MB, SEQS), ENC_LEAST, TE + 1)
    lengths = jnp.minimum(first_len, second_len)
    chosen = jax.random.randint(third_key, (MB,), 0, SEQS)
    lengths = lengths.at[jnp.arange(MB), chosen].set(TE)
    return lengths.astype(jnp.int32)


def block_scale(stream_key, extent, shards, low, high):
    level = 1.0
    for axis_at, parts in shards:
        heights = jax.random.uniform(jax.random.fold_in(jax.random.fold_in(stream_key, 6), axis_at), (parts,), jnp.float32, low / len(shards), high / len(shards))
        level = level * jnp.repeat(jnp.exp(heights), extent[axis_at] // parts).reshape((-1,) + (1,) * (len(extent) - 1 - axis_at))
    return level


def noise(stream_key, shape, deviation, limit, pieces=(), held_as=jnp.bfloat16):
    loudness = block_scale(stream_key, shape, pieces, -0.22, 0.18) if pieces else 1.0
    result = jax.random.normal(stream_key, shape, jnp.float32) * deviation * loudness
    return jnp.minimum(jnp.maximum(result, -limit), limit).astype(held_as)


def setup_inputs(seed: int = 0) -> dict:
    key_list = jax.random.split(jax.random.key(seed), 20)
    dec_in = noise(key_list[0], (MB, SEQS, TD, D), 1.0, 6.0, ((1, 32),))
    enc_out = noise(key_list[1], (MB, SEQS, TE, D), 1.0, 6.0, ((1, 32),))
    dec_len = draw_dec_len(jax.random.fold_in(key_list[19], 71), 0)
    enc_len = draw_enc_len(jax.random.fold_in(key_list[19], 71), 0)
    cotangent = noise(key_list[4], (MB, SEQS, TD, D), 1.0, 6.0, ((1, 32),))
    norm_self = jnp.clip(1.0 + 0.1 * jax.random.normal(key_list[5], (D,), jnp.float32), 0.5, 1.5).astype(jnp.bfloat16)
    self_q = noise(key_list[6], (D, D), (4 * D) ** -0.5, 0.109375, ((0, 32),))
    self_k = noise(key_list[7], (D, D), (4 * D) ** -0.5, 0.109375, ((0, 32),))
    self_v = noise(key_list[8], (D, D), D ** -0.5, 0.21875, ((0, 32),))
    self_o = noise(key_list[9], (D, D), (D // 8) ** -0.5, 0.625, ((0, 32),))
    rel_bias = noise(key_list[10], (NB, H), 1.0, 4.0, ((0, 8),))
    norm_cross = jnp.clip(1.0 + 0.1 * jax.random.normal(key_list[11], (D,), jnp.float32), 0.5, 1.5).astype(jnp.bfloat16)
    cross_q = noise(key_list[12], (D, D), (4 * D) ** -0.5, 0.109375, ((0, 32),))
    cross_k = noise(key_list[13], (D, D), (4 * D) ** -0.5, 0.109375, ((0, 32),))
    cross_v = noise(key_list[14], (D, D), D ** -0.5, 0.21875, ((0, 32),))
    cross_o = noise(key_list[15], (D, D), (D // 32) ** -0.5, 1.25, ((0, 32),))
    norm_ffn = jnp.clip(1.0 + 0.1 * jax.random.normal(key_list[16], (D,), jnp.float32), 0.5, 1.5).astype(jnp.bfloat16)
    ffn_in = noise(key_list[17], (D, FF), D ** -0.5, 0.21875, ((0, 32),))
    ffn_out = noise(key_list[18], (FF, D), (FF // 2) ** -0.5, 0.15625, ((0, 32),))
    return {"dec_in": dec_in, "enc_out": enc_out, "dec_len": dec_len, "enc_len": enc_len, "cotangent": cotangent, "norm_self": norm_self, "self_q": self_q, "self_k": self_k, "self_v": self_v, "self_o": self_o, "rel_bias": rel_bias, "norm_cross": norm_cross, "cross_q": cross_q, "cross_k": cross_k, "cross_v": cross_v, "cross_o": cross_o, "norm_ffn": norm_ffn, "ffn_in": ffn_in, "ffn_out": ffn_out}


EPSILON = 1e-06
MASKED = -1000000000.0
bucket_reach = 128

@jax.custom_vjp
def low(v):
    return lax.optimization_barrier(v.astype(jnp.bfloat16)).astype(jnp.float32)

@jax.custom_vjp
def low_back(v):
    return v

def low_keep(v):
    return (low(v), None)

def low_pass(kept, grad):
    return (grad,)

def back_keep(v):
    return (v, None)

def back_low(kept, grad):
    return (low(grad),)
low.defvjp(low_keep, low_pass)
low_back.defvjp(back_keep, back_low)

def both_ways(values):
    return low(low_back(values))

def bucket_table(dec_slots, bucket_count):
    near_count = bucket_count // 2
    places = np.arange(dec_slots, dtype=np.int32)
    distance = np.maximum(places[:, None] - places[None, :], 0).astype(np.int32)
    edges = np.array([math.ceil(near_count * (bucket_reach / near_count) ** (level / near_count) - 1e-09) for level in range(1, near_count)], dtype=np.int32)
    far_bucket = near_count + np.sum((distance[:, :, None] >= edges[None, None, :]).astype(np.int32), axis=-1, dtype=np.int32)
    return np.where(distance < near_count, distance, far_bucket).astype(np.int32)

def rms_norm(values, gain_vec):
    return values * lax.rsqrt(lax.optimization_barrier(jnp.mean(values * values, axis=-1, keepdims=True)) + EPSILON) * gain_vec

def smooth(values):
    return jax.nn.gelu(values, approximate=True)

def dense(left_op, weight):
    return jnp.einsum('bsd,df->bsf', left_op, weight, precision=lax.Precision.HIGHEST)

def attend(queries, keys_in, values_in, bias_term, mask_in):
    scores = jnp.einsum('bqhe,bkhe->bhqk', queries, keys_in, precision=lax.Precision.HIGHEST)
    scores = low_back(scores + bias_term)
    scores = jnp.where(mask_in, scores, MASKED)
    row_top = lax.optimization_barrier(jnp.max(scores, axis=-1, keepdims=True))
    exp_terms = jnp.exp(scores - row_top)
    attn_probs = low(exp_terms / lax.optimization_barrier(jnp.sum(exp_terms, axis=-1, keepdims=True)))
    return both_ways(jnp.einsum('bhqk,bkhe->bqhe', attn_probs, values_in, precision=lax.Precision.HIGHEST))

def layer(dec_rows, enc_rows, weights, self_mask, cross_mask, buckets):
    norm_self, self_q, self_k, self_v, self_o, rel_bias, norm_cross, cross_q, cross_k, cross_v, cross_o, norm_ffn, ffn_in, ffn_out = weights
    model_width = dec_rows.shape[2]
    head_count = rel_bias.shape[1]
    head_size = model_width // head_count

    def split_heads(tensor):
        return tensor.reshape(tensor.shape[0], tensor.shape[1], head_count, head_size)

    def join_heads(tensor):
        return tensor.reshape(tensor.shape[0], tensor.shape[1], model_width)
    a_self = low(rms_norm(dec_rows, norm_self))
    q_self = both_ways(dense(a_self, self_q))
    k_self = both_ways(dense(a_self, self_k))
    v_self = both_ways(dense(a_self, self_v))
    bias_term = jnp.transpose(rel_bias[buckets], (2, 0, 1))[None]
    o_self = join_heads(attend(split_heads(q_self), split_heads(k_self), split_heads(v_self), bias_term, self_mask))
    y_self = dec_rows + low_back(dense(o_self, self_o))
    a_cross = low(rms_norm(y_self, norm_cross))
    q_cross = both_ways(dense(a_cross, cross_q))
    k_cross = both_ways(dense(enc_rows, cross_k))
    v_cross = both_ways(dense(enc_rows, cross_v))
    o_cross = join_heads(attend(split_heads(q_cross), split_heads(k_cross), split_heads(v_cross), 0.0, cross_mask))
    y_cross = y_self + low_back(dense(o_cross, cross_o))
    a_ffn = low(rms_norm(y_cross, norm_ffn))
    pre_act = low_back(dense(a_ffn, ffn_in))
    hidden = low(smooth(pre_act))
    return y_cross + low_back(dense(hidden, ffn_out))

def add_trees(first, second):
    return jax.tree.map(jnp.add, first, second)

def reference(dec_in, enc_out, dec_len, enc_len, cotangent, norm_self, self_q, self_k, self_v, self_o, rel_bias, norm_cross, cross_q, cross_k, cross_v, cross_o, norm_ffn, ffn_in, ffn_out):
    weights = tuple((w.astype(jnp.float32) for w in (norm_self, self_q, self_k, self_v, self_o, rel_bias, norm_cross, cross_q, cross_k, cross_v, cross_o, norm_ffn, ffn_in, ffn_out)))
    seq_total = dec_in.shape[0] * dec_in.shape[1]
    dec_slots = dec_in.shape[2]
    enc_slots = enc_out.shape[2]
    group_size = math.gcd(seq_total, max(1, 4096 // dec_slots))
    group_count = seq_total // group_size
    buckets = jnp.asarray(bucket_table(dec_slots, rel_bias.shape[0]), dtype=jnp.int32)
    places = jnp.arange(dec_slots, dtype=jnp.int32)
    enc_places = jnp.arange(enc_slots, dtype=jnp.int32)

    def regroup(tensor):
        return tensor.reshape((group_count, group_size) + tensor.shape[2:])

    def one_group(carry, batch_in):
        dec_rows, enc_rows, dec_lengths, enc_lengths, cot_rows = batch_in
        causal = places[None, :] <= places[:, None]
        self_mask = causal[None, None] & (places[None, None, None, :] < dec_lengths[:, None, None, None])
        cross_mask = enc_places[None, None, None, :] < enc_lengths[:, None, None, None]
        row_mask = (places[None, :] < dec_lengths[:, None]).astype(jnp.float32)

        def forward(dec_part, enc_part, weight_part):
            return layer(dec_part, enc_part, weight_part, self_mask, cross_mask, buckets)
        out_rows, pull_back = jax.vjp(forward, dec_rows.astype(jnp.float32), enc_rows.astype(jnp.float32), weights)
        g_dec, g_enc, g_weights = pull_back(cot_rows.astype(jnp.float32) * row_mask[:, :, None])
        return (add_trees(carry, g_weights), (out_rows.astype(jnp.bfloat16), g_dec.astype(jnp.bfloat16), g_enc.astype(jnp.bfloat16)))
    start = jax.tree.map(jnp.zeros_like, weights)
    grads, (out_all, dec_grads, enc_grads) = lax.scan(one_group, start, (regroup(dec_in), regroup(enc_out), regroup(dec_len), regroup(enc_len), regroup(cotangent)))
    return (out_all.reshape(dec_in.shape), dec_grads.reshape(dec_in.shape), enc_grads.reshape(enc_out.shape), grads[0], grads[1], grads[2], grads[3], grads[4], grads[5], grads[6], grads[7], grads[8], grads[9], grads[10], grads[11], grads[12], grads[13])
```

```python
import functools
import math

import jax
import jax.numpy as jnp
import numpy as np
from jax import lax
from jax.experimental import pallas as pl
from jax.experimental.pallas import tpu as pltpu
from jax.sharding import PartitionSpec as P

MESH = pl.DeviceIdType.MESH
NP = 8
ROWS = 48
COLS = 768
SIZE = {"y": 2, "z": 4, "x": 2}
AG_ORDERS = ["xyz", "zyx", "zxy", "zyx", "yxz", "zxy", "zyx", "zxy"]
RS_ORDERS = ["zxy", "xyz", "yxz", "xyz", "zyx", "yxz", "xyz", "yxz"]

class Place:
    def __init__(s):
        dp = lax.axis_index("dp"); f = lax.axis_index("fsdp")
        s.c = dp % 2; s.y = dp // 2; s.x = f % 2; s.z = f // 2
        s.pos = {"x": s.x, "y": s.y, "z": s.z}
    def dev(s, c=None, y=None, z=None, x=None):
        c = s.c if c is None else c; y = s.y if y is None else y
        z = s.z if z is None else z; x = s.x if x is None else x
        return (y * 2 + c, z * 2 + x)
    def toward(s, axis, step=None):
        if axis == "core": return s.dev(c=1 - s.c)
        if axis == "x": return s.dev(x=1 - s.x)
        if axis == "y": return s.dev(y=1 - s.y)
        return s.dev(z=s.z + step)

def barrier(me):
    bar = pltpu.get_barrier_semaphore()
    def sig(d): pl.semaphore_signal(bar, inc=1, device_id=d, device_id_type=MESH)
    sig(me.toward("core")); sig(me.toward("x")); sig(me.toward("y"))
    @pl.when(me.z > 0)
    def _(): sig(me.toward("z", -1))
    @pl.when(me.z < 3)
    def _(): sig(me.toward("z", 1))
    pl.semaphore_wait(bar, 4 + me.z * (3 - me.z) // 2)

ALL = slice(None)

class Gather:
    def __init__(s, me, A, ss, rs, units):
        s.me, s.A, s.ss, s.rs, s.units = me, A, ss, rs, units
        s.sent = []
    def region(s, u, done, c=None, **at):
        me = s.me
        ix = {a: (at[a] if a in at else ALL if a in done else me.pos[a]) for a in "yzx"}
        p, c0, nc = s.units[u]
        return s.A.at[p, ix["y"], me.c if c is None else c, ix["z"], ix["x"], :, pl.ds(c0, nc)]
    def copy(s, p, slot, reg, dev):
        return pltpu.make_async_remote_copy(src_ref=reg, dst_ref=reg, send_sem=s.ss.at[p, slot], recv_sem=s.rs.at[p, slot], device_id=dev, device_id_type=MESH)
    def send(s, p, slot, reg, dev, cond=None):
        def go(): s.copy(p, slot, reg, dev).start()
        def fin(): s.copy(p, slot, reg, dev).wait_send()
        if cond is None: go(); s.sent.append((None, fin))
        else: pl.when(cond)(go); s.sent.append((cond, fin))
    def recv(s, p, slot, reg, dev, cond=None):
        def go(): s.copy(p, slot, reg, dev).wait_recv()
        if cond is None: go()
        else: pl.when(cond)(go)
    def steps(s, p, order):
        me = s.me; out = []
        pend = []
        done = ""
        for a in order:
            if a == "z":
                for k in range(3):
                    def step(k=k, done=done, pend=pend):
                        for w in pend: w()
                        zs = me.z - k
                        s.send(p, 3 + k, s.region(p, done, z=zs), me.toward("z", 1), (zs >= 0) & (me.z < 3))
                        zd = me.z + k
                        s.send(p, 6 + k, s.region(p, done, z=zd), me.toward("z", -1), (zd <= 3) & (me.z > 0))
                    out.append(step)
                    def w(k=k, done=done):
                        s.recv(p, 3 + k, s.region(p, done, z=me.z - 1 - k), me.toward("core"), me.z - 1 - k >= 0)
                        s.recv(p, 6 + k, s.region(p, done, z=me.z + 1 + k), me.toward("core"), me.z + 1 + k <= 3)
                    pend = [w]
            else:
                slot = 0 if a == "x" else 1
                def step(a=a, slot=slot, done=done, pend=pend):
                    for w in pend: w()
                    s.send(p, slot, s.region(p, done), me.toward(a))
                out.append(step)
                def w(a=a, slot=slot, done=done):
                    s.recv(p, slot, s.region(p, done, **{a: 1 - me.pos[a]}), me.toward(a))
                pend = [w]
            done += a
        def step(done=done, pend=pend):
            for w in pend: w()
            s.send(p, 2, s.region(p, done), me.toward("core"))
        out.append(step)
        def fin(done=done):
            s.recv(p, 2, s.region(p, done, c=1 - me.c), me.toward("core"))
        out.append(fin)
        return out
    def drain(s):
        for cond, fin in s.sent:
            if cond is None: fin()
            else: pl.when(cond)(fin)


SLOTS = 4

def when(cond, fn):
    if cond is None: fn()
    else: pl.when(cond)(fn)

class Reduce:
    def __init__(s, me, G, RC, W3, WZ, WB, out, ss, rs, ready, free):
        s.me, s.G, s.RC, s.W3, s.WZ, s.WB, s.out, s.ss, s.rs, s.ready, s.free = me, G, RC, W3, WZ, WB, out, ss, rs, ready, free
        s.sent = []
    def copy(s, u, slot, src, dst, dev):
        return pltpu.make_async_remote_copy(src_ref=src, dst_ref=dst, send_sem=s.ss.at[u, slot], recv_sem=s.rs.at[u, slot], device_id=dev, device_id_type=MESH)
    def around(s, fn):
        me = s.me
        fn(0, me.toward("x"), None); fn(1, me.toward("y"), None)
        pl.when(me.z > 0)(lambda: fn(2, me.toward("z", -1), None))
        pl.when(me.z < 3)(lambda: fn(3, me.toward("z", 1), None))
    def steps(s, p, g, units, u0):
        me = s.me; G = s.G; oc = 1 - me.c
        def cols(u): return pl.ds(units[u][0], units[u][1])
        def region(u, done, **at):
            ix = {a: (at[a] if a in at else me.pos[a] if a in done else ALL) for a in "yzx"}
            return G.at[g, ix["y"], me.c, ix["z"], ix["x"], :, cols(u)]
        def add(dst, src):
            dst[...] = (dst[...].astype(jnp.float32) + src[...].astype(jnp.float32)).astype(jnp.bfloat16)
        def hops(u):
            c0, nc, order = units[u]
            zfirst = order[0] == "z"
            res = []; done = ""
            for i, a in enumerate(order):
                last = i == 2
                if a == "z":
                    for k in (2, 1, 0):
                        if zfirst:
                            up = G.at[g, :, oc, k, :, :, cols(u)]
                            dn = G.at[g, :, oc, 3, :, :, cols(u)] if k == 0 else s.WZ.at[p, k - 1]
                        else:
                            up = G.at[g, 1, oc, k, 1, :, cols(u)]
                            dn = s.W3.at[p, k, :, cols(u)]
                        def snd(k=k, up=up, dn=dn, done=done):
                            for slot, dst, d, st, cond in ((3 + k, up, me.z + 1 + k, 1, me.z + 1 + k <= 3), (6 + k, dn, me.z - 1 - k, -1, me.z - 1 - k >= 0)):
                                cp = s.copy(u0 + u, slot, region(u, done, z=d), dst, me.toward("z", st))
                                pl.when(cond)(cp.start); s.sent.append((cond, cp))
                        def rcv(k=k, up=up, dn=dn, done=done, last=last):
                            fin = last and k == 0
                            if fin: s.out[p, :, cols(u)] = region(u, done, z=me.z)[...].astype(jnp.float32)
                            for slot, buf, d, cond in ((3 + k, up, me.z + k, (me.z + k <= 3) & (me.z >= 1)), (6 + k, dn, me.z - k, (me.z - k >= 0) & (me.z <= 2))):
                                def go():
                                    s.copy(u0 + u, slot, buf, buf, me.toward("core")).wait_recv()
                                    if fin: s.out[p, :, cols(u)] += buf[...].astype(jnp.float32)
                                    else: add(region(u, done, z=d), buf)
                                pl.when(cond)(go)
                        res.append((snd, rcv))
                else:
                    slot = 1 if a == "x" else 2
                    if zfirst: buf = s.WB.at[p, 0:2] if i == 1 else s.WB.at[p, 2]
                    elif a == "x": buf = G.at[g, :, oc, :, 0, :, cols(u)] if i == 0 else G.at[g, 1, oc, :, 0, :, cols(u)]
                    else: buf = G.at[g, 0, oc, :, :, :, cols(u)] if i == 0 else G.at[g, 0, oc, :, 1, :, cols(u)]
                    def snd(a=a, slot=slot, buf=buf, done=done):
                        cp = s.copy(u0 + u, slot, region(u, done, **{a: 1 - me.pos[a]}), buf, me.toward(a))
                        cp.start(); s.sent.append((None, cp))
                    def rcv(a=a, slot=slot, buf=buf, done=done, last=last):
                        s.copy(u0 + u, slot, buf, buf, me.toward("core")).wait_recv()
                        own = region(u, done, **{a: me.pos[a]})
                        if last: s.out[p, :, cols(u)] = own[...].astype(jnp.float32) + buf[...].astype(jnp.float32)
                        else: add(own, buf)
                    res.append((snd, rcv))
                done += a
            return res
        hop = [hops(u) for u in range(len(units))]
        n = len(units)
        def core(u):
            return s.copy(u0 + u, 0, G.at[g, :, oc, :, :, :, cols(u)], s.RC.at[p % SLOTS, :, :, :, :, cols(u)], me.toward("core"))
        out = []
        def first():
            if p >= SLOTS: pl.semaphore_wait(s.free.at[p], 1)
            for u in range(n): core(u).start()
        out.append(first)
        def open_():
            for u in range(n): core(u).wait_send()
            s.around(lambda i, d, _: pl.semaphore_signal(s.ready.at[p, i ^ (1 if i > 1 else 0)], inc=1, device_id=d, device_id_type=MESH))
        out.append(open_)
        def second():
            for u in range(n):
                core(u).wait_recv()
                def body(i, _):
                    y = i // 4; z = i % 4
                    add(G.at[g, y, me.c, z, :, :, cols(u)], s.RC.at[p % SLOTS, y, z, :, :, cols(u)])
                    return 0
                lax.fori_loop(0, 8, body, 0)
                if u == 0:
                    s.around(lambda i, d, _: pl.semaphore_wait(s.ready.at[p, i], 1))
                hop[u][0][0]()
            if p + SLOTS < NP:
                pl.semaphore_signal(s.free.at[p + SLOTS], inc=1, device_id=me.toward("core"), device_id_type=MESH)
        out.append(second)
        for k in range(1, 6):
            def step(k=k):
                for u in range(n):
                    hop[u][k - 1][1]()
                    if k < 5: hop[u][k][0]()
            out.append(step)
        return out
    def drain(s):
        for cond, cp in s.sent: when(cond, cp.wait_send)

NB = 32


EPSILON = 1e-06
MASKED = -1000000000.0
bucket_reach = 128
weight_names = (
    "norm_self",
    "self_q",
    "self_k",
    "self_v",
    "self_o",
    "rel_bias",
    "norm_cross",
    "cross_q",
    "cross_k",
    "cross_v",
    "cross_o",
    "norm_ffn",
    "ffn_in",
    "ffn_out",
)
attn_names = (
    "norm_self",
    "self_q",
    "self_k",
    "self_v",
    "self_o",
    "rel_bias",
    "norm_cross",
    "cross_q",
    "cross_k",
    "cross_v",
    "cross_o",
    "norm_ffn",
)
ffn_names = ("ffn_in", "ffn_out")


def bucket_table(dec_slots, bucket_count):
    near_count = bucket_count // 2
    places = np.arange(dec_slots, dtype=np.int32)
    distance = np.maximum(places[:, None] - places[None, :], 0).astype(np.int32)
    edges = np.array(
        [
            math.ceil(near_count * (bucket_reach / near_count) ** (level / near_count) - 1e-09)
            for level in range(1, near_count)
        ],
        dtype=np.int32,
    )
    far_bucket = near_count + np.sum(
        (distance[:, :, None] >= edges[None, None, :]).astype(np.int32), axis=-1, dtype=np.int32
    )
    return np.where(distance < near_count, distance, far_bucket).astype(np.int32)


def rms_norm(values, gain_vec):
    return (
        values * lax.rsqrt(jnp.mean(values * values, axis=-1, keepdims=True) + EPSILON) * gain_vec
    )


def smooth(values):
    return jax.nn.gelu(values, approximate=True)


def matmul(left_op, right_op):
    return jnp.dot(left_op, right_op, preferred_element_type=jnp.float32)


def matmul_back(grad_op, weight):
    return lax.dot_general(
        grad_op, weight, (((1,), (1,)), ((), ())), preferred_element_type=jnp.float32
    )


def weight_grad(left_op, grad_op):
    return lax.dot_general(
        left_op, grad_op, (((0,), (0,)), ((), ())), preferred_element_type=jnp.float32
    )


def score_block(queries, keys_in, bias_term, mask_in):
    scores = jnp.einsum("bqhe,bkhe->bhqk", queries, keys_in, preferred_element_type=jnp.float32)
    if bias_term is not None:
        scores = scores + bias_term
    return jnp.where(mask_in, scores, MASKED)


def attend(queries, keys_in, values_in, bias_term, mask_in):
    scores = score_block(queries, keys_in, bias_term, mask_in)
    row_top = jnp.max(scores, axis=-1, keepdims=True)
    exp_terms = jnp.exp(scores - row_top)
    exp_total = jnp.sum(exp_terms, axis=-1, keepdims=True)
    attn_probs = exp_terms / exp_total
    log_total = row_top + jnp.log(exp_total)
    mixed = jnp.einsum(
        "bhqk,bkhe->bqhe",
        attn_probs.astype(jnp.bfloat16),
        values_in,
        preferred_element_type=jnp.float32,
    )
    return (mixed.astype(jnp.bfloat16), log_total)


def attend_back(queries, keys_in, values_in, bias_term, mask_in, log_total, grad_mixed):
    scores = score_block(queries, keys_in, bias_term, mask_in)
    attn_probs = jnp.exp(scores - log_total)
    g_values = jnp.einsum(
        "bhqk,bqhe->bkhe",
        attn_probs.astype(jnp.bfloat16),
        grad_mixed,
        preferred_element_type=jnp.float32,
    ).astype(jnp.bfloat16)
    g_probs = jnp.einsum(
        "bqhe,bkhe->bhqk", grad_mixed, values_in, preferred_element_type=jnp.float32
    )
    g_scores = (
        attn_probs * (g_probs - jnp.sum(attn_probs * g_probs, axis=-1, keepdims=True))
    ).astype(jnp.bfloat16)
    g_queries = jnp.einsum(
        "bhqk,bkhe->bqhe", g_scores, keys_in, preferred_element_type=jnp.float32
    ).astype(jnp.bfloat16)
    g_keys = jnp.einsum(
        "bhqk,bqhe->bkhe", g_scores, queries, preferred_element_type=jnp.float32
    ).astype(jnp.bfloat16)
    return (g_queries, g_keys, g_values, g_scores)


def build_masks(dec_lengths, enc_lengths, dec_slots, enc_slots):
    places = jnp.arange(dec_slots, dtype=jnp.int32)
    enc_places = jnp.arange(enc_slots, dtype=jnp.int32)
    causal = places[None, :] <= places[:, None]
    self_mask = causal[None, None] & (
        places[None, None, None, :] < dec_lengths[:, None, None, None]
    )
    cross_mask = enc_places[None, None, None, :] < enc_lengths[:, None, None, None]
    row_mask = (places[None, :] < dec_lengths[:, None]).astype(jnp.float32)
    return ((self_mask, cross_mask), row_mask)


def layer_forward(params, dec_rows, enc_rows, masks, onehot):
    self_mask, cross_mask = masks
    seq_count, dec_slots, model_width = dec_rows.shape
    enc_slots = enc_rows.shape[1]
    head_count = params["rel_bias"].shape[1]
    head_size = model_width // head_count
    row_count = seq_count * dec_slots
    dims = (seq_count, dec_slots, enc_slots, head_count, head_size)

    def split_heads(tensor, slot_count):
        return tensor.reshape(seq_count, slot_count, head_count, head_size)

    x_rows = dec_rows.reshape(row_count, model_width).astype(jnp.float32)
    enc_flat = enc_rows.reshape(seq_count * enc_slots, model_width)
    a_self = rms_norm(x_rows, params["norm_self"].astype(jnp.float32)).astype(jnp.bfloat16)
    q_self = matmul(a_self, params["self_q"]).astype(jnp.bfloat16)
    k_self = matmul(a_self, params["self_k"]).astype(jnp.bfloat16)
    v_self = matmul(a_self, params["self_v"]).astype(jnp.bfloat16)
    bias_term = lax.dot_general(
        params["rel_bias"], onehot, (((0,), (1,)), ((), ())), preferred_element_type=jnp.float32
    )
    bias_term = bias_term.reshape(head_count, dec_slots, dec_slots)[None]
    mixed_self, lse_self = attend(
        split_heads(q_self, dec_slots),
        split_heads(k_self, dec_slots),
        split_heads(v_self, dec_slots),
        bias_term,
        self_mask,
    )
    o_self = mixed_self.reshape(row_count, model_width)
    y_self = x_rows + matmul(o_self, params["self_o"])
    a_cross = rms_norm(y_self, params["norm_cross"].astype(jnp.float32)).astype(jnp.bfloat16)
    q_cross = matmul(a_cross, params["cross_q"]).astype(jnp.bfloat16)
    k_cross = matmul(enc_flat, params["cross_k"]).astype(jnp.bfloat16)
    v_cross = matmul(enc_flat, params["cross_v"]).astype(jnp.bfloat16)
    mixed_cross, lse_cross = attend(
        split_heads(q_cross, dec_slots),
        split_heads(k_cross, enc_slots),
        split_heads(v_cross, enc_slots),
        None,
        cross_mask,
    )
    o_cross = mixed_cross.reshape(row_count, model_width)
    y_cross = y_self + matmul(o_cross, params["cross_o"])
    a_ffn = rms_norm(y_cross, params["norm_ffn"].astype(jnp.float32)).astype(jnp.bfloat16)
    pre_act = matmul(a_ffn, params["ffn_in"])
    hidden = smooth(pre_act).astype(jnp.bfloat16)
    output = y_cross + matmul(hidden, params["ffn_out"])
    state = dict(
        dims=dims,
        x_rows=x_rows,
        enc_flat=enc_flat,
        a_self=a_self,
        q_self=q_self,
        k_self=k_self,
        v_self=v_self,
        bias_term=bias_term,
        lse_self=lse_self,
        o_self=o_self,
        y_self=y_self,
        a_cross=a_cross,
        q_cross=q_cross,
        k_cross=k_cross,
        v_cross=v_cross,
        lse_cross=lse_cross,
        o_cross=o_cross,
        y_cross=y_cross,
        a_ffn=a_ffn,
        pre_act=pre_act,
        hidden=hidden,
    )
    return (output, state)


def layer_backward(params, state, grad_out, masks, onehot):
    self_mask, cross_mask = masks
    seq_count, dec_slots, enc_slots, head_count, head_size = state["dims"]
    model_width = head_count * head_size

    def split_heads(tensor, slot_count):
        return tensor.reshape(seq_count, slot_count, head_count, head_size)

    def flat_rows(tensor):
        return tensor.reshape(-1, model_width)

    grads = {}
    g_ffo = grad_out.astype(jnp.bfloat16)
    grads["ffn_out"] = weight_grad(state["hidden"], g_ffo)
    g_hidden = matmul_back(g_ffo, params["ffn_out"])
    g_pre = jax.vjp(smooth, state["pre_act"])[1](g_hidden)[0].astype(jnp.bfloat16)
    grads["ffn_in"] = weight_grad(state["a_ffn"], g_pre)
    g_a_ffn = matmul_back(g_pre, params["ffn_in"])
    g_normed, grads["norm_ffn"] = jax.vjp(
        rms_norm, state["y_cross"], params["norm_ffn"].astype(jnp.float32)
    )[1](g_a_ffn)
    g_y_cross = grad_out + g_normed
    g_branch = g_y_cross.astype(jnp.bfloat16)
    grads["cross_o"] = weight_grad(state["o_cross"], g_branch)
    g_mixed = matmul_back(g_branch, params["cross_o"]).astype(jnp.bfloat16)
    g_q, g_k, g_v, g_scores = attend_back(
        split_heads(state["q_cross"], dec_slots),
        split_heads(state["k_cross"], enc_slots),
        split_heads(state["v_cross"], enc_slots),
        None,
        cross_mask,
        state["lse_cross"],
        split_heads(g_mixed, dec_slots),
    )
    g_q, g_k, g_v = (flat_rows(g_q), flat_rows(g_k), flat_rows(g_v))
    grads["cross_q"] = weight_grad(state["a_cross"], g_q)
    grads["cross_k"] = weight_grad(state["enc_flat"], g_k)
    grads["cross_v"] = weight_grad(state["enc_flat"], g_v)
    g_enc = matmul_back(g_k, params["cross_k"]) + matmul_back(g_v, params["cross_v"])
    g_a_cross = matmul_back(g_q, params["cross_q"])
    g_normed, grads["norm_cross"] = jax.vjp(
        rms_norm, state["y_self"], params["norm_cross"].astype(jnp.float32)
    )[1](g_a_cross)
    g_y_self = g_y_cross + g_normed
    g_branch = g_y_self.astype(jnp.bfloat16)
    grads["self_o"] = weight_grad(state["o_self"], g_branch)
    g_mixed = matmul_back(g_branch, params["self_o"]).astype(jnp.bfloat16)
    g_q, g_k, g_v, g_scores = attend_back(
        split_heads(state["q_self"], dec_slots),
        split_heads(state["k_self"], dec_slots),
        split_heads(state["v_self"], dec_slots),
        state["bias_term"],
        self_mask,
        state["lse_self"],
        split_heads(g_mixed, dec_slots),
    )
    grads["rel_bias"] = jnp.einsum(
        "bhp,pn->nh",
        g_scores.reshape(seq_count, head_count, dec_slots * dec_slots),
        onehot,
        preferred_element_type=jnp.float32,
    )
    g_q, g_k, g_v = (flat_rows(g_q), flat_rows(g_k), flat_rows(g_v))
    grads["self_q"] = weight_grad(state["a_self"], g_q)
    grads["self_k"] = weight_grad(state["a_self"], g_k)
    grads["self_v"] = weight_grad(state["a_self"], g_v)
    g_a_self = (
        matmul_back(g_q, params["self_q"])
        + matmul_back(g_k, params["self_k"])
        + matmul_back(g_v, params["self_v"])
    )
    g_normed, grads["norm_self"] = jax.vjp(
        rms_norm, state["x_rows"], params["norm_self"].astype(jnp.float32)
    )[1](g_a_self)
    g_dec = g_y_self + g_normed
    return (g_dec, g_enc, grads)


TABLE_ROWS = 16
PAIRS = (("self_q", "self_k"), ("self_v", "self_o"), ("cross_k", "cross_v"), ("cross_q", "cross_o"))
AT = ("dp", "fsdp")
CHUNKS = (2, 2, 4, 2)


def units_of(p):
    wide = 384 if p % 2 == 0 else 256
    return ((0, wide), (wide, 640 - wide), (640, 128))


def gather_kernel(own_ref, small_ref, all_ref, table_ref, A, T, ss, rs, sem):
    me = Place()
    for p in range(NP):
        A[p, me.y, me.c, me.z, me.x] = own_ref[p]
    T[0, me.y, me.c, me.z, me.x] = small_ref[...]
    barrier(me)
    units = [(p, c0, nc) for p in range(NP) for c0, nc in units_of(p)]
    g = Gather(me, A, ss, rs, units)
    h = Gather(me, T, ss, rs, [(0, 0, 128)] * (len(units) + 1))
    ev = []
    for i, (p, c0, nc) in enumerate(units):
        order = ("zyx", "zxy", "xyz" if p % 2 else "yxz")[i % 3]
        for k, st in enumerate(g.steps(i, order)):
            ev.append((p + 2 * k, i, st))
    for k, st in enumerate(h.steps(len(units), "zyx")):
        ev.append((2 * k, -1, st))
    ev.sort(key=lambda e: (e[0], e[1]))
    for _, _, st in ev:
        st()
    g.drain()
    h.drain()
    one = pltpu.make_async_copy(A, all_ref, sem.at[0])
    two = pltpu.make_async_copy(T.at[0], table_ref, sem.at[1])
    one.start()
    two.start()
    one.wait()
    two.wait()


def gather(own, small):
    n = 3 * NP + 1
    return pl.pallas_call(
        gather_kernel,
        out_shape=(
            jax.ShapeDtypeStruct((NP, *CHUNKS, ROWS, COLS), jnp.bfloat16),
            jax.ShapeDtypeStruct((*CHUNKS, TABLE_ROWS, 128), jnp.bfloat16),
        ),
        in_specs=[pl.BlockSpec(memory_space=pltpu.VMEM)] * 2,
        out_specs=[pl.BlockSpec(memory_space=pl.ANY)] * 2,
        scratch_shapes=[
            pltpu.VMEM((NP, *CHUNKS, ROWS, COLS), jnp.bfloat16),
            pltpu.VMEM((1, *CHUNKS, TABLE_ROWS, 128), jnp.bfloat16),
            pltpu.SemaphoreType.DMA((n, 9)),
            pltpu.SemaphoreType.DMA((n, 9)),
            pltpu.SemaphoreType.DMA((2,)),
        ],
        compiler_params=pltpu.CompilerParams(
            collective_id=0, has_side_effects=True, vmem_limit_bytes=60 * 2**20
        ),
    )(own, small)


def reduce_kernel(in_ref, out_ref, G, RC, W3, WZ, WB, ss, rs, ready, free, sem):
    me = Place()
    load = pltpu.make_async_copy(in_ref, G, sem)
    load.start()
    load.wait()
    barrier(me)
    r = Reduce(me, G, RC, W3, WZ, WB, out_ref, ss, rs, ready, free)
    at = (0, 1, 2, 4, 6, 8, 10, 12)
    ev = []
    for p in range(NP):
        orders = ("xyz", "yxz", "zyx" if p % 2 else "zxy")
        units = [(c0, nc, o) for (c0, nc), o in zip(units_of(p), orders)]
        for k, st in enumerate(r.steps(p, p, units, 3 * p)):
            ev.append((p + at[k], p, st))
    ev.sort(key=lambda e: (e[0], e[1]))
    for _, _, st in ev:
        st()
    r.drain()


def reduce_out(local):
    return pl.pallas_call(
        reduce_kernel,
        out_shape=jax.ShapeDtypeStruct((NP, ROWS, COLS), jnp.float32),
        in_specs=[pl.BlockSpec(memory_space=pl.ANY)],
        out_specs=pl.BlockSpec(memory_space=pltpu.VMEM),
        scratch_shapes=[
            pltpu.VMEM((NP, *CHUNKS, ROWS, COLS), jnp.bfloat16),
            pltpu.VMEM((SLOTS, 2, 4, 2, ROWS, COLS), jnp.bfloat16),
            pltpu.VMEM((NP, 3, ROWS, COLS), jnp.bfloat16),
            pltpu.VMEM((NP, 2, 2, 2, ROWS, 128), jnp.bfloat16),
            pltpu.VMEM((NP, 3, ROWS, 128), jnp.bfloat16),
            pltpu.SemaphoreType.DMA((3 * NP, 9)),
            pltpu.SemaphoreType.DMA((3 * NP, 9)),
            pltpu.SemaphoreType.REGULAR((NP, 4)),
            pltpu.SemaphoreType.REGULAR((NP,)),
            pltpu.SemaphoreType.DMA,
        ],
        compiler_params=pltpu.CompilerParams(
            collective_id=1, has_side_effects=True, vmem_limit_bytes=60 * 2**20
        ),
    )(local)


def own_pieces(w):
    pairs = [jnp.concatenate([w[a], w[b]], axis=0) for a, b in PAIRS]
    out = [w["ffn_out"][:48], w["ffn_out"][48:]]
    cut = [w["ffn_in"][:, 768 * j : 768 * (j + 1)] for j in range(4)]
    return jnp.stack(pairs + out + [jnp.concatenate(cut[:2], 0), jnp.concatenate(cut[2:], 0)])


def gather_here(w):
    small = jnp.zeros((TABLE_ROWS, 128), jnp.bfloat16)
    for i, name in enumerate(("norm_self", "norm_cross", "norm_ffn")):
        small = small.at[i, :24].set(w[name])
    small = small.at[4:8, :12].set(w["rel_bias"])
    got, table = gather(own_pieces(w), small)
    got = got.reshape(NP, 32, ROWS, COLS)
    table = table.reshape(32, TABLE_ROWS, 128)
    full = {}
    for i, (a, b) in enumerate(PAIRS):
        full[a] = got[i, :, :24].reshape(768, 768)
        full[b] = got[i, :, 24:].reshape(768, 768)
    full["ffn_out"] = jnp.concatenate([got[4], got[5]], axis=1).reshape(3072, 768)
    cut = [got[6, :, :24], got[6, :, 24:], got[7, :, :24], got[7, :, 24:]]
    full["ffn_in"] = jnp.concatenate([c.reshape(768, 768) for c in cut], axis=1)
    for i, name in enumerate(("norm_self", "norm_cross", "norm_ffn")):
        full[name] = table[:, i, :24].reshape(768)
    full["rel_bias"] = table[:8, 4:8, :12].reshape(32, 12)
    return full


def scatter_here(grads):
    def rows(name):
        return grads[name].reshape(32, -1, grads[name].shape[-1]).astype(jnp.bfloat16)

    def pair(a, b):
        return jnp.concatenate([a, b], axis=1)

    out = rows("ffn_out")
    cut = [rows("ffn_in")[:, :, 768 * j : 768 * (j + 1)] for j in range(4)]
    pieces = [pair(cut[0], cut[1]), pair(cut[2], cut[3]), out[:, :48], out[:, 48:]]
    pieces += [pair(rows(a), rows(b)) for a, b in PAIRS]
    mine = reduce_out(jnp.stack(pieces).reshape(NP, *CHUNKS, ROWS, COLS))
    got = {}
    for i, (a, b) in enumerate(PAIRS):
        got[a] = mine[4 + i, :24]
        got[b] = mine[4 + i, 24:]
    got["ffn_out"] = jnp.concatenate([mine[2], mine[3]], axis=0)
    got["ffn_in"] = jnp.concatenate([mine[0, :24], mine[0, 24:], mine[1, :24], mine[1, 24:]], axis=1)
    return got


def on_device(dec_in, enc_out, dec_len, enc_len, cotangent, *shards):
    micro_count, per, dec_slots, model_width = dec_in.shape
    enc_slots = enc_out.shape[2]
    seq_count = micro_count * per
    row_count = seq_count * dec_slots
    table = bucket_table(dec_slots, NB)
    onehot = jnp.asarray(
        (table.reshape(-1)[:, None] == np.arange(NB, dtype=np.int32)[None, :]).astype(np.float32),
        dtype=jnp.bfloat16,
    )
    w = dict(zip(weight_names, shards))
    copies = lax.axis_size("dp")
    here = (copies, lax.axis_size("fsdp")) == (4, 8)
    if here:
        params = gather_here(w)
    else:
        params = {k: lax.all_gather(v, "fsdp" if k == "rel_bias" else AT, axis=0, tiled=True) for k, v in w.items()}
    masks, row_mask = build_masks(
        dec_len.reshape(-1), enc_len.reshape(-1), dec_slots, enc_slots
    )
    out_rows, state = layer_forward(
        params,
        dec_in.reshape(seq_count, dec_slots, model_width),
        enc_out.reshape(seq_count, enc_slots, model_width),
        masks,
        onehot,
    )
    grad_out = (
        cotangent.reshape(seq_count, dec_slots, model_width).astype(jnp.float32)
        * row_mask[:, :, None]
    ).reshape(row_count, model_width)
    g_dec, g_enc, grads = layer_backward(params, state, grad_out, masks, onehot)
    small = ("norm_self", "norm_cross", "norm_ffn", "rel_bias")
    total = {}
    if here:
        total = scatter_here(grads)
        left = small
    else:
        left = weight_names
    for name in left:
        if name == "rel_bias":
            total[name] = lax.psum_scatter(lax.psum(grads[name], "dp"), "fsdp", scatter_dimension=0, tiled=True)
        else:
            total[name] = lax.psum_scatter(grads[name], AT, scatter_dimension=0, tiled=True)
    return (
        out_rows.reshape(dec_in.shape).astype(jnp.bfloat16),
        g_dec.reshape(dec_in.shape).astype(jnp.bfloat16),
        g_enc.reshape(enc_out.shape).astype(jnp.bfloat16),
        *(total[name] for name in weight_names),
    )


def solution(mesh):
    placed = (
        P(None, ("dp", "fsdp"), None, None),
        P(None, ("dp", "fsdp"), None, None),
        P(None, ("dp", "fsdp")),
        P(None, ("dp", "fsdp")),
        P(None, ("dp", "fsdp"), None, None),
        P(("dp", "fsdp")),
        P(("dp", "fsdp"), None),
        P(("dp", "fsdp"), None),
        P(("dp", "fsdp"), None),
        P(("dp", "fsdp"), None),
        P("fsdp", None),
        P(("dp", "fsdp")),
        P(("dp", "fsdp"), None),
        P(("dp", "fsdp"), None),
        P(("dp", "fsdp"), None),
        P(("dp", "fsdp"), None),
        P(("dp", "fsdp")),
        P(("dp", "fsdp"), None),
        P(("dp", "fsdp"), None),
    )
    return jax.shard_map(
        on_device,
        mesh=mesh,
        in_specs=placed,
        out_specs=(
            P(None, ("dp", "fsdp"), None, None),
            P(None, ("dp", "fsdp"), None, None),
            P(None, ("dp", "fsdp"), None, None),
            P(("dp", "fsdp")),
            P(("dp", "fsdp"), None),
            P(("dp", "fsdp"), None),
            P(("dp", "fsdp"), None),
            P(("dp", "fsdp"), None),
            P("fsdp", None),
            P(("dp", "fsdp")),
            P(("dp", "fsdp"), None),
            P(("dp", "fsdp"), None),
            P(("dp", "fsdp"), None),
            P(("dp", "fsdp"), None),
            P(("dp", "fsdp")),
            P(("dp", "fsdp"), None),
            P(("dp", "fsdp"), None),
        ),
        check_vma=False,
    )
```

```python
import functools
import math

import jax
import jax.numpy as jnp
import numpy as np
from jax import lax
from jax.experimental import pallas as pl
from jax.experimental.pallas import tpu as pltpu
from jax.sharding import PartitionSpec as P

MESH = pl.DeviceIdType.MESH
NP = 8
ROWS = 48
COLS = 768

class Place:
    def __init__(s):
        dp = lax.axis_index("dp"); f = lax.axis_index("fsdp")
        s.c = dp % 2; s.y = dp // 2; s.x = f % 2; s.z = f // 2
        s.pos = {"x": s.x, "y": s.y, "z": s.z}
    def dev(s, c=None, y=None, z=None, x=None):
        c = s.c if c is None else c; y = s.y if y is None else y
        z = s.z if z is None else z; x = s.x if x is None else x
        return (y * 2 + c, z * 2 + x)
    def toward(s, axis, step=None):
        if axis == "core": return s.dev(c=1 - s.c)
        if axis == "x": return s.dev(x=1 - s.x)
        if axis == "y": return s.dev(y=1 - s.y)
        return s.dev(z=s.z + step)

def barrier(me):
    bar = pltpu.get_barrier_semaphore()
    def sig(d): pl.semaphore_signal(bar, inc=1, device_id=d, device_id_type=MESH)
    sig(me.toward("core")); sig(me.toward("x")); sig(me.toward("y"))
    @pl.when(me.z > 0)
    def _(): sig(me.toward("z", -1))
    @pl.when(me.z < 3)
    def _(): sig(me.toward("z", 1))
    pl.semaphore_wait(bar, 4 + me.z * (3 - me.z) // 2)

ALL = slice(None)

class Gather:
    def __init__(s, me, A, ss, rs, units):
        s.me, s.A, s.ss, s.rs, s.units = me, A, ss, rs, units
        s.sent = []
    def region(s, u, done, c=None, **at):
        me = s.me
        ix = {a: (at[a] if a in at else ALL if a in done else me.pos[a]) for a in "yzx"}
        p, c0, nc = s.units[u]
        return s.A.at[p, ix["y"], me.c if c is None else c, ix["z"], ix["x"], :, pl.ds(c0, nc)]
    def copy(s, p, slot, reg, dev):
        return pltpu.make_async_remote_copy(src_ref=reg, dst_ref=reg, send_sem=s.ss.at[p, slot], recv_sem=s.rs.at[p, slot], device_id=dev, device_id_type=MESH)
    def send(s, p, slot, reg, dev, cond=None):
        def go(): s.copy(p, slot, reg, dev).start()
        def fin(): s.copy(p, slot, reg, dev).wait_send()
        when(cond, go); s.sent.append((p, cond, fin))
    def recv(s, p, slot, reg, dev, cond=None):
        def go(): s.copy(p, slot, reg, dev).wait_recv()
        if cond is None: go()
        else: pl.when(cond)(go)
    def steps(s, p, order):
        me = s.me; out = []
        pend = []
        done = ""
        for a in order:
            if a == "z":
                for k in range(3):
                    def step(k=k, done=done, pend=pend):
                        for w in pend: w()
                        zs = me.z - k
                        s.send(p, 3 + k, s.region(p, done, z=zs), me.toward("z", 1), (zs >= 0) & (me.z < 3))
                        zd = me.z + k
                        s.send(p, 6 + k, s.region(p, done, z=zd), me.toward("z", -1), (zd <= 3) & (me.z > 0))
                    out.append(step)
                    def w(k=k, done=done):
                        s.recv(p, 3 + k, s.region(p, done, z=me.z - 1 - k), me.toward("core"), me.z - 1 - k >= 0)
                        s.recv(p, 6 + k, s.region(p, done, z=me.z + 1 + k), me.toward("core"), me.z + 1 + k <= 3)
                    pend = [w]
            else:
                slot = 0 if a == "x" else 1
                def step(a=a, slot=slot, done=done, pend=pend):
                    for w in pend: w()
                    s.send(p, slot, s.region(p, done), me.toward(a))
                out.append(step)
                def w(a=a, slot=slot, done=done):
                    s.recv(p, slot, s.region(p, done, **{a: 1 - me.pos[a]}), me.toward(a))
                pend = [w]
            done += a
        def step(done=done, pend=pend):
            for w in pend: w()
            s.send(p, 2, s.region(p, done), me.toward("core"))
        out.append(step)
        def fin(done=done):
            s.recv(p, 2, s.region(p, done, c=1 - me.c), me.toward("core"))
        out.append(fin)
        return out
    def drain(s, *us):
        for u, cond, fin in s.sent:
            if u in us: when(cond, fin)
        s.sent = [e for e in s.sent if e[0] not in us]


def when(cond, fn):
    if cond is None: fn()
    else: pl.when(cond)(fn)

class Reduce:
    def __init__(s, me, G, RC, W3, WZ, WB, out, ss, rs, ready, free, slots, count):
        s.slots, s.count = slots, count
        s.me, s.G, s.RC, s.W3, s.WZ, s.WB, s.out, s.ss, s.rs, s.ready, s.free = me, G, RC, W3, WZ, WB, out, ss, rs, ready, free
        s.sent = []
    def copy(s, u, slot, src, dst, dev):
        return pltpu.make_async_remote_copy(src_ref=src, dst_ref=dst, send_sem=s.ss.at[u, slot], recv_sem=s.rs.at[u, slot], device_id=dev, device_id_type=MESH)
    def around(s, fn):
        me = s.me
        fn(0, me.toward("x"), None); fn(1, me.toward("y"), None)
        pl.when(me.z > 0)(lambda: fn(2, me.toward("z", -1), None))
        pl.when(me.z < 3)(lambda: fn(3, me.toward("z", 1), None))
    def steps(s, p, g, units, u0):
        me = s.me; G = s.G; oc = 1 - me.c
        def cols(u): return pl.ds(units[u][0], units[u][1])
        def region(u, done, **at):
            ix = {a: (at[a] if a in at else me.pos[a] if a in done else ALL) for a in "yzx"}
            return G.at[g, ix["y"], me.c, ix["z"], ix["x"], :, cols(u)]
        def add(dst, src):
            dst[...] = (dst[...].astype(jnp.float32) + src[...].astype(jnp.float32)).astype(jnp.bfloat16)
        def hops(u):
            c0, nc, order = units[u]
            zfirst = order[0] == "z"
            res = []; done = ""
            for i, a in enumerate(order):
                last = i == 2
                if a == "z":
                    for k in (2, 1, 0):
                        if zfirst:
                            up = G.at[g, :, oc, k, :, :, cols(u)]
                            dn = G.at[g, :, oc, 3, :, :, cols(u)] if k == 0 else s.WZ.at[p, k - 1]
                        else:
                            up = G.at[g, 1, oc, k, 1, :, cols(u)]
                            dn = s.W3.at[p, k, :, cols(u)]
                        def snd(k=k, up=up, dn=dn, done=done):
                            for slot, dst, d, st, cond in ((3 + k, up, me.z + 1 + k, 1, me.z + 1 + k <= 3), (6 + k, dn, me.z - 1 - k, -1, me.z - 1 - k >= 0)):
                                cp = s.copy(u0 + u, slot, region(u, done, z=d), dst, me.toward("z", st))
                                pl.when(cond)(cp.start); s.sent.append((cond, cp))
                        def rcv(k=k, up=up, dn=dn, done=done, last=last):
                            fin = last and k == 0
                            if fin: s.out[p, :, cols(u)] = region(u, done, z=me.z)[...].astype(jnp.float32)
                            for slot, buf, d, cond in ((3 + k, up, me.z + k, (me.z + k <= 3) & (me.z >= 1)), (6 + k, dn, me.z - k, (me.z - k >= 0) & (me.z <= 2))):
                                def go():
                                    s.copy(u0 + u, slot, buf, buf, me.toward("core")).wait_recv()
                                    if fin: s.out[p, :, cols(u)] += buf[...].astype(jnp.float32)
                                    else: add(region(u, done, z=d), buf)
                                pl.when(cond)(go)
                        res.append((snd, rcv))
                else:
                    slot = 1 if a == "x" else 2
                    if zfirst: buf = s.WB.at[p, 0:2] if i == 1 else s.WB.at[p, 2]
                    elif a == "x": buf = G.at[g, :, oc, :, 0, :, cols(u)] if i == 0 else G.at[g, 1, oc, :, 0, :, cols(u)]
                    else: buf = G.at[g, 0, oc, :, :, :, cols(u)] if i == 0 else G.at[g, 0, oc, :, 1, :, cols(u)]
                    def snd(a=a, slot=slot, buf=buf, done=done):
                        cp = s.copy(u0 + u, slot, region(u, done, **{a: 1 - me.pos[a]}), buf, me.toward(a))
                        cp.start(); s.sent.append((None, cp))
                    def rcv(a=a, slot=slot, buf=buf, done=done, last=last):
                        s.copy(u0 + u, slot, buf, buf, me.toward("core")).wait_recv()
                        own = region(u, done, **{a: me.pos[a]})
                        if last: s.out[p, :, cols(u)] = own[...].astype(jnp.float32) + buf[...].astype(jnp.float32)
                        else: add(own, buf)
                    res.append((snd, rcv))
                done += a
            return res
        hop = [hops(u) for u in range(len(units))]
        n = len(units)
        def core(u):
            return s.copy(u0 + u, 0, G.at[g, :, oc, :, :, :, cols(u)], s.RC.at[p % s.slots, :, :, :, :, cols(u)], me.toward("core"))
        out = []
        def first():
            if p >= s.slots: pl.semaphore_wait(s.free.at[p], 1)
            for u in range(n): core(u).start()
        out.append(first)
        def open_():
            for u in range(n): core(u).wait_send()
            s.around(lambda i, d, _: pl.semaphore_signal(s.ready.at[p, i ^ (1 if i > 1 else 0)], inc=1, device_id=d, device_id_type=MESH))
        out.append(open_)
        def second():
            for u in range(n):
                core(u).wait_recv()
                def body(i, _):
                    y = i // 4; z = i % 4
                    add(G.at[g, y, me.c, z, :, :, cols(u)], s.RC.at[p % s.slots, y, z, :, :, cols(u)])
                    return 0
                lax.fori_loop(0, 8, body, 0)
                if u == 0:
                    s.around(lambda i, d, _: pl.semaphore_wait(s.ready.at[p, i], 1))
                hop[u][0][0]()
            if p + s.slots < s.count:
                pl.semaphore_signal(s.free.at[p + s.slots], inc=1, device_id=me.toward("core"), device_id_type=MESH)
        out.append(second)
        for k in range(1, 6):
            def step(k=k):
                for u in range(n):
                    hop[u][k - 1][1]()
                    if k < 5: hop[u][k][0]()
            out.append(step)
        return out
    def drain(s):
        for cond, cp in s.sent: when(cond, cp.wait_send)

WIDTH = 768
DEC = 128
ENC = 512
SEQS = 2
HERE = (4, 8, SEQS, DEC, ENC, WIDTH)
CHUNKS = (2, 2, 4, 2)
TROWS = 16
SLOTS = 3
OWN = WIDTH // 32
PAIRS = WIDTH // 128
HALF = WIDTH // 2
BLK = 256
RD = SEQS * DEC
RE = SEQS * ENC
GELU = math.sqrt(2.0 / math.pi)
PLACE = (9, 10, 11, 12, 5, 6, 4, 7)
START = (0, 1, 2, 3, 6, 7, 9, 10)
AFTER = (0, 1, 2, 4, 6, 8, 10, 12)


def bucket_rows():
    table = bucket_table(DEC, NB)[:, 0]
    far = table[(-np.arange(DEC)) % DEC]
    rows = np.full((8, TROWS), -1)
    rows[:, 4:8] = np.arange(NB).reshape(8, 4)
    return jnp.asarray((rows.reshape(-1, 1) == far[None, :]).astype(np.float32), jnp.bfloat16)


def units_of(p):
    wide = 384 if p % 2 == 0 else 256
    return ((0, wide), (wide, 640 - wide), (640, 128))


def loop(n, body):
    def step(i, carry):
        body(i)
        return carry

    lax.fori_loop(0, n, step, 0)


def tile(i, n):
    return pl.ds(pl.multiple_of(i * n, n), n)


def f32(v):
    return v.astype(jnp.float32)


def layer_kernel(
    dlen, elen, dec_hbm, enc_hbm, cot_hbm, small, bmap,
    sq, sk, sv, so, cq, ck, cv, co, fi, fo,
    out_hbm, gdec_hbm, genc_hbm, gw, gt,
    BUF, T, GT, RCT, W3T, RC, W3, WZ, WB,
    X, C, E, K, V, A1, Q1, K1, V1, O1, A2, Q2, O2, A3, HID, GP,
    Y1, Y2, F1, F2, GY, PS, PC, BIAS, NRM, DM,
    ags, agr, rss, rsr, ready, free, tready, tfree, lsem,
):
    me = Place()
    loads = [
        pltpu.make_async_copy(a, b, lsem.at[i])
        for i, (a, b) in enumerate(((dec_hbm, X), (cot_hbm, C), (enc_hbm, E)))
    ]
    for cp in loads:
        cp.start()

    def pack(p, top, bottom):
        both = jnp.concatenate([f32(top), f32(bottom)], axis=0)
        BUF[p + 1, me.y, me.c, me.z, me.x] = low(both)

    pack(0, sq[...], sk[...])
    pack(1, sv[...], so[...])
    pack(2, ck[...], cv[...])
    pack(3, cq[...], co[...])
    BUF[5, me.y, me.c, me.z, me.x] = fo[0:48]
    BUF[6, me.y, me.c, me.z, me.x] = fo[48:96]
    for h in range(2):
        pack(6 + h, fi[:, 1536 * h : 1536 * h + 768], fi[:, 1536 * h + 768 : 1536 * h + 1536])
    T[0, me.y, me.c, me.z, me.x] = small[...]
    barrier(me)

    units = [(p + 1, c0, nc) for p in range(NP) for c0, nc in units_of(p)]
    g = Gather(me, BUF, ags, agr, units)
    h = Gather(me, T, ags, agr, [(0, 0, 128)] * (len(units) + 1))
    events = []
    for i, (b, c0, nc) in enumerate(units):
        order = ("zyx", "zxy", "yxz" if b % 2 else "xyz")[i % 3]
        for k, st in enumerate(g.steps(i, order)):
            events.append((b - 1 + 2 * k, i, st))
    for k, st in enumerate(h.steps(len(units), "zyx")):
        events.append((k, -1, st))
    events.sort(key=lambda e: (e[0], e[1]))

    def until(t):
        while events and events[0][0] <= t:
            events.pop(0)[2]()

    def first_lanes(shape):
        return lax.broadcasted_iota(jnp.int32, shape, 1) < 64

    def two(v):
        keep = first_lanes(v.shape)
        w = f32(v)
        return low(jnp.concatenate([jnp.where(keep, w, 0.0), jnp.where(keep, 0.0, w)], axis=0))

    def one(v):
        return jnp.where(first_lanes((DEC, 128)), v[:DEC], v[DEC:])

    def unpack(src, dst):
        def body(j):
            w = f32(BUF[src, j // 8, (j // 4) % 2, j % 4])
            for k in range(2):
                rows = slice(OWN * k, OWN * k + OWN)
                BUF[dst, k, j // 8, (j // 2) % 4, j % 2] = low(jnp.concatenate([w[0, rows], w[1, rows]], axis=0))

        loop(16, body)

    def weight(b, k, cols):
        return BUF[b, k, :, :, :, :, cols].reshape(WIDTH, -1)

    def weight_rows(b, k, c):
        return BUF[b, k, c].reshape(HALF, WIDTH)

    def project(a, b, k, dst, rows=RD):
        def body(i):
            r, cols = tile(i // 3, RD), tile(i % 3, BLK)
            dst[r, cols] = low(dot_nn(a[r, :], weight(b, k, cols)))

        loop(3 * (rows // RD), body)

    def project_add(a, b, k, base, dst):
        def body(i):
            cols = tile(i, BLK)
            dst[:, cols] = f32(base[:, cols]) + dot_nn(a[...], weight(b, k, cols))

        loop(3, body)

    def norm(v, gain, dst):
        def body(i):
            r = tile(i, 32)
            x = f32(v[r, :])
            s = lax.rsqrt(jnp.mean(x * x, axis=-1, keepdims=True) + EPSILON)
            dst[r, :] = low(x * s * NRM[gain : gain + 1, :])

        loop(RD // 32, body)

    def norm_back(v, gain, G, base, dst):
        def body(i, total):
            r = tile(i, 32)
            x = f32(v[r, :])
            s = lax.rsqrt(jnp.mean(x * x, axis=-1, keepdims=True) + EPSILON)
            n = x * s
            w = G[r, :]
            u = w * NRM[gain : gain + 1, :]
            dst[r, :] = f32(base[r, :]) + s * (u - n * jnp.mean(u * n, axis=-1, keepdims=True))
            return total + jnp.sum((w * n).reshape(4, 8, WIDTH), axis=0)

        total = lax.fori_loop(0, RD // 32, body, jnp.zeros((8, WIDTH), jnp.float32))
        return jnp.sum(total, axis=0, keepdims=True)

    def softmax(s):
        e = jnp.exp(s - jnp.max(s, axis=-1, keepdims=True))
        return e * (1.0 / jnp.sum(e, axis=-1, keepdims=True))

    def attend(q, k, v, o, probs, slots, mask):
        def body(i):
            at, lanes = i // PAIRS, tile(i % PAIRS, 128)
            r, kr = tile(at, DEC), tile(at, slots)
            s = dot_nt(two(q[r, lanes]), k[kr, lanes])
            p = low(softmax(mask(s, at, i % PAIRS)))
            probs[i] = p
            o[r, lanes] = low(one(dot_nn(p, v[kr, lanes])))

        loop(SEQS * PAIRS, body)

    def attend_back(q, k, v, go, probs, slots, lo, hi, extra):
        def body(j):
            i = j + lo
            at, lanes = i // PAIRS, tile(i % PAIRS, 128)
            r, kr = tile(at, DEC), tile(at, slots)
            q2, g2, p = two(q[r, lanes]), two(go[r, lanes]), probs[i]
            d = dot_nt(g2, v[kr, lanes])
            pf = f32(p)
            gs = low(pf * (d - jnp.sum(pf * d, axis=-1, keepdims=True)))
            v[kr, lanes] = low(dot_tn(p, g2))
            q[r, lanes] = low(one(dot_nn(gs, k[kr, lanes])))
            k[kr, lanes] = low(dot_tn(gs, q2))
            extra(gs, i % PAIRS)

        loop(hi - lo, body)

    def back_project(pairs, dst, cast, rows=RD):
        def body(i):
            r = tile(i // 2, RD)
            v = None
            for a, b, k in pairs:
                d = dot_nt(a[r, :], weight_rows(b, k, i % 2))
                v = d if v is None else v + d
            dst[r, tile(i % 2, HALF)] = cast(v)

        loop(2 * (rows // RD), body)

    def grad_pair(aa, ga, ab, gb, place, oa=0, ob=0):
        def body(i):
            y, n = i // 3, i % 3
            va = dot_tn(aa[:, tile(y, HALF)], ga[:, tile(n + oa, BLK)]).reshape(16, OWN, BLK)
            vb = dot_tn(ab[:, tile(y, HALF)], gb[:, tile(n + ob, BLK)]).reshape(16, OWN, BLK)
            both = low(jnp.concatenate([va, vb], axis=1))
            BUF[place, y, :, :, :, :, tile(n, BLK)] = both.reshape(2, 4, 2, ROWS, BLK)

        loop(6, body)

    until(8)
    for cp in loads:
        cp.wait()
    owner = jnp.floor((f32(lax.broadcasted_iota(jnp.int32, (1, WIDTH), 1)) + 0.5) * (1.0 / OWN))

    def spread():
        place = f32(lax.broadcasted_iota(jnp.int32, (128, WIDTH), 1)) - OWN * owner
        return low(jnp.where(place == f32(lax.broadcasted_iota(jnp.int32, (128, WIDTH), 0)), 1.0, 0.0))

    table = T[0].reshape(32 * TROWS, 128)
    row = f32(lax.broadcasted_iota(jnp.int32, (32 * TROWS, 1), 0)) - TROWS * owner
    wide = dot_nn(table, spread())
    NRM[...] = jnp.concatenate(
        [jnp.sum(jnp.where(row == float(n), wide, 0.0), axis=0, keepdims=True) for n in range(3)]
        + [jnp.zeros((5, WIDTH), jnp.float32)],
        axis=0,
    )
    DM[...] = dot_tn(T[0, 0, 0].reshape(8 * TROWS, 128), bmap[...])
    for j in range(2 * PAIRS):
        v = jnp.broadcast_to(DM[j : j + 1, :], (DEC, DEC))
        BIAS[j // 2, DEC * (j % 2) : DEC * (j % 2) + DEC, :] = pltpu.roll(v, 0, 1, stride=1, stride_axis=0)
    norm(X, 0, A1)
    place = lax.broadcasted_iota(jnp.int32, (DEC, WIDTH), 0)
    for s in range(SEQS):
        r = slice(DEC * s, DEC * s + DEC)
        C[r, :] = low(jnp.where(place < dlen[s], f32(C[r, :]), 0.0))

    def self_mask(s, at, pair):
        k = lax.broadcasted_iota(jnp.int32, s.shape, 1)
        q = lax.broadcasted_iota(jnp.int32, s.shape, 0) % DEC
        return jnp.where((k <= q) & (k < dlen[at]), s + BIAS[pair], MASKED)

    def cross_mask(s, at, pair):
        return jnp.where(lax.broadcasted_iota(jnp.int32, s.shape, 1) < elen[at], s, MASKED)

    until(12)
    unpack(1, 0)
    project(A1, 0, 0, Q1)
    project(A1, 0, 1, K1)
    until(13)
    g.drain(*range(0, 3))
    unpack(2, 1)
    project(A1, 1, 0, V1)
    attend(Q1, K1, V1, O1, PS, DEC, self_mask)
    project_add(O1, 1, 1, X, Y1)
    norm(Y1, 1, A2)
    until(14)
    g.drain(*range(3, 6))
    unpack(3, 2)
    project(E, 2, 0, K, RE)
    project(E, 2, 1, V, RE)
    until(15)
    g.drain(*range(6, 9))
    unpack(4, 3)
    project(A2, 3, 0, Q2)
    attend(Q2, K, V, O2, PC, ENC, cross_mask)
    project_add(O2, 3, 1, Y1, Y2)
    norm(Y2, 2, A3)
    F1[...] = jnp.zeros_like(F1)
    F2[...] = jnp.zeros_like(F2)

    def out_rows(j, zs, cols):
        return jnp.concatenate(
            [BUF[b, j // 2, j % 2, zs, :, :, cols] for b in (5, 6)], axis=2
        ).reshape(-1, cols.stop - cols.start if isinstance(cols, slice) else BLK)

    def feed(j, b):
        k = j % 2

        def body(t):
            cols = tile(t, HALF)
            pre = dot_nn(A3[...], weight(b, k, cols))
            gh = dot_nt(C[...], out_rows(j, pl.ds(2 * t, 2), slice(0, WIDTH)))
            th = jnp.tanh(GELU * (pre + 0.044715 * (pre * pre * pre)))
            HID[:, cols] = low(0.5 * pre * (1.0 + th))
            slope = 0.5 * (1.0 + th) + 0.5 * pre * (1.0 - th * th) * (GELU * (1.0 + 0.134145 * (pre * pre)))
            GP[:, tile(t + 2 * k, HALF)] = low(slope * gh)

        loop(2, body)

        def mix(n):
            cols = tile(n, BLK)
            F1[:, cols] += dot_nn(HID[...], out_rows(j, pl.ds(0, 4), cols))

        loop(3, mix)

        def mix_back(t):
            F2[:, tile(t, HALF)] += dot_nt(GP[:, k * WIDTH : (k + 1) * WIDTH], weight_rows(b, k, t))

        loop(2, mix_back)

        def grads(i):
            t, n = i // 3, i % 3
            w = low(dot_tn(HID[:, tile(t, HALF)], C[:, tile(n, BLK)]).reshape(4, 2 * ROWS, BLK))
            w = w.reshape(2, 2, 2 * ROWS, BLK)
            for e in range(2):
                BUF[PLACE[2 + e], j // 2, j % 2, pl.ds(2 * t, 2), :, :, tile(n, BLK)] = w[:, :, ROWS * e : ROWS * e + ROWS]

        loop(6, grads)

    r = Reduce(me, BUF, RC, W3, WZ, WB, gw, rss, rsr, ready, free, SLOTS, NP)
    rt = Reduce(me, GT, RCT, W3T, None, None, gt, rss, rsr, tready, tfree, 1, 1)
    moves = []
    for p in range(NP):
        orders = ("xyz", "yxz", "zyx" if p % 2 else "zxy")
        cut = [(c0, nc, o) for (c0, nc), o in zip(units_of(p), orders)]
        for k, st in enumerate(r.steps(p, PLACE[p], cut, 3 * p)):
            moves.append((START[p] + AFTER[k], p, st))
    small_moves = rt.steps(0, 0, [(0, 128, "xyz")], 3 * NP)
    moves.sort(key=lambda e: (e[0], e[1]))

    def upto(t):
        while moves and moves[0][0] <= t:
            moves.pop(0)[2]()

    until(18)
    g.drain(*range(9, 12))
    unpack(7, 4)
    feed(0, 4)
    feed(1, 4)
    grad_pair(A3, GP, A3, GP, PLACE[0], 0, 3)
    upto(0)
    until(99)
    g.drain(*range(18, 21))
    unpack(8, 7)
    feed(2, 7)
    feed(3, 7)
    grad_pair(A3, GP, A3, GP, PLACE[1], 0, 3)
    upto(3)

    def finish(i):
        q = tile(i, 32)
        O1x[q, :] = low(Y2[q, :] + F1[q, :])

    O1x = A3
    loop(RD // 32, finish)
    stores = [pltpu.make_async_copy(A3, out_hbm, lsem.at[0])]
    stores[0].start()
    g.drain(*range(12, 15))
    g.drain(*range(15, 18))
    g.drain(*range(21, 24))
    h.drain(len(units))
    gain3 = norm_back(Y2, 2, F2, C, GY)
    GC = C

    def cast_rows(src, dst):
        def body(i):
            q = tile(i, 32)
            dst[q, :] = low(src[q, :])

        loop(RD // 32, body)

    cast_rows(GY, GC)
    back_project([(GC, 3, 1)], HID, low)
    upto(4)

    def nothing(gs, pair):
        pass

    attend_back(Q2, K, V, HID, PC, ENC, 0, 6, nothing)
    upto(5)
    attend_back(Q2, K, V, HID, PC, ENC, 6, 12, nothing)
    grad_pair(A2, Q2, O2, GC, PLACE[4])
    upto(6)
    grad_pair(E, K, E, V, PLACE[5])
    upto(7)
    back_project([(Q2, 3, 0)], F2, f32)
    gain2 = norm_back(Y1, 1, F2, GY, GY)
    cast_rows(GY, GC)
    back_project([(GC, 1, 1)], HID, low)
    BIAS[...] = jnp.zeros_like(BIAS)

    def sum_bias(gs, pair):
        BIAS[pair] += f32(gs)

    attend_back(Q1, K1, V1, HID, PS, DEC, 0, 12, sum_bias)
    upto(8)
    grad_pair(A1, V1, O1, GC, PLACE[6])
    grad_pair(A1, Q1, A1, K1, PLACE[7])
    upto(10)
    back_project([(K, 2, 0), (V, 2, 1)], E, low, RE)
    stores.append(pltpu.make_async_copy(E, genc_hbm, lsem.at[2]))
    stores[1].start()
    upto(11)
    back_project([(Q1, 0, 0), (K1, 0, 1), (V1, 1, 0)], F2, f32)
    gain1 = norm_back(X, 0, F2, GY, GY)
    cast_rows(GY, HID)
    stores.append(pltpu.make_async_copy(HID, gdec_hbm, lsem.at[1]))
    stores[2].start()
    DM[...] = jnp.zeros_like(DM)
    flip = lax.broadcasted_iota(jnp.int32, (DEC, DEC), 0) + lax.broadcasted_iota(jnp.int32, (DEC, DEC), 1)
    flip = low(jnp.where(flip == DEC - 1, 1.0, 0.0))
    for j in range(2 * PAIRS):
        v = BIAS[j // 2, DEC * (j % 2) : DEC * (j % 2) + DEC, :]
        hi = low(v)
        v = dot_nn(flip, hi) + dot_nn(flip, low(v - f32(hi)))
        v = pltpu.roll(v, 0, 1, stride=1, stride_axis=0)
        DM[j : j + 1, :] = jnp.sum(v, axis=0, keepdims=True)
    DM[...] = pltpu.roll(DM[...], 1, 1)
    hi = low(DM[...])
    rel = dot_nt(bmap[...], hi) + dot_nt(bmap[...], low(DM[...] - f32(hi)))
    gains = (gain1, gain2, gain3)
    spots = sum(jnp.where(row == float(n), gains[n], 0.0) for n in range(3))
    spots = dot_nt(low(spots), spread()).reshape(4, 128, 128)
    for d in range(4):
        GT[0, d // 2, d % 2] = low(spots[d] + rel).reshape(4, 2, TROWS, 128)
    for i, st in enumerate(small_moves):
        st()
        upto(12 + i)
    upto(99)
    r.drain()
    rt.drain()
    for cp in stores:
        cp.wait()


def layer_here(shards, dec_in, enc_out, dec_len, enc_len, cotangent):
    ns, sq, sk, sv, so, rel, nc, cq, ck, cv, co, nf, fi, fo = shards
    gains = jnp.pad(jnp.stack([ns, nc, nf]), ((0, 1), (0, 128 - OWN)))
    small = jnp.concatenate([gains, jnp.pad(rel, ((0, 8), (0, 128 - rel.shape[1])))], axis=0)
    b16, w32 = jnp.bfloat16, jnp.float32

    def vm(shape, dtype=b16):
        return pltpu.VMEM(shape, dtype)

    dec, enc = (RD, WIDTH), (RE, WIDTH)
    scratch = [
        vm((13, *CHUNKS, ROWS, COLS)),
        vm((1, *CHUNKS, TROWS, 128)),
        vm((1, *CHUNKS, TROWS, 128)),
        vm((1, 2, 4, 2, TROWS, 128)),
        vm((1, 3, TROWS, 128)),
        vm((SLOTS, 2, 4, 2, ROWS, COLS)),
        vm((NP, 3, ROWS, COLS)),
        vm((NP, 2, 2, 2, ROWS, 128)),
        vm((NP, 3, ROWS, 128)),
        vm(dec), vm(dec), vm(enc), vm(enc), vm(enc),
        *[vm(dec)] * 10,
        vm((RD, 2 * WIDTH)),
        *[vm(dec, w32)] * 5,
        vm((SEQS * PAIRS, 2 * DEC, DEC)),
        vm((SEQS * PAIRS, 2 * DEC, ENC)),
        vm((PAIRS, 2 * DEC, DEC), w32),
        vm((8, WIDTH), w32),
        vm((128, 128), w32),
        *[pltpu.SemaphoreType.DMA((3 * NP + 1, 9))] * 4,
        pltpu.SemaphoreType.REGULAR((NP, 4)),
        pltpu.SemaphoreType.REGULAR((NP,)),
        pltpu.SemaphoreType.REGULAR((1, 4)),
        pltpu.SemaphoreType.REGULAR((1,)),
        pltpu.SemaphoreType.DMA((3,)),
    ]
    here, away = pl.BlockSpec(memory_space=pltpu.VMEM), pl.BlockSpec(memory_space=pl.ANY)
    scalars = pl.BlockSpec(memory_space=pltpu.SMEM)
    out, g_dec, g_enc, gw, gt = pl.pallas_call(
        layer_kernel,
        out_shape=(
            jax.ShapeDtypeStruct(dec, b16),
            jax.ShapeDtypeStruct(dec, b16),
            jax.ShapeDtypeStruct(enc, b16),
            jax.ShapeDtypeStruct((NP, ROWS, COLS), w32),
            jax.ShapeDtypeStruct((1, TROWS, 128), w32),
        ),
        in_specs=[scalars] * 2 + [away] * 3 + [here] * 12,
        out_specs=[away] * 3 + [here] * 2,
        scratch_shapes=scratch,
        compiler_params=pltpu.CompilerParams(
            collective_id=0, has_side_effects=True, vmem_limit_bytes=60 * 2**20
        ),
    )(
        dec_len.reshape(-1), enc_len.reshape(-1),
        dec_in.reshape(dec), enc_out.reshape(enc), cotangent.reshape(dec),
        small, bucket_rows(), sq, sk, sv, so, cq, ck, cv, co, fi, fo,
    )
    gt = gt[0]
    top, bottom = gw[:, :OWN], gw[:, OWN:]
    w_fi = jnp.concatenate([top[0], bottom[0], top[1], bottom[1]], axis=1)
    w_fo = gw[2:4].reshape(2 * ROWS, COLS)
    gains = [gt[n, :OWN] for n in range(3)]
    w_rel = gt[4 : 4 + rel.shape[0], : rel.shape[1]]
    return out, g_dec, g_enc, (
        gains[0], top[7], bottom[7], top[6], bottom[6], w_rel,
        gains[1], top[4], top[5], bottom[5], bottom[4], gains[2], w_fi, w_fo,
    )


EPSILON = 1e-06
MASKED = -1000000000.0
NB = 32
AT = ("dp", "fsdp")


def bucket_table(dec_slots, bucket_count):
    near = bucket_count // 2
    places = np.arange(dec_slots, dtype=np.int32)
    distance = np.maximum(places[:, None] - places[None, :], 0).astype(np.int32)
    edges = np.array(
        [math.ceil(near * (128 / near) ** (level / near) - 1e-09) for level in range(1, near)],
        dtype=np.int32,
    )
    far = near + np.sum(
        (distance[:, :, None] >= edges[None, None, :]).astype(np.int32), axis=-1, dtype=np.int32
    )
    return np.where(distance < near, distance, far).astype(np.int32)


def rms_norm(values, gain):
    return values * lax.rsqrt(jnp.mean(values * values, axis=-1, keepdims=True) + EPSILON) * gain


def smooth(values):
    return jax.nn.gelu(values, approximate=True)


def dot_nn(a, b):
    return jnp.dot(a, b, preferred_element_type=jnp.float32)


def dot_nt(a, b):
    return lax.dot_general(a, b, (((1,), (1,)), ((), ())), preferred_element_type=jnp.float32)


def dot_tn(a, b):
    return lax.dot_general(a, b, (((0,), (0,)), ((), ())), preferred_element_type=jnp.float32)


def low(v):
    return v.astype(jnp.bfloat16)


def layer_plain(weights, dec_rows, enc_rows, dec_len, enc_len, cot_rows):
    ns, sq, sk, sv, so, rel, nc, cq, ck, cv, co, nf, fi, fo = weights
    seqs, dec_slots, width = dec_rows.shape
    enc_slots = enc_rows.shape[1]
    heads = rel.shape[1]
    size = width // heads
    ns, nc, nf = (v.astype(jnp.float32) for v in (ns, nc, nf))
    places = jnp.arange(dec_slots, dtype=jnp.int32)
    causal = places[None, :] <= places[:, None]
    self_mask = causal[None, None] & (places[None, None, None, :] < dec_len[:, None, None, None])
    enc_places = jnp.arange(enc_slots, dtype=jnp.int32)
    cross_mask = enc_places[None, None, None, :] < enc_len[:, None, None, None]
    row_mask = (places[None, :] < dec_len[:, None]).astype(jnp.float32)
    table = bucket_table(dec_slots, NB).reshape(-1)
    onehot = jnp.asarray((table[:, None] == np.arange(NB)[None, :]).astype(np.float32), jnp.bfloat16)
    bias = lax.dot_general(rel, onehot, (((0,), (1,)), ((), ())), preferred_element_type=jnp.float32)
    bias = bias.reshape(heads, dec_slots, dec_slots)[None]

    def split(t):
        return t.reshape(seqs, -1, heads, size).transpose(0, 2, 1, 3)

    def join(t):
        return t.transpose(0, 2, 1, 3).reshape(-1, width)

    def many(a, b, ca, cb):
        return lax.dot_general(
            a, b, (((ca,), (cb,)), ((0, 1), (0, 1))), preferred_element_type=jnp.float32
        )

    def attend(q, k, v, add, mask):
        s = jnp.where(mask, many(q, k, 3, 3) + add, MASKED)
        top = jnp.max(s, axis=-1, keepdims=True)
        e = jnp.exp(s - top)
        p = e / jnp.sum(e, axis=-1, keepdims=True)
        return p, low(many(low(p), v, 3, 2))

    def back(q, k, v, p, g):
        gv = low(many(low(p), g, 2, 2))
        d = many(g, v, 3, 3)
        gs = low(p * (d - jnp.sum(p * d, axis=-1, keepdims=True)))
        return low(many(gs, k, 3, 2)), low(many(gs, q, 2, 2)), gv, gs

    x = dec_rows.reshape(-1, width).astype(jnp.float32)
    enc = enc_rows.reshape(-1, width)
    a1 = low(rms_norm(x, ns))
    q1, k1, v1 = (split(low(dot_nn(a1, w))) for w in (sq, sk, sv))
    p1, o1 = attend(q1, k1, v1, bias, self_mask)
    o1 = join(o1)
    y1 = x + dot_nn(o1, so)
    a2 = low(rms_norm(y1, nc))
    q2 = split(low(dot_nn(a2, cq)))
    k2, v2 = (split(low(dot_nn(enc, w))) for w in (ck, cv))
    p2, o2 = attend(q2, k2, v2, 0.0, cross_mask)
    o2 = join(o2)
    y2 = y1 + dot_nn(o2, co)
    a3 = low(rms_norm(y2, nf))
    pre = dot_nn(a3, fi)
    hidden = low(smooth(pre))
    out = y2 + dot_nn(hidden, fo)
    g = (cot_rows.astype(jnp.float32) * row_mask[:, :, None]).reshape(-1, width)
    gf = low(g)
    w_fo = dot_tn(hidden, gf)
    gp = low(jax.vjp(smooth, pre)[1](dot_nt(gf, fo))[0])
    w_fi = dot_tn(a3, gp)
    part, w_nf = jax.vjp(rms_norm, y2, nf)[1](dot_nt(gp, fi))
    gy = g + part
    gc = low(gy)
    w_co = dot_tn(o2, gc)
    gq, gk, gv, _ = back(q2, k2, v2, p2, split(low(dot_nt(gc, co))))
    gq, gk, gv = join(gq), join(gk), join(gv)
    w_cq, w_ck, w_cv = dot_tn(a2, gq), dot_tn(enc, gk), dot_tn(enc, gv)
    g_enc = dot_nt(gk, ck) + dot_nt(gv, cv)
    part, w_nc = jax.vjp(rms_norm, y1, nc)[1](dot_nt(gq, cq))
    gy = gy + part
    ga = low(gy)
    w_so = dot_tn(o1, ga)
    gq, gk, gv, gs = back(q1, k1, v1, p1, split(low(dot_nt(ga, so))))
    w_rel = lax.dot_general(
        onehot, gs.reshape(seqs, heads, -1), (((0,), (2,)), ((), ())), preferred_element_type=jnp.float32
    ).sum(axis=1)
    gq, gk, gv = join(gq), join(gk), join(gv)
    w_sq, w_sk, w_sv = dot_tn(a1, gq), dot_tn(a1, gk), dot_tn(a1, gv)
    part, w_ns = jax.vjp(rms_norm, x, ns)[1](dot_nt(gq, sq) + dot_nt(gk, sk) + dot_nt(gv, sv))
    grads = (w_ns, w_sq, w_sk, w_sv, w_so, w_rel, w_nc, w_cq, w_ck, w_cv, w_co, w_nf, w_fi, w_fo)
    return low(out), low(gy + part), low(g_enc), grads


REL = 5


def on_device(dec_in, enc_out, dec_len, enc_len, cotangent, *shards):
    micro, per, dec_slots, width = dec_in.shape
    seqs, enc_slots = micro * per, enc_out.shape[2]
    if (lax.axis_size("dp"), lax.axis_size("fsdp"), seqs, dec_slots, enc_slots, width) == HERE:
        out, g_dec, g_enc, grads = layer_here(shards, dec_in, enc_out, dec_len, enc_len, cotangent)
    else:
        whole = [lax.all_gather(w, AT[1] if i == REL else AT, axis=0, tiled=True) for i, w in enumerate(shards)]
        out, g_dec, g_enc, grads = layer_plain(
            whole,
            dec_in.reshape(seqs, dec_slots, width),
            enc_out.reshape(seqs, enc_slots, width),
            dec_len.reshape(-1),
            enc_len.reshape(-1),
            cotangent.reshape(seqs, dec_slots, width),
        )
        grads = [
            lax.psum_scatter(
                lax.psum(w, AT[0]) if i == REL else w,
                AT[1] if i == REL else AT,
                scatter_dimension=0,
                tiled=True,
            )
            for i, w in enumerate(grads)
        ]
    return (out.reshape(dec_in.shape), g_dec.reshape(dec_in.shape), g_enc.reshape(enc_out.shape), *grads)


def solution(mesh):
    rows, seq = P(AT, None), P(None, AT, None, None)
    gain, lens, rel = P(AT), P(None, AT), P(AT[1], None)
    placed = (gain, rows, rows, rows, rows, rel, gain, rows, rows, rows, rows, gain, rows, rows)
    return jax.shard_map(
        on_device,
        mesh=mesh,
        in_specs=(seq, seq, lens, lens, seq, *placed),
        out_specs=(seq, seq, seq, *placed),
        check_vma=False,
    )
```

```python
import functools
import math

import jax
import jax.numpy as jnp
import numpy as np
from jax import lax
from jax.experimental import pallas as pl
from jax.experimental.pallas import tpu as pltpu
from jax.sharding import PartitionSpec as P

MESH = pl.DeviceIdType.MESH
NP = 8
ROWS = 48
COLS = 768
ALL = slice(None)


class Place:
    def __init__(s):
        dp, f = lax.axis_index("dp"), lax.axis_index("fsdp")
        s.c, s.y, s.x, s.z = dp % 2, dp // 2, f % 2, f // 2
        s.pos = {"x": s.x, "y": s.y, "z": s.z}

    def dev(s, c=None, y=None, z=None, x=None):
        c = s.c if c is None else c
        y = s.y if y is None else y
        z = s.z if z is None else z
        x = s.x if x is None else x
        return (y * 2 + c, z * 2 + x)

    def core(s):
        return s.dev(c=1 - s.c)

    def over(s, axis, j=1):
        if axis == "x":
            return s.dev(x=1 - s.x)
        if axis == "y":
            return s.dev(y=1 - s.y)
        return s.dev(z=(s.z + j) % 4)

    def others(s):
        return [s.over("x"), s.over("y")] + [s.over("z", j) for j in (1, 2, 3)]


def signal(sem, dev):
    pl.semaphore_signal(sem, inc=1, device_id=dev, device_id_type=MESH)


def greet(me):
    for d in me.others() + [me.core()]:
        signal(pltpu.get_barrier_semaphore(), d)


def all_here():
    pl.semaphore_wait(pltpu.get_barrier_semaphore(), 6)


class Mover:
    def __init__(s, me, ss, rs, rows):
        s.me, s.ss, s.rs, s.rows, s.sent = me, ss, rs, rows, []

    def copy(s, u, slot, src, dst, dev):
        return pltpu.make_async_remote_copy(
            src_ref=src, dst_ref=dst, send_sem=s.ss.at[s.rows[u], slot], recv_sem=s.rs.at[s.rows[u], slot],
            device_id=dev, device_id_type=MESH,
        )

    def send(s, *what):
        cp = s.copy(*what)
        cp.start()
        s.sent.append((what[0], cp))

    def arrived(s, u, slot, dst):
        s.copy(u, slot, dst, dst, s.me.core()).wait_recv()

    def drain(s, us=None):
        for u, cp in s.sent:
            if us is None or u in us:
                cp.wait_send()
        s.sent = [] if us is None else [e for e in s.sent if e[0] not in us]


class Gather(Mover):
    def __init__(s, me, A, ss, rs, rows):
        super().__init__(me, ss, rs, rows)
        s.A = A

    def steps(s, u, b, c0, nc, order):
        me = s.me

        def region(done, c=me.c, **at):
            ix = {a: (at[a] if a in at else ALL if a in done else me.pos[a]) for a in "yzx"}
            return s.A.at[b, ix["y"], c, ix["z"], ix["x"], :, pl.ds(c0, nc)]

        def hop(a, done):
            if a == "z":
                for j in (3, 2, 1):
                    s.send(u, 2 + j, region(done), region(done), me.over(a, j))
            else:
                s.send(u, 1 if a == "x" else 2, region(done), region(done), me.over(a))

        def land(a, done):
            if a == "z":
                for j in (1, 2, 3):
                    s.arrived(u, 2 + j, region(done, z=(me.z + 4 - j) % 4))
            else:
                s.arrived(u, 1 if a == "x" else 2, region(done, **{a: 1 - me.pos[a]}))

        def step(k):
            if 0 < k < 4:
                land(order[k - 1], order[: k - 1])
            if k < 3:
                hop(order[k], order[:k])
            elif k == 3:
                s.send(u, 0, region(order), region(order), me.core())
            else:
                s.arrived(u, 0, region(order, c=1 - me.c))

        return [functools.partial(step, k) for k in range(5)]


class Reduce(Mover):
    def __init__(s, me, G, RC, out, ss, rs, rows, ready, free, slots, count):
        super().__init__(me, ss, rs, rows)
        s.G, s.RC, s.out, s.ready, s.free, s.slots, s.count = G, RC, out, ready, free, slots, count
        s.todo = {}

    def steps(s, u, p, g, c0, nc, order, units):
        me, G, oc = s.me, s.G, 1 - s.me.c
        cols = pl.ds(c0, nc)
        opened, added = s.todo.setdefault(p, ([], []))

        def region(done, **at):
            ix = {a: (at[a] if a in at else me.pos[a] if a in done else ALL) for a in "yzx"}
            return G.at[g, ix["y"], me.c, ix["z"], ix["x"], :, cols]

        def slot(k, z=None):
            i = {
                "xyz": ((ALL, ALL, 0), (0, ALL, 1), (1, z, 1)),
                "yxz": ((0, ALL, ALL), (1, ALL, 0), (1, z, 1)),
                "zyx": ((ALL, z, ALL), (0, me.z, ALL), (1, me.z, 0)),
                "zxy": ((ALL, z, ALL), (ALL, me.z, 0), (0, me.z, 1)),
            }[order][k]
            return G.at[g, i[0], oc, i[1], i[2], :, cols]

        def hop(k):
            a = order[k]
            if a == "z":
                for j in (3, 2, 1):
                    s.send(u, 2 + j, region(order[:k], z=(me.z + j) % 4), slot(k, me.z), me.over(a, j))
            else:
                s.send(u, 1 if a == "x" else 2, region(order[:k], **{a: 1 - me.pos[a]}), slot(k), me.over(a))

        def land(k):
            a = order[k]
            own = region(order[:k], **{a: me.pos[a]})
            if a == "z":
                got = [(2 + j, slot(k, (me.z + 4 - j) % 4)) for j in (1, 2, 3)]
            else:
                got = [(1 if a == "x" else 2, slot(k))]
            total = own[...].astype(jnp.float32)
            for n, ref in got:
                s.arrived(u, n, ref)
                total = total + ref[...].astype(jnp.float32)
            if k == 2:
                s.out[p, :, cols] = total
            else:
                own[...] = total.astype(jnp.bfloat16)

        def core():
            return s.copy(
                u, 0, G.at[g, :, oc, :, :, :, cols], s.RC.at[p % s.slots, :, :, :, :, cols], me.core()
            )

        def first():
            if p >= s.slots and p not in s.todo[-1]:
                pl.semaphore_wait(s.free.at[p], 1)
                s.todo[-1].add(p)
            core().start()

        def open_up():
            core().wait_send()
            opened.append(u)
            if len(opened) == units:
                for i, d in enumerate(me.others()):
                    signal(s.ready.at[p, i], d)

        def second():
            s.arrived(u, 0, s.RC.at[p % s.slots, :, :, :, :, cols])
            for y in range(2):
                own, got = G.at[g, y, me.c, :, :, :, cols], s.RC.at[p % s.slots, y, :, :, :, cols]
                own[...] = (own[...].astype(jnp.float32) + got[...].astype(jnp.float32)).astype(jnp.bfloat16)
            if not added:
                for i in range(5):
                    pl.semaphore_wait(s.ready.at[p, i], 1)
            added.append(u)
            hop(0)
            if len(added) == units and p + s.slots < s.count:
                signal(s.free.at[p + s.slots], me.core())

        def later(k):
            land(k)
            if k < 2:
                hop(k + 1)

        s.todo.setdefault(-1, set())
        return [first, open_up, second] + [functools.partial(later, k) for k in range(3)]

WIDTH = 768
DEC = 128
ENC = 512
SEQS = 2
HERE = (4, 8, SEQS, DEC, ENC, WIDTH)
CHUNKS = (2, 2, 4, 2)
TROWS = 16
SLOTS = 4
OWN = WIDTH // 32
PAIRS = WIDTH // 128
HALF = WIDTH // 2
BLK = 256
RD = SEQS * DEC
RE = SEQS * ENC
GELU = math.sqrt(2.0 / math.pi)
PLACE = (9, 8, 10, 11, 4, 7, 5, 6)
GATHERED = (
    (1, 0, 128, "zyx"),
    (1, 128, 512, "zyx"),
    (1, 640, 128, "zyx"),
    (2, 0, 384, "zxy"),
    (2, 384, 256, "yzx"),
    (2, 640, 128, "zyx"),
    (3, 0, 256, "zxy"),
    (3, 256, 384, "zxy"),
    (3, 640, 128, "zyx"),
    (4, 0, 512, "xzy"),
    (4, 512, 128, "zyx"),
    (4, 640, 128, "zxy"),
    (5, 0, 384, "zyx"),
    (5, 384, 256, "xzy"),
    (5, 640, 128, "yxz"),
    (6, 0, 384, "yzx"),
    (6, 384, 256, "zyx"),
    (6, 640, 128, "xzy"),
    (7, 0, 512, "zxy"),
    (7, 512, 128, "xyz"),
    (7, 640, 128, "zyx"),
    (8, 0, 256, "zxy"),
    (8, 256, 256, "xyz"),
    (8, 512, 256, "zyx"),
)
REDUCED = (
    (0, 0, 384, "xyz"),
    (0, 384, 256, "yxz"),
    (0, 640, 128, "zxy"),
    (1, 0, 256, "xyz"),
    (1, 256, 384, "yxz"),
    (1, 640, 128, "zxy"),
    (2, 0, 640, "xyz"),
    (2, 640, 128, "zxy"),
    (3, 0, 640, "yxz"),
    (3, 640, 128, "zyx"),
    (4, 0, 384, "xyz"),
    (4, 384, 256, "yxz"),
    (4, 640, 128, "zyx"),
    (5, 0, 384, "xyz"),
    (5, 384, 256, "yxz"),
    (5, 640, 128, "zyx"),
    (6, 0, 256, "xyz"),
    (6, 256, 384, "yxz"),
    (6, 640, 128, "zyx"),
    (7, 0, 384, "xyz"),
    (7, 384, 384, "yxz"),
)
PLAN = (
    240, 2000, 90, 100, 110, 0, 10, 20, 60, 241, 70, 80, 91, 101, 242, 111,
    1, 102, 243, 112, 244, 2001, 11, 21, 2, 103, 2002, 61, 113, 104, 30, 40,
    50, 114, 71, 3, 81, 4, 12, 62, 22, 41, 82, 72, 150, 160, 170, 63,
    92, 64, 120, 130, 140, 31, 51, 13, 73, 180, 190, 200, 23, 14, 151, 74,
    24, 2003, 42, 83, 171, 131, 161, 2004, 84, 210, 220, 230, 32, 191, 121, 93,
    141, 52, 43, 94, 221, 181, 142, 162, 201, 44, 53, 54, 33, 182, 192, 152,
    34, 2005, 172, 2006, 122, 2007, 222, 163, 2008, 202, 2009, 132, 164, 2010, 2011, 2012,
    211, 2013, 2014, 2015, 231, 2016, 153, 2017, 2018, 2019, 154, 2020, 183, 2021, 143, 2022,
    173, 2023, 123, 144, 184, 2024, 174, 2025, 193, 124, 203, 133, 194, 212, 204, 134,
    2026, 232, 2027, 2028, 2029, 1000, 1010, 1020, 1001, 213, 1011, 1021, 223, 233, 1002, 214,
    1012, 1022, 224, 234, 2030, 2031, 2032, 2033, 1030, 1040, 1050, 2034, 1031, 2035, 2036, 1013,
    1041, 1051, 2037, 1060, 1070, 1080, 1090, 1003, 1032, 2038, 2039, 1061, 1023, 1071, 1042, 1052,
    1014, 1081, 1091, 2040, 1062, 1072, 1004, 1082, 1092, 1033, 1024, 2041, 2042, 2043, 2044, 2045,
    2046, 1043, 1053, 2047, 2048, 1015, 2049, 2050, 1100, 1110, 1120, 2051, 1101, 2052, 1063, 1073,
    1111, 1121, 2053, 1130, 1140, 1150, 1102, 1044, 1005, 1083, 1074, 1131, 1141, 1151, 1054, 1112,
    1122, 1034, 1025, 2054, 1132, 1142, 1152, 1093, 2055, 2056, 1075, 1064, 1045, 1055, 1103, 2057,
    2058, 2059, 2060, 2061, 1113, 1123, 1084, 1035, 1160, 1170, 1180, 2062, 1190, 1200, 1161, 2063,
    1171, 1181, 1143, 2064, 1094, 1191, 1162, 1153, 1201, 1172, 1182, 1133, 1192, 1104, 1202, 1154,
    1114, 1124, 2065, 2066, 1065, 1144, 1095, 2067, 2068, 2069, 1085, 1163, 1173, 1210, 1211, 1134,
    1183, 1212, 1193, 1155, 1125, 1105, 1115, 1203, 1174, 1213, 1145, 1164, 1184, 1135, 1194, 1204,
    1185, 1214, 1175, 1165, 1195, 1205, 1215,
)


def bucket_rows():
    table = bucket_table(DEC, NB)[:, 0]
    far = table[(-np.arange(DEC)) % DEC]
    rows = np.full((8, TROWS), -1)
    rows[:, 4:8] = np.arange(NB).reshape(8, 4)
    return jnp.asarray((rows.reshape(-1, 1) == far[None, :]).astype(np.float32), jnp.bfloat16)


def sem_rows(gathered, reduced):
    deep = [max(gathered.count(p), reduced.count(p)) for p in range(NP)]

    def rows(pieces):
        return [sum(deep[:p]) + pieces[:i].count(p) for i, p in enumerate(pieces)] + [sum(deep)]

    return rows(gathered), rows(reduced), sum(deep)


def loop(n, body):
    def step(i, carry):
        body(i)
        return carry

    lax.fori_loop(0, n, step, 0)


def tile(i, n):
    return pl.ds(pl.multiple_of(i * n, n), n)


def f32(v):
    return v.astype(jnp.float32)


def layer_kernel(
    dlen, elen, dec_hbm, enc_hbm, cot_hbm, small, bmap,
    sq, sk, sv, so, cq, ck, cv, co, fi, fo,
    out_hbm, gdec_hbm, genc_hbm, gw, gt,
    BUF, T, GT, RCT, RC,
    X, C, E, K, V, A1, Q1, K1, V1, O1, A2, Q2, O2, A3, GO, HID, GP,
    Y1, Y2, F2, GY, PS, PC, BIAS, NRM, DM,
    ss, rs, ready, free, tready, tfree, lsem,
):
    me = Place()
    greet(me)
    loads = [
        pltpu.make_async_copy(a, b, lsem.at[i])
        for i, (a, b) in enumerate(((dec_hbm, X), (cot_hbm, C), (enc_hbm, E)))
    ]
    for cp in loads:
        cp.start()

    def pack(p, top, bottom):
        both = jnp.concatenate([f32(top), f32(bottom)], axis=0)
        BUF[p + 1, me.y, me.c, me.z, me.x] = low(both)

    pack(0, sq[...], sk[...])
    pack(1, sv[...], so[...])
    pack(2, ck[...], cv[...])
    pack(3, cq[...], co[...])
    BUF[5, me.y, me.c, me.z, me.x] = fo[0:48]
    BUF[6, me.y, me.c, me.z, me.x] = fo[48:96]
    for h in range(2):
        pack(6 + h, fi[:, 1536 * h : 1536 * h + 768], fi[:, 1536 * h + 768 : 1536 * h + 1536])
    T[0, me.y, me.c, me.z, me.x] = small[...]
    all_here()

    def first_lanes(shape):
        return lax.broadcasted_iota(jnp.int32, shape, 1) < 64

    def two(v):
        keep = first_lanes(v.shape)
        w = f32(v)
        return low(jnp.concatenate([jnp.where(keep, w, 0.0), jnp.where(keep, 0.0, w)], axis=0))

    def one(v):
        return jnp.where(first_lanes((DEC, 128)), v[:DEC], v[DEC:])

    def unpack(src, dst):
        def body(i):
            for z in range(4):
                w = f32(BUF[src, i // 2, i % 2, z])
                for k in range(2):
                    rows = slice(OWN * k, OWN * k + OWN)
                    both = low(jnp.concatenate([w[0, rows], w[1, rows]], axis=0))
                    BUF[dst, k, i // 2, (i % 2) * 2 + z // 2, z % 2] = both

        loop(4, body)

    def whole(b, k):
        return BUF[b, k].reshape(WIDTH, WIDTH)

    def project(a, b, k, dst, i=0):
        r = slice(i * RD, i * RD + RD)
        dst[r, :] = low(dot_nn(a[r, :], whole(b, k)))

    def project_add(a, b, k, base, dst):
        dst[...] = f32(base[...]) + dot_nn(a[...], whole(b, k))

    def norm(v, gain, dst):
        def body(i):
            r = tile(i, 128)
            x = f32(v[r, :])
            s = lax.rsqrt(jnp.mean(x * x, axis=-1, keepdims=True) + EPSILON)
            dst[r, :] = low(x * s * NRM[gain : gain + 1, :])

        loop(RD // 128, body)

    def norm_back(v, gain, G, base, dst):
        def body(i, total):
            r = tile(i, 64)
            x = f32(v[r, :])
            s = lax.rsqrt(jnp.mean(x * x, axis=-1, keepdims=True) + EPSILON)
            n = x * s
            w = G[r, :]
            u = w * NRM[gain : gain + 1, :]
            dst[r, :] = f32(base[r, :]) + s * (u - n * jnp.mean(u * n, axis=-1, keepdims=True))
            return total + jnp.sum((w * n).reshape(8, 8, WIDTH), axis=0)

        total = lax.fori_loop(0, RD // 64, body, jnp.zeros((8, WIDTH), jnp.float32))
        return jnp.sum(total, axis=0, keepdims=True)

    def softmax(s):
        e = jnp.exp(s - jnp.max(s, axis=-1, keepdims=True))
        return e * (1.0 / jnp.sum(e, axis=-1, keepdims=True))

    def attend(q, k, v, o, probs, slots, mask, lo, hi):
        def body(j):
            i = j + lo
            lanes = tile(i, 128)
            for at in range(SEQS):
                r, kr = slice(at * DEC, at * DEC + DEC), slice(at * slots, at * slots + slots)
                s = dot_nt(two(q[r, lanes]), k[kr, lanes])
                p = low(softmax(mask(s, at, i)))
                probs[i, at] = p
                o[r, lanes] = low(one(dot_nn(p, v[kr, lanes])))

        loop(hi - lo, body)

    def attend_back(q, k, v, go, probs, slots, lo, hi, extra):
        def body(j):
            i = j + lo
            lanes = tile(i, 128)
            for at in range(SEQS):
                r, kr = slice(at * DEC, at * DEC + DEC), slice(at * slots, at * slots + slots)
                q2, g2, p = two(q[r, lanes]), two(go[r, lanes]), probs[i, at]
                d = dot_nt(g2, v[kr, lanes])
                pf = f32(p)
                gs = low(pf * (d - jnp.sum(pf * d, axis=-1, keepdims=True)))
                v[kr, lanes] = low(dot_tn(p, g2))
                q[r, lanes] = low(one(dot_nn(gs, k[kr, lanes])))
                k[kr, lanes] = low(dot_tn(gs, q2))
                extra(gs, i)

        loop(hi - lo, body)

    def back_project(pairs, dst, cast, i=0):
        r = slice(i * RD, i * RD + RD)
        v = None
        for a, b, k in pairs:
            d = dot_nt(a[r, :], whole(b, k))
            v = d if v is None else v + d
        dst[r, :] = cast(v)

    def grad_pair(aa, ga, ab, gb, place, oa=0, ob=0, tiles=(0, 1, 2)):
        for n in tiles:
            va = dot_tn(aa[...], ga[:, (n + oa) * BLK : (n + oa + 1) * BLK]).reshape(32, OWN, BLK)
            vb = dot_tn(ab[...], gb[:, (n + ob) * BLK : (n + ob + 1) * BLK]).reshape(32, OWN, BLK)
            both = low(jnp.concatenate([va, vb], axis=1))
            BUF[place, :, :, :, :, :, n * BLK : (n + 1) * BLK] = both.reshape(2, 2, 4, 2, ROWS, BLK)

    owner = jnp.floor((f32(lax.broadcasted_iota(jnp.int32, (1, WIDTH), 1)) + 0.5) * (1.0 / OWN))

    def spread():
        place = f32(lax.broadcasted_iota(jnp.int32, (128, WIDTH), 1)) - OWN * owner
        return low(jnp.where(place == f32(lax.broadcasted_iota(jnp.int32, (128, WIDTH), 0)), 1.0, 0.0))

    row = f32(lax.broadcasted_iota(jnp.int32, (32 * TROWS, 1), 0)) - TROWS * owner
    def self_mask(s, at, pair):
        k = lax.broadcasted_iota(jnp.int32, s.shape, 1)
        q = lax.broadcasted_iota(jnp.int32, s.shape, 0) % DEC
        return jnp.where((k <= q) & (k < dlen[at]), s + BIAS[pair], MASKED)

    def cross_mask(s, at, pair):
        return jnp.where(lax.broadcasted_iota(jnp.int32, s.shape, 1) < elen[at], s, MASKED)

    def out_rows(j):
        return jnp.concatenate([BUF[b, j // 2, j % 2] for b in (5, 6)], axis=2).reshape(WIDTH, WIDTH)

    def feed(j, b):
        k = j % 2
        pre = dot_nn(A3[...], whole(b, k))
        gh = dot_nt(C[...], out_rows(j))
        th = jnp.tanh(GELU * (pre + 0.044715 * (pre * pre * pre)))
        HID[:, j * WIDTH : (j + 1) * WIDTH] = low(0.5 * pre * (1.0 + th))
        slope = 0.5 * (1.0 + th) + 0.5 * pre * (1.0 - th * th) * (GELU * (1.0 + 0.134145 * (pre * pre)))
        GP[:, j * WIDTH : (j + 1) * WIDTH] = low(slope * gh)

    def feed_grads(j):
        for n in range(3):
            w = low(dot_tn(HID[:, j * WIDTH : (j + 1) * WIDTH], C[:, n * BLK : (n + 1) * BLK]))
            w = w.reshape(4, 2, 2 * ROWS, BLK)
            for e in range(2):
                part = w[:, :, ROWS * e : ROWS * e + ROWS]
                BUF[PLACE[2 + e], j // 2, j % 2, :, :, :, n * BLK : (n + 1) * BLK] = part

    def mix_back(j, b):
        d = dot_nt(GP[:, j * WIDTH : (j + 1) * WIDTH], whole(b, j % 2))
        F2[...] = d if j == 0 else F2[...] + d

    def mix():
        v = Y2[...]
        for j in range(4):
            v = v + dot_nn(HID[:, j * WIDTH : (j + 1) * WIDTH], out_rows(j))
        A3[...] = low(v)


    def cast_rows(src, dst):
        def body(i):
            q = tile(i, 64)
            dst[q, :] = low(src[q, :])

        loop(RD // 64, body)

    def nothing(gs, pair):
        pass

    def sum_bias(gs, pair):
        BIAS[pair] += f32(gs)

    def done(*pieces):
        g.drain([u for u, unit in enumerate(GATHERED) if unit[0] - 1 in pieces])

    stores, gains = [], {}

    def store(src, dst, i):
        stores.append(pltpu.make_async_copy(src, dst, lsem.at[i]))
        stores[-1].start()

    def init():
        for cp in loads:
            cp.wait()
        place = lax.broadcasted_iota(jnp.int32, (DEC, WIDTH), 0)
        for s in range(SEQS):
            r = slice(DEC * s, DEC * s + DEC)
            C[r, :] = low(jnp.where(place < dlen[s], f32(C[r, :]), 0.0))

    def tables():
        h.drain()
        table = T[0].reshape(32 * TROWS, 128)
        wide = dot_nn(table, spread())
        NRM[...] = jnp.concatenate(
            [jnp.sum(jnp.where(row == float(n), wide, 0.0), axis=0, keepdims=True) for n in range(3)]
            + [jnp.zeros((5, WIDTH), jnp.float32)],
            axis=0,
        )
        DM[...] = dot_tn(T[0, 0, 0].reshape(8 * TROWS, 128), bmap[...])
        for j in range(2 * PAIRS):
            v = jnp.broadcast_to(DM[j : j + 1, :], (DEC, DEC))
            BIAS[j // 2, DEC * (j % 2) : DEC * (j % 2) + DEC, :] = pltpu.roll(v, 0, 1, stride=1, stride_axis=0)

    def unpack_to(src, dst, *pieces):
        done(*pieces)
        unpack(src, dst)

    def self_out():
        project_add(O1, 1, 1, X, Y1)
        norm(Y1, 1, A2)

    def cross_out():
        project_add(O2, 3, 1, Y1, Y2)
        norm(Y2, 2, A3)

    def in_grads(h):
        if h:
            done(4, 5, 7)
        grad_pair(A3, GP, A3, GP, PLACE[h], 6 * h, 6 * h + 3)

    def finish():
        mix()
        store(A3, out_hbm, 0)

    def norm_back_ffn():
        gains[2] = norm_back(Y2, 2, F2, C, GY)
        cast_rows(GY, C)

    def norm_back_cross():
        gains[1] = norm_back(Y1, 1, F2, GY, GY)
        cast_rows(GY, C)
        BIAS[...] = jnp.zeros_like(BIAS)

    def norm_back_self():
        gains[0] = norm_back(X, 0, F2, GY, GY)
        cast_rows(GY, GO)
        store(GO, gdec_hbm, 1)

    def enc_grad(i):
        back_project([(K, 2, 0), (V, 2, 1)], E, low, i)
        if i == 3:
            store(E, genc_hbm, 2)

    def small_grads():
        DM[...] = jnp.zeros_like(DM)
        flip = lax.broadcasted_iota(jnp.int32, (DEC, DEC), 0) + lax.broadcasted_iota(jnp.int32, (DEC, DEC), 1)
        flip = low(jnp.where(flip == DEC - 1, 1.0, 0.0))
        for j in range(2 * PAIRS):
            v = BIAS[j // 2, DEC * (j % 2) : DEC * (j % 2) + DEC, :]
            hi = low(v)
            v = dot_nn(flip, hi) + dot_nn(flip, low(v - f32(hi)))
            v = pltpu.roll(v, 0, 1, stride=1, stride_axis=0)
            DM[j : j + 1, :] = jnp.sum(v, axis=0, keepdims=True)
        DM[...] = pltpu.roll(DM[...], 1, 1)
        hi = low(DM[...])
        rel = dot_nt(bmap[...], hi) + dot_nt(bmap[...], low(DM[...] - f32(hi)))
        spots = sum(jnp.where(row == float(n), gains[n], 0.0) for n in range(3))
        spots = dot_nt(low(spots), spread()).reshape(4, 128, 128)
        for d in range(4):
            GT[0, d // 2, d % 2] = low(spots[d] + rel).reshape(4, 2, TROWS, 128)

    def many(n, fn):
        return [functools.partial(fn, i) for i in range(n)]

    work = [
        init,
        tables,
        lambda: norm(X, 0, A1),
        lambda: (unpack(1, 0), project(A1, 0, 0, Q1)),
        lambda: project(A1, 0, 1, K1),
        lambda: (unpack_to(2, 1, 0), project(A1, 1, 0, V1)),
        *many(3, lambda i: attend(Q1, K1, V1, O1, PS, DEC, self_mask, 2 * i, 2 * i + 2)),
        self_out,
        *many(4, lambda i: (unpack_to(3, 2, 1) if i == 0 else None, project(E, 2, 0, K, i))),
        *many(4, lambda i: project(E, 2, 1, V, i)),
        lambda: (unpack_to(4, 3, 2), project(A2, 3, 0, Q2)),
        *many(6, lambda i: attend(Q2, K, V, O2, PC, ENC, cross_mask, i, i + 1)),
        cross_out,
        lambda: unpack_to(7, 4, 3),
        *many(2, lambda i: feed(i, 4)),
        lambda: in_grads(0),
        lambda: unpack_to(8, 7, 6),
        *many(2, lambda i: feed(2 + i, 7)),
        lambda: in_grads(1),
        *many(4, feed_grads),
        *many(4, lambda j: mix_back(j, 4 if j < 2 else 7)),
        norm_back_ffn,
        lambda: back_project([(C, 3, 1)], GO, low),
        *many(6, lambda i: attend_back(Q2, K, V, GO, PC, ENC, i, i + 1, nothing)),
        lambda: grad_pair(A2, Q2, O2, C, PLACE[4]),
        *many(3, lambda n: grad_pair(E, K, E, V, PLACE[5], tiles=(n,))),
        finish,
        lambda: back_project([(Q2, 3, 0)], F2, f32),
        norm_back_cross,
        lambda: back_project([(C, 1, 1)], GO, low),
        *many(3, lambda i: attend_back(Q1, K1, V1, GO, PS, DEC, 2 * i, 2 * i + 2, sum_bias)),
        lambda: grad_pair(A1, V1, O1, C, PLACE[6]),
        lambda: grad_pair(A1, Q1, A1, K1, PLACE[7]),
        *many(4, enc_grad),
        lambda: back_project([(Q1, 0, 0), (K1, 0, 1), (V1, 1, 0)], F2, f32),
        norm_back_self,
        small_grads,
    ]
    rows_g, rows_r, last = sem_rows([unit[0] - 1 for unit in GATHERED], [unit[0] for unit in REDUCED])
    g = Gather(me, BUF, ss, rs, rows_g)
    h = Gather(me, T, ss, rs, rows_g)
    r = Reduce(me, BUF, RC, gw, ss, rs, rows_r, ready, free, SLOTS, NP)
    rt = Reduce(me, GT, RCT, gt, ss, rs, rows_r, tready, tfree, 1, 1)
    na, nr = len(GATHERED), len(REDUCED)
    gathers = [g.steps(u, *unit) for u, unit in enumerate(GATHERED)] + [h.steps(na, 0, 0, 128, "zyx")]
    parts = [sum(unit[0] == p for unit in REDUCED) for p in range(NP)]
    reduces = [r.steps(u, p, PLACE[p], *cut, parts[p]) for u, (p, *cut) in enumerate(REDUCED)]
    reduces.append(rt.steps(nr, 0, 0, 0, 128, "xyz", 1))
    for code in PLAN:
        if code >= 2000:
            work[code - 2000]()
        else:
            (reduces if code >= 1000 else gathers)[code % 1000 // 10][code % 10]()
    g.drain()
    h.drain()
    r.drain()
    rt.drain()
    for cp in stores:
        cp.wait()


def layer_here(shards, dec_in, enc_out, dec_len, enc_len, cotangent):
    ns, sq, sk, sv, so, rel, nc, cq, ck, cv, co, nf, fi, fo = shards
    gains = jnp.pad(jnp.stack([ns, nc, nf]), ((0, 1), (0, 128 - OWN)))
    small = jnp.concatenate([gains, jnp.pad(rel, ((0, 8), (0, 128 - rel.shape[1])))], axis=0)
    b16, w32 = jnp.bfloat16, jnp.float32

    def vm(shape, dtype=b16):
        return pltpu.VMEM(shape, dtype)

    dec, enc = (RD, WIDTH), (RE, WIDTH)
    scratch = [
        vm((12, *CHUNKS, ROWS, COLS)),
        vm((1, *CHUNKS, TROWS, 128)),
        vm((1, *CHUNKS, TROWS, 128)),
        vm((1, 2, 4, 2, TROWS, 128)),
        vm((SLOTS, 2, 4, 2, ROWS, COLS)),
        vm(dec), vm(dec), vm(enc), vm(enc), vm(enc),
        *[vm(dec)] * 10,
        *[vm((RD, 4 * WIDTH))] * 2,
        *[vm(dec, w32)] * 4,
        vm((PAIRS, SEQS, 2 * DEC, DEC)),
        vm((PAIRS, SEQS, 2 * DEC, ENC)),
        vm((PAIRS, 2 * DEC, DEC), w32),
        vm((8, WIDTH), w32),
        vm((128, 128), w32),
        *[pltpu.SemaphoreType.DMA((sem_rows([u[0] - 1 for u in GATHERED], [u[0] for u in REDUCED])[2] + 1, 6))] * 2,
        pltpu.SemaphoreType.REGULAR((NP, 5)),
        pltpu.SemaphoreType.REGULAR((NP,)),
        pltpu.SemaphoreType.REGULAR((1, 5)),
        pltpu.SemaphoreType.REGULAR((1,)),
        pltpu.SemaphoreType.DMA((3,)),
    ]
    here, away = pl.BlockSpec(memory_space=pltpu.VMEM), pl.BlockSpec(memory_space=pl.ANY)
    scalars = pl.BlockSpec(memory_space=pltpu.SMEM)
    out, g_dec, g_enc, gw, gt = pl.pallas_call(
        layer_kernel,
        out_shape=(
            jax.ShapeDtypeStruct(dec, b16),
            jax.ShapeDtypeStruct(dec, b16),
            jax.ShapeDtypeStruct(enc, b16),
            jax.ShapeDtypeStruct((NP, ROWS, COLS), w32),
            jax.ShapeDtypeStruct((1, TROWS, 128), w32),
        ),
        in_specs=[scalars] * 2 + [away] * 3 + [here] * 12,
        out_specs=[away] * 3 + [here] * 2,
        scratch_shapes=scratch,
        compiler_params=pltpu.CompilerParams(
            collective_id=0, has_side_effects=True, vmem_limit_bytes=60 * 2**20
        ),
    )(
        dec_len.reshape(-1), enc_len.reshape(-1),
        dec_in.reshape(dec), enc_out.reshape(enc), cotangent.reshape(dec),
        small, bucket_rows(), sq, sk, sv, so, cq, ck, cv, co, fi, fo,
    )
    return deliver(out, g_dec, g_enc, gw, gt, rel.shape)


def deliver_kernel(out, gdec, genc, gw, gt, o0, o1, o2, *outs):
    grads, (w_fi, w_fo, n1, n2, n3, rel, sem) = outs[:8], outs[8:]
    moves = [(out, o0), (gdec, o1), (genc, o2)]
    at = ((7, 0), (7, 1), (6, 0), (6, 1), (4, 0), (5, 0), (5, 1), (4, 1))
    moves += [(gw.at[p, pl.ds(OWN * h, OWN)], o) for (p, h), o in zip(at, grads)]
    for j in range(4):
        moves.append((gw.at[j // 2, pl.ds(OWN * (j % 2), OWN)], w_fi.at[:, pl.ds(WIDTH * j, WIDTH)]))
    moves += [(gw.at[2 + e], w_fo.at[pl.ds(ROWS * e, ROWS)]) for e in range(2)]
    copies = [pltpu.make_async_copy(a, b, sem.at[i]) for i, (a, b) in enumerate(moves)]
    for cp in copies:
        cp.start()
    for n, o in enumerate((n1, n2, n3)):
        o[...] = gt[0, n : n + 1, :OWN]
    rel[...] = gt[0, 4 : 4 + rel.shape[0], : rel.shape[1]]
    for cp in copies:
        cp.wait()


def deliver(out, g_dec, g_enc, gw, gt, rel):
    here, away = pl.BlockSpec(memory_space=pltpu.VMEM), pl.BlockSpec(memory_space=pl.ANY)
    w32 = [(OWN, WIDTH)] * 8 + [(OWN, 4 * WIDTH), (2 * ROWS, WIDTH)] + [(1, OWN)] * 3 + [rel]
    got = pl.pallas_call(
        deliver_kernel,
        out_shape=[jax.ShapeDtypeStruct(v.shape, v.dtype) for v in (out, g_dec, g_enc)]
        + [jax.ShapeDtypeStruct(v, jnp.float32) for v in w32],
        in_specs=[away] * 4 + [here],
        out_specs=[here] * 17,
        scratch_shapes=[pltpu.SemaphoreType.DMA((17,))],
    )(out, g_dec, g_enc, gw, gt)
    sq, sk, sv, so, cq, ck, cv, co, w_fi, w_fo, n1, n2, n3, w_rel = got[3:]
    n1, n2, n3 = (v.reshape(-1) for v in (n1, n2, n3))
    return got[0], got[1], got[2], (n1, sq, sk, sv, so, w_rel, n2, cq, ck, cv, co, n3, w_fi, w_fo)


EPSILON = 1e-06
MASKED = -1000000000.0
NB = 32
AT = ("dp", "fsdp")


def bucket_table(dec_slots, bucket_count):
    near = bucket_count // 2
    places = np.arange(dec_slots, dtype=np.int32)
    distance = np.maximum(places[:, None] - places[None, :], 0).astype(np.int32)
    edges = np.array(
        [math.ceil(near * (128 / near) ** (level / near) - 1e-09) for level in range(1, near)],
        dtype=np.int32,
    )
    far = near + np.sum(
        (distance[:, :, None] >= edges[None, None, :]).astype(np.int32), axis=-1, dtype=np.int32
    )
    return np.where(distance < near, distance, far).astype(np.int32)


def rms_norm(values, gain):
    return values * lax.rsqrt(jnp.mean(values * values, axis=-1, keepdims=True) + EPSILON) * gain


def smooth(values):
    return jax.nn.gelu(values, approximate=True)


def dot_nn(a, b):
    return jnp.dot(a, b, preferred_element_type=jnp.float32)


def dot_nt(a, b):
    return lax.dot_general(a, b, (((1,), (1,)), ((), ())), preferred_element_type=jnp.float32)


def dot_tn(a, b):
    return lax.dot_general(a, b, (((0,), (0,)), ((), ())), preferred_element_type=jnp.float32)


def low(v):
    return v.astype(jnp.bfloat16)


def layer_plain(weights, dec_rows, enc_rows, dec_len, enc_len, cot_rows):
    ns, sq, sk, sv, so, rel, nc, cq, ck, cv, co, nf, fi, fo = weights
    seqs, dec_slots, width = dec_rows.shape
    enc_slots = enc_rows.shape[1]
    heads = rel.shape[1]
    size = width // heads
    ns, nc, nf = (v.astype(jnp.float32) for v in (ns, nc, nf))
    places = jnp.arange(dec_slots, dtype=jnp.int32)
    causal = places[None, :] <= places[:, None]
    self_mask = causal[None, None] & (places[None, None, None, :] < dec_len[:, None, None, None])
    enc_places = jnp.arange(enc_slots, dtype=jnp.int32)
    cross_mask = enc_places[None, None, None, :] < enc_len[:, None, None, None]
    row_mask = (places[None, :] < dec_len[:, None]).astype(jnp.float32)
    table = bucket_table(dec_slots, NB).reshape(-1)
    onehot = jnp.asarray((table[:, None] == np.arange(NB)[None, :]).astype(np.float32), jnp.bfloat16)
    bias = lax.dot_general(rel, onehot, (((0,), (1,)), ((), ())), preferred_element_type=jnp.float32)
    bias = bias.reshape(heads, dec_slots, dec_slots)[None]

    def split(t):
        return t.reshape(seqs, -1, heads, size).transpose(0, 2, 1, 3)

    def join(t):
        return t.transpose(0, 2, 1, 3).reshape(-1, width)

    def many(a, b, ca, cb):
        return lax.dot_general(
            a, b, (((ca,), (cb,)), ((0, 1), (0, 1))), preferred_element_type=jnp.float32
        )

    def attend(q, k, v, add, mask):
        s = jnp.where(mask, many(q, k, 3, 3) + add, MASKED)
        top = jnp.max(s, axis=-1, keepdims=True)
        e = jnp.exp(s - top)
        p = e / jnp.sum(e, axis=-1, keepdims=True)
        return p, low(many(low(p), v, 3, 2))

    def back(q, k, v, p, g):
        gv = low(many(low(p), g, 2, 2))
        d = many(g, v, 3, 3)
        gs = low(p * (d - jnp.sum(p * d, axis=-1, keepdims=True)))
        return low(many(gs, k, 3, 2)), low(many(gs, q, 2, 2)), gv, gs

    x = dec_rows.reshape(-1, width).astype(jnp.float32)
    enc = enc_rows.reshape(-1, width)
    a1 = low(rms_norm(x, ns))
    q1, k1, v1 = (split(low(dot_nn(a1, w))) for w in (sq, sk, sv))
    p1, o1 = attend(q1, k1, v1, bias, self_mask)
    o1 = join(o1)
    y1 = x + dot_nn(o1, so)
    a2 = low(rms_norm(y1, nc))
    q2 = split(low(dot_nn(a2, cq)))
    k2, v2 = (split(low(dot_nn(enc, w))) for w in (ck, cv))
    p2, o2 = attend(q2, k2, v2, 0.0, cross_mask)
    o2 = join(o2)
    y2 = y1 + dot_nn(o2, co)
    a3 = low(rms_norm(y2, nf))
    pre = dot_nn(a3, fi)
    hidden = low(smooth(pre))
    out = y2 + dot_nn(hidden, fo)
    g = (cot_rows.astype(jnp.float32) * row_mask[:, :, None]).reshape(-1, width)
    gf = low(g)
    w_fo = dot_tn(hidden, gf)
    gp = low(jax.vjp(smooth, pre)[1](dot_nt(gf, fo))[0])
    w_fi = dot_tn(a3, gp)
    part, w_nf = jax.vjp(rms_norm, y2, nf)[1](dot_nt(gp, fi))
    gy = g + part
    gc = low(gy)
    w_co = dot_tn(o2, gc)
    gq, gk, gv, _ = back(q2, k2, v2, p2, split(low(dot_nt(gc, co))))
    gq, gk, gv = join(gq), join(gk), join(gv)
    w_cq, w_ck, w_cv = dot_tn(a2, gq), dot_tn(enc, gk), dot_tn(enc, gv)
    g_enc = dot_nt(gk, ck) + dot_nt(gv, cv)
    part, w_nc = jax.vjp(rms_norm, y1, nc)[1](dot_nt(gq, cq))
    gy = gy + part
    ga = low(gy)
    w_so = dot_tn(o1, ga)
    gq, gk, gv, gs = back(q1, k1, v1, p1, split(low(dot_nt(ga, so))))
    w_rel = lax.dot_general(
        onehot, gs.reshape(seqs, heads, -1), (((0,), (2,)), ((), ())), preferred_element_type=jnp.float32
    ).sum(axis=1)
    gq, gk, gv = join(gq), join(gk), join(gv)
    w_sq, w_sk, w_sv = dot_tn(a1, gq), dot_tn(a1, gk), dot_tn(a1, gv)
    part, w_ns = jax.vjp(rms_norm, x, ns)[1](dot_nt(gq, sq) + dot_nt(gk, sk) + dot_nt(gv, sv))
    grads = (w_ns, w_sq, w_sk, w_sv, w_so, w_rel, w_nc, w_cq, w_ck, w_cv, w_co, w_nf, w_fi, w_fo)
    return low(out), low(gy + part), low(g_enc), grads


REL = 5


def on_device(dec_in, enc_out, dec_len, enc_len, cotangent, *shards):
    micro, per, dec_slots, width = dec_in.shape
    seqs, enc_slots = micro * per, enc_out.shape[2]
    if (lax.axis_size("dp"), lax.axis_size("fsdp"), seqs, dec_slots, enc_slots, width) == HERE:
        out, g_dec, g_enc, grads = layer_here(shards, dec_in, enc_out, dec_len, enc_len, cotangent)
    else:
        whole = [lax.all_gather(w, AT[1] if i == REL else AT, axis=0, tiled=True) for i, w in enumerate(shards)]
        out, g_dec, g_enc, grads = layer_plain(
            whole,
            dec_in.reshape(seqs, dec_slots, width),
            enc_out.reshape(seqs, enc_slots, width),
            dec_len.reshape(-1),
            enc_len.reshape(-1),
            cotangent.reshape(seqs, dec_slots, width),
        )
        grads = [
            lax.psum_scatter(
                lax.psum(w, AT[0]) if i == REL else w,
                AT[1] if i == REL else AT,
                scatter_dimension=0,
                tiled=True,
            )
            for i, w in enumerate(grads)
        ]
    return (out.reshape(dec_in.shape), g_dec.reshape(dec_in.shape), g_enc.reshape(enc_out.shape), *grads)


def solution(mesh):
    rows, seq = P(AT, None), P(None, AT, None, None)
    gain, lens, rel = P(AT), P(None, AT), P(AT[1], None)
    placed = (gain, rows, rows, rows, rows, rel, gain, rows, rows, rows, rows, gain, rows, rows)
    return jax.shard_map(
        on_device,
        mesh=mesh,
        in_specs=(seq, seq, lens, lens, seq, *placed),
        out_specs=(seq, seq, seq, *placed),
        check_vma=False,
    )
```

```python
import functools
import math

import jax
import jax.numpy as jnp
import numpy as np
from jax import lax
from jax.experimental import pallas as pl
from jax.experimental.pallas import tpu as pltpu
from jax.sharding import PartitionSpec as P

MESH = pl.DeviceIdType.MESH
NP = 8
ROWS = 48
COLS = 768
ALL = slice(None)


class Place:
    def __init__(s):
        dp, f = lax.axis_index("dp"), lax.axis_index("fsdp")
        s.c, s.y, s.x, s.z = dp % 2, dp // 2, f % 2, f // 2
        s.pos = {"x": s.x, "y": s.y, "z": s.z}

    def dev(s, c=None, y=None, z=None, x=None):
        c = s.c if c is None else c
        y = s.y if y is None else y
        z = s.z if z is None else z
        x = s.x if x is None else x
        return (y * 2 + c, z * 2 + x)

    def core(s):
        return s.dev(c=1 - s.c)

    def over(s, axis, j=1):
        if axis == "x":
            return s.dev(x=1 - s.x)
        if axis == "y":
            return s.dev(y=1 - s.y)
        return s.dev(z=(s.z + j) % 4)

    def others(s):
        return [s.over("x"), s.over("y")] + [s.over("z", j) for j in (1, 2, 3)]


def signal(sem, dev):
    pl.semaphore_signal(sem, inc=1, device_id=dev, device_id_type=MESH)


def greet(me):
    for d in me.others() + [me.core()]:
        signal(pltpu.get_barrier_semaphore(), d)


def all_here():
    pl.semaphore_wait(pltpu.get_barrier_semaphore(), 6)


class Mover:
    def __init__(s, me, ss, rs, rows):
        s.me, s.ss, s.rs, s.rows, s.sent = me, ss, rs, rows, []

    def copy(s, u, slot, src, dst, dev):
        return pltpu.make_async_remote_copy(
            src_ref=src, dst_ref=dst, send_sem=s.ss.at[s.rows[u], slot], recv_sem=s.rs.at[s.rows[u], slot],
            device_id=dev, device_id_type=MESH,
        )

    def send(s, *what):
        cp = s.copy(*what)
        cp.start()
        s.sent.append((what[0], cp))

    def arrived(s, u, slot, dst):
        s.copy(u, slot, dst, dst, s.me.core()).wait_recv()

    def drain(s, us=None):
        for u, cp in s.sent:
            if us is None or u in us:
                cp.wait_send()
        s.sent = [] if us is None else [e for e in s.sent if e[0] not in us]


class Gather(Mover):
    def __init__(s, me, A, ss, rs, rows):
        super().__init__(me, ss, rs, rows)
        s.A = A

    def steps(s, u, b, c0, nc, order):
        me = s.me

        def region(done, c=me.c, **at):
            ix = {a: (at[a] if a in at else ALL if a in done else me.pos[a]) for a in "yzx"}
            return s.A.at[b, ix["y"], c, ix["z"], ix["x"], :, pl.ds(c0, nc)]

        def hop(a, done):
            if a == "z":
                for j in (3, 2, 1):
                    s.send(u, 2 + j, region(done), region(done), me.over(a, j))
            else:
                s.send(u, 1 if a == "x" else 2, region(done), region(done), me.over(a))

        def land(a, done):
            if a == "z":
                for j in (1, 2, 3):
                    s.arrived(u, 2 + j, region(done, z=(me.z + 4 - j) % 4))
            else:
                s.arrived(u, 1 if a == "x" else 2, region(done, **{a: 1 - me.pos[a]}))

        def step(k):
            if 0 < k < 4:
                land(order[k - 1], order[: k - 1])
            if k < 3:
                hop(order[k], order[:k])
            elif k == 3:
                s.send(u, 0, region(order), region(order), me.core())
            else:
                s.arrived(u, 0, region(order, c=1 - me.c))

        return [functools.partial(step, k) for k in range(5)]


class Reduce(Mover):
    def __init__(s, me, G, RC, out, ss, rs, rows, ready, free, slots, count):
        super().__init__(me, ss, rs, rows)
        s.G, s.RC, s.out, s.ready, s.free, s.slots, s.count = G, RC, out, ready, free, slots, count
        s.todo = {}

    def steps(s, u, p, g, c0, nc, order, units):
        me, G, oc = s.me, s.G, 1 - s.me.c
        cols = pl.ds(c0, nc)
        opened, added = s.todo.setdefault(p, ([], []))

        def region(done, **at):
            ix = {a: (at[a] if a in at else me.pos[a] if a in done else ALL) for a in "yzx"}
            return G.at[g, ix["y"], me.c, ix["z"], ix["x"], :, cols]

        def slot(k, z=None):
            i = {
                "xyz": ((ALL, ALL, 0), (0, ALL, 1), (1, z, 1)),
                "yxz": ((0, ALL, ALL), (1, ALL, 0), (1, z, 1)),
                "zyx": ((ALL, z, ALL), (0, me.z, ALL), (1, me.z, 0)),
                "zxy": ((ALL, z, ALL), (ALL, me.z, 0), (0, me.z, 1)),
            }[order][k]
            return G.at[g, i[0], oc, i[1], i[2], :, cols]

        def hop(k):
            a = order[k]
            if a == "z":
                for j in (3, 2, 1):
                    s.send(u, 2 + j, region(order[:k], z=(me.z + j) % 4), slot(k, me.z), me.over(a, j))
            else:
                s.send(u, 1 if a == "x" else 2, region(order[:k], **{a: 1 - me.pos[a]}), slot(k), me.over(a))

        def land(k):
            a = order[k]
            own = region(order[:k], **{a: me.pos[a]})
            if a == "z":
                got = [(2 + j, slot(k, (me.z + 4 - j) % 4)) for j in (1, 2, 3)]
            else:
                got = [(1 if a == "x" else 2, slot(k))]
            total = own[...].astype(jnp.float32)
            for n, ref in got:
                s.arrived(u, n, ref)
                total = total + ref[...].astype(jnp.float32)
            if k == 2:
                s.out[p, :, cols] = total
            else:
                own[...] = total.astype(jnp.bfloat16)

        def core():
            return s.copy(
                u, 0, G.at[g, :, oc, :, :, :, cols], s.RC.at[p % s.slots, :, :, :, :, cols], me.core()
            )

        def first():
            if p >= s.slots and p not in s.todo[-1]:
                pl.semaphore_wait(s.free.at[p], 1)
                s.todo[-1].add(p)
            core().start()

        def open_up():
            core().wait_send()
            opened.append(u)
            if len(opened) == units:
                for i, d in enumerate(me.others()):
                    signal(s.ready.at[p, i], d)

        def second():
            s.arrived(u, 0, s.RC.at[p % s.slots, :, :, :, :, cols])
            for y in range(2):
                own, got = G.at[g, y, me.c, :, :, :, cols], s.RC.at[p % s.slots, y, :, :, :, cols]
                own[...] = (own[...].astype(jnp.float32) + got[...].astype(jnp.float32)).astype(jnp.bfloat16)
            if not added:
                for i in range(5):
                    pl.semaphore_wait(s.ready.at[p, i], 1)
            added.append(u)
            hop(0)
            if len(added) == units and p + s.slots < s.count:
                signal(s.free.at[p + s.slots], me.core())

        def later(k):
            land(k)
            if k < 2:
                hop(k + 1)

        s.todo.setdefault(-1, set())
        return [first, open_up, second] + [functools.partial(later, k) for k in range(3)]

WIDTH = 768
DEC = 128
ENC = 512
SEQS = 2
HERE = (4, 8, SEQS, DEC, ENC, WIDTH)
CHUNKS = (2, 2, 4, 2)
TROWS = 16
SLOTS = 4
OWN = WIDTH // 32
PAIRS = WIDTH // 128
HALF = WIDTH // 2
BLK = 256
RD = SEQS * DEC
RE = SEQS * ENC
GELU = math.sqrt(2.0 / math.pi)
PLACE = (9, 8, 10, 11, 4, 7, 5, 6)
GATHERED = (
    (1, 0, 128, "zyx"),
    (1, 128, 512, "zyx"),
    (1, 640, 128, "zyx"),
    (2, 0, 384, "zxy"),
    (2, 384, 256, "yzx"),
    (2, 640, 128, "zyx"),
    (3, 0, 256, "zxy"),
    (3, 256, 384, "zxy"),
    (3, 640, 128, "zyx"),
    (4, 0, 512, "xzy"),
    (4, 512, 128, "zyx"),
    (4, 640, 128, "zxy"),
    (5, 0, 384, "zyx"),
    (5, 384, 256, "xzy"),
    (5, 640, 128, "yxz"),
    (6, 0, 384, "yzx"),
    (6, 384, 256, "zyx"),
    (6, 640, 128, "xzy"),
    (7, 0, 512, "zxy"),
    (7, 512, 128, "xyz"),
    (7, 640, 128, "zyx"),
    (8, 0, 256, "zxy"),
    (8, 256, 256, "xyz"),
    (8, 512, 256, "zyx"),
)
REDUCED = (
    (0, 0, 384, "xyz"),
    (0, 384, 256, "yxz"),
    (0, 640, 128, "zxy"),
    (1, 0, 256, "xyz"),
    (1, 256, 384, "yxz"),
    (1, 640, 128, "zxy"),
    (2, 0, 640, "xyz"),
    (2, 640, 128, "zxy"),
    (3, 0, 640, "yxz"),
    (3, 640, 128, "zyx"),
    (4, 0, 384, "xyz"),
    (4, 384, 256, "yxz"),
    (4, 640, 128, "zyx"),
    (5, 0, 384, "xyz"),
    (5, 384, 256, "yxz"),
    (5, 640, 128, "zyx"),
    (6, 0, 256, "xyz"),
    (6, 256, 384, "yxz"),
    (6, 640, 128, "zyx"),
    (7, 0, 384, "xyz"),
    (7, 384, 384, "yxz"),
)
PLAN = (
    240, 2000, 90, 100, 110, 0, 10, 20, 60, 241, 70, 80, 91, 101, 242, 111,
    1, 102, 243, 112, 244, 2001, 11, 21, 2, 103, 2002, 61, 113, 104, 30, 40,
    50, 114, 71, 3, 81, 4, 12, 62, 22, 41, 82, 72, 150, 160, 170, 63,
    92, 64, 120, 130, 140, 31, 51, 13, 73, 180, 190, 200, 23, 14, 151, 74,
    24, 2003, 42, 83, 171, 131, 161, 2004, 84, 210, 220, 230, 32, 191, 121, 93,
    141, 52, 43, 94, 221, 181, 142, 162, 201, 44, 53, 54, 33, 182, 192, 152,
    34, 2005, 172, 2006, 122, 2007, 222, 163, 2008, 202, 2009, 132, 164, 2010, 2011, 2012,
    211, 2013, 2014, 2015, 231, 2016, 153, 2017, 2018, 2019, 154, 2020, 183, 2021, 143, 2022,
    173, 2023, 123, 144, 184, 2024, 174, 2025, 193, 124, 203, 133, 194, 212, 204, 134,
    2026, 232, 2027, 2028, 2029, 1000, 1010, 1020, 1001, 213, 1011, 1021, 223, 233, 1002, 214,
    1012, 1022, 224, 234, 2030, 2031, 2032, 2033, 1030, 1040, 1050, 2034, 1031, 2035, 2036, 1013,
    1041, 1051, 2037, 1060, 1070, 1080, 1090, 1003, 1032, 2038, 2039, 1061, 1023, 1071, 1042, 1052,
    1014, 1081, 1091, 2040, 1062, 1072, 1004, 1082, 1092, 1033, 1024, 2041, 2042, 2043, 2044, 2045,
    2046, 1043, 1053, 2047, 2048, 1015, 2049, 2050, 1100, 1110, 1120, 2051, 1101, 2052, 1063, 1073,
    1111, 1121, 2053, 1130, 1140, 1150, 1102, 1044, 1005, 1083, 1074, 1131, 1141, 1151, 1054, 1112,
    1122, 1034, 1025, 2054, 1132, 1142, 1152, 1093, 2055, 2056, 1075, 1064, 1045, 1055, 1103, 2057,
    2058, 2059, 2060, 2061, 1113, 1123, 1084, 1035, 1160, 1170, 1180, 2062, 1190, 1200, 1161, 2063,
    1171, 1181, 1143, 2064, 1094, 1191, 1162, 1153, 1201, 1172, 1182, 1133, 1192, 1104, 1202, 1154,
    1114, 1124, 2065, 2066, 1065, 1144, 1095, 2067, 2068, 2069, 1085, 1163, 1173, 1210, 1211, 1134,
    1183, 1212, 1193, 1155, 1125, 1105, 1115, 1203, 1174, 1213, 1145, 1164, 1184, 1135, 1194, 1204,
    1185, 1214, 1175, 1165, 1195, 1205, 1215,
)


def bucket_rows():
    table = bucket_table(DEC, NB)[:, 0]
    far = table[(-np.arange(DEC)) % DEC]
    rows = np.full((8, TROWS), -1)
    rows[:, 4:8] = np.arange(NB).reshape(8, 4)
    return jnp.asarray((rows.reshape(-1, 1) == far[None, :]).astype(np.float32), jnp.bfloat16)


def sem_rows(gathered, reduced):
    deep = [max(gathered.count(p), reduced.count(p)) for p in range(NP)]

    def rows(pieces):
        return [sum(deep[:p]) + pieces[:i].count(p) for i, p in enumerate(pieces)] + [sum(deep)]

    return rows(gathered), rows(reduced), sum(deep)


def loop(n, body):
    def step(i, carry):
        body(i)
        return carry

    lax.fori_loop(0, n, step, 0)


def tile(i, n):
    return pl.ds(pl.multiple_of(i * n, n), n)


def f32(v):
    return v.astype(jnp.float32)


def layer_kernel(
    dlen, elen, dec_hbm, enc_hbm, cot_hbm, small, bmap,
    sq, sk, sv, so, cq, ck, cv, co, fi, fo,
    out_hbm, gdec_hbm, genc_hbm, gw, gt,
    BUF, T, GT, RCT, RC,
    X, C, E, K, V, A1, Q1, K1, V1, O1, A2, Q2, O2, A3, GO, HID, GP,
    Y1, Y2, F2, GY, PS, PC, BIAS, NRM, DM,
    ss, rs, ready, free, tready, tfree, lsem,
):
    me = Place()
    greet(me)
    loads = [
        pltpu.make_async_copy(a, b, lsem.at[i])
        for i, (a, b) in enumerate(((dec_hbm, X), (cot_hbm, C), (enc_hbm, E)))
    ]
    for cp in loads:
        cp.start()

    def pack(p, top, bottom):
        both = jnp.concatenate([f32(top), f32(bottom)], axis=0)
        BUF[p + 1, me.y, me.c, me.z, me.x] = low(both)

    pack(0, sq[...], sk[...])
    pack(1, sv[...], so[...])
    pack(2, ck[...], cv[...])
    pack(3, cq[...], co[...])
    BUF[5, me.y, me.c, me.z, me.x] = fo[0:48]
    BUF[6, me.y, me.c, me.z, me.x] = fo[48:96]
    for h in range(2):
        pack(6 + h, fi[:, 1536 * h : 1536 * h + 768], fi[:, 1536 * h + 768 : 1536 * h + 1536])
    T[0, me.y, me.c, me.z, me.x] = small[...]
    all_here()

    def first_lanes(shape):
        return lax.broadcasted_iota(jnp.int32, shape, 1) < 64

    def two(v):
        keep = first_lanes(v.shape)
        w = f32(v)
        return low(jnp.concatenate([jnp.where(keep, w, 0.0), jnp.where(keep, 0.0, w)], axis=0))

    def one(v):
        return jnp.where(first_lanes((DEC, 128)), v[:DEC], v[DEC:])

    def unpack(src, dst):
        def body(i):
            for z in range(4):
                w = f32(BUF[src, i // 2, i % 2, z])
                for k in range(2):
                    rows = slice(OWN * k, OWN * k + OWN)
                    both = low(jnp.concatenate([w[0, rows], w[1, rows]], axis=0))
                    BUF[dst, k, i // 2, (i % 2) * 2 + z // 2, z % 2] = both

        loop(4, body)

    def whole(b, k):
        return BUF[b, k].reshape(WIDTH, WIDTH)

    def project(a, b, k, dst, i=0):
        r = slice(i * RD, i * RD + RD)
        dst[r, :] = low(dot_nn(a[r, :], whole(b, k)))

    def project_add(a, b, k, base, dst):
        dst[...] = f32(base[...]) + dot_nn(a[...], whole(b, k))

    def norm(v, gain, dst):
        def body(i):
            r = tile(i, 128)
            x = f32(v[r, :])
            s = lax.rsqrt(jnp.mean(x * x, axis=-1, keepdims=True) + EPSILON)
            dst[r, :] = low(x * s * NRM[gain : gain + 1, :])

        loop(RD // 128, body)

    def norm_back(v, gain, G, base, dst):
        def body(i, total):
            r = tile(i, 64)
            x = f32(v[r, :])
            s = lax.rsqrt(jnp.mean(x * x, axis=-1, keepdims=True) + EPSILON)
            n = x * s
            w = G[r, :]
            u = w * NRM[gain : gain + 1, :]
            dst[r, :] = f32(base[r, :]) + s * (u - n * jnp.mean(u * n, axis=-1, keepdims=True))
            return total + jnp.sum((w * n).reshape(8, 8, WIDTH), axis=0)

        total = lax.fori_loop(0, RD // 64, body, jnp.zeros((8, WIDTH), jnp.float32))
        return jnp.sum(total, axis=0, keepdims=True)

    def softmax(s):
        e = jnp.exp(s - jnp.max(s, axis=-1, keepdims=True))
        return e * (1.0 / jnp.sum(e, axis=-1, keepdims=True))

    def attend(q, k, v, o, probs, slots, mask, lo, hi):
        def body(j):
            i = j + lo
            lanes = tile(i, 128)
            for at in range(SEQS):
                r, kr = slice(at * DEC, at * DEC + DEC), slice(at * slots, at * slots + slots)
                s = dot_nt(two(q[r, lanes]), k[kr, lanes])
                p = low(softmax(mask(s, at, i)))
                probs[i, at] = p
                o[r, lanes] = low(one(dot_nn(p, v[kr, lanes])))

        loop(hi - lo, body)

    def attend_back(q, k, v, go, probs, slots, lo, hi, extra):
        def body(j):
            i = j + lo
            lanes = tile(i, 128)
            for at in range(SEQS):
                r, kr = slice(at * DEC, at * DEC + DEC), slice(at * slots, at * slots + slots)
                q2, g2, p = two(q[r, lanes]), two(go[r, lanes]), probs[i, at]
                d = dot_nt(g2, v[kr, lanes])
                pf = f32(p)
                gs = low(pf * (d - jnp.sum(pf * d, axis=-1, keepdims=True)))
                v[kr, lanes] = low(dot_tn(p, g2))
                q[r, lanes] = low(one(dot_nn(gs, k[kr, lanes])))
                k[kr, lanes] = low(dot_tn(gs, q2))
                extra(gs, i)

        loop(hi - lo, body)

    def back_project(pairs, dst, cast, i=0):
        r = slice(i * RD, i * RD + RD)
        v = None
        for a, b, k in pairs:
            d = dot_nt(a[r, :], whole(b, k))
            v = d if v is None else v + d
        dst[r, :] = cast(v)

    def grad_pair(aa, ga, ab, gb, place, oa=0, ob=0, tiles=(0, 1, 2)):
        for n in tiles:
            va = dot_tn(aa[...], ga[:, (n + oa) * BLK : (n + oa + 1) * BLK]).reshape(32, OWN, BLK)
            vb = dot_tn(ab[...], gb[:, (n + ob) * BLK : (n + ob + 1) * BLK]).reshape(32, OWN, BLK)
            both = low(jnp.concatenate([va, vb], axis=1))
            BUF[place, :, :, :, :, :, n * BLK : (n + 1) * BLK] = both.reshape(2, 2, 4, 2, ROWS, BLK)

    owner = jnp.floor((f32(lax.broadcasted_iota(jnp.int32, (1, WIDTH), 1)) + 0.5) * (1.0 / OWN))

    def spread():
        place = f32(lax.broadcasted_iota(jnp.int32, (128, WIDTH), 1)) - OWN * owner
        return low(jnp.where(place == f32(lax.broadcasted_iota(jnp.int32, (128, WIDTH), 0)), 1.0, 0.0))

    row = f32(lax.broadcasted_iota(jnp.int32, (32 * TROWS, 1), 0)) - TROWS * owner
    def self_mask(s, at, pair):
        k = lax.broadcasted_iota(jnp.int32, s.shape, 1)
        q = lax.broadcasted_iota(jnp.int32, s.shape, 0) % DEC
        return jnp.where((k <= q) & (k < dlen[at]), s + BIAS[pair], MASKED)

    def cross_mask(s, at, pair):
        return jnp.where(lax.broadcasted_iota(jnp.int32, s.shape, 1) < elen[at], s, MASKED)

    def out_rows(j):
        return jnp.concatenate([BUF[b, j // 2, j % 2] for b in (5, 6)], axis=2).reshape(WIDTH, WIDTH)

    def feed(j, b):
        k = j % 2
        pre = dot_nn(A3[...], whole(b, k))
        gh = dot_nt(C[...], out_rows(j))
        th = jnp.tanh(GELU * (pre + 0.044715 * (pre * pre * pre)))
        HID[:, j * WIDTH : (j + 1) * WIDTH] = low(0.5 * pre * (1.0 + th))
        slope = 0.5 * (1.0 + th) + 0.5 * pre * (1.0 - th * th) * (GELU * (1.0 + 0.134145 * (pre * pre)))
        GP[:, j * WIDTH : (j + 1) * WIDTH] = low(slope * gh)

    def feed_grads(j):
        for n in range(3):
            w = low(dot_tn(HID[:, j * WIDTH : (j + 1) * WIDTH], C[:, n * BLK : (n + 1) * BLK]))
            w = w.reshape(4, 2, 2 * ROWS, BLK)
            for e in range(2):
                part = w[:, :, ROWS * e : ROWS * e + ROWS]
                BUF[PLACE[2 + e], j // 2, j % 2, :, :, :, n * BLK : (n + 1) * BLK] = part

    def mix_back(j, b):
        d = dot_nt(GP[:, j * WIDTH : (j + 1) * WIDTH], whole(b, j % 2))
        F2[...] = d if j == 0 else F2[...] + d

    def mix():
        v = Y2[...]
        for j in range(4):
            v = v + dot_nn(HID[:, j * WIDTH : (j + 1) * WIDTH], out_rows(j))
        A3[...] = low(v)


    def cast_rows(src, dst):
        def body(i):
            q = tile(i, 64)
            dst[q, :] = low(src[q, :])

        loop(RD // 64, body)

    def nothing(gs, pair):
        pass

    def sum_bias(gs, pair):
        BIAS[pair] += f32(gs)

    def done(*pieces):
        g.drain([u for u, unit in enumerate(GATHERED) if unit[0] - 1 in pieces])

    stores, gains = [], {}

    def store(src, dst, i):
        stores.append(pltpu.make_async_copy(src, dst, lsem.at[i]))
        stores[-1].start()

    def init():
        for cp in loads:
            cp.wait()
        place = lax.broadcasted_iota(jnp.int32, (DEC, WIDTH), 0)
        for s in range(SEQS):
            r = slice(DEC * s, DEC * s + DEC)
            C[r, :] = low(jnp.where(place < dlen[s], f32(C[r, :]), 0.0))

    def tables():
        h.drain()
        table = T[0].reshape(32 * TROWS, 128)
        wide = dot_nn(table, spread())
        NRM[...] = jnp.concatenate(
            [jnp.sum(jnp.where(row == float(n), wide, 0.0), axis=0, keepdims=True) for n in range(3)]
            + [jnp.zeros((5, WIDTH), jnp.float32)],
            axis=0,
        )
        DM[...] = dot_tn(T[0, 0, 0].reshape(8 * TROWS, 128), bmap[...])
        for j in range(2 * PAIRS):
            v = jnp.broadcast_to(DM[j : j + 1, :], (DEC, DEC))
            BIAS[j // 2, DEC * (j % 2) : DEC * (j % 2) + DEC, :] = pltpu.roll(v, 0, 1, stride=1, stride_axis=0)

    def unpack_to(src, dst, *pieces):
        done(*pieces)
        unpack(src, dst)

    def self_out():
        project_add(O1, 1, 1, X, Y1)
        norm(Y1, 1, A2)

    def cross_out():
        project_add(O2, 3, 1, Y1, Y2)
        norm(Y2, 2, A3)

    def in_grads(h):
        if h:
            done(4, 5, 7)
        grad_pair(A3, GP, A3, GP, PLACE[h], 6 * h, 6 * h + 3)

    def finish():
        mix()
        store(A3, out_hbm, 0)

    def norm_back_ffn():
        gains[2] = norm_back(Y2, 2, F2, C, GY)
        cast_rows(GY, C)

    def norm_back_cross():
        gains[1] = norm_back(Y1, 1, F2, GY, GY)
        cast_rows(GY, C)
        BIAS[...] = jnp.zeros_like(BIAS)

    def norm_back_self():
        gains[0] = norm_back(X, 0, F2, GY, GY)
        cast_rows(GY, GO)
        store(GO, gdec_hbm, 1)

    def enc_grad(i):
        back_project([(K, 2, 0), (V, 2, 1)], E, low, i)
        if i == 3:
            store(E, genc_hbm, 2)

    def small_grads():
        DM[...] = jnp.zeros_like(DM)
        flip = lax.broadcasted_iota(jnp.int32, (DEC, DEC), 0) + lax.broadcasted_iota(jnp.int32, (DEC, DEC), 1)
        flip = low(jnp.where(flip == DEC - 1, 1.0, 0.0))
        for j in range(2 * PAIRS):
            v = BIAS[j // 2, DEC * (j % 2) : DEC * (j % 2) + DEC, :]
            hi = low(v)
            v = dot_nn(flip, hi) + dot_nn(flip, low(v - f32(hi)))
            v = pltpu.roll(v, 0, 1, stride=1, stride_axis=0)
            DM[j : j + 1, :] = jnp.sum(v, axis=0, keepdims=True)
        DM[...] = pltpu.roll(DM[...], 1, 1)
        hi = low(DM[...])
        rel = dot_nt(bmap[...], hi) + dot_nt(bmap[...], low(DM[...] - f32(hi)))
        spots = sum(jnp.where(row == float(n), gains[n], 0.0) for n in range(3))
        spots = dot_nt(low(spots), spread()).reshape(4, 128, 128)
        for d in range(4):
            GT[0, d // 2, d % 2] = low(spots[d] + rel).reshape(4, 2, TROWS, 128)

    def many(n, fn):
        return [functools.partial(fn, i) for i in range(n)]

    work = [
        init,
        tables,
        lambda: norm(X, 0, A1),
        lambda: (unpack(1, 0), project(A1, 0, 0, Q1)),
        lambda: project(A1, 0, 1, K1),
        lambda: (unpack_to(2, 1, 0), project(A1, 1, 0, V1)),
        *many(3, lambda i: attend(Q1, K1, V1, O1, PS, DEC, self_mask, 2 * i, 2 * i + 2)),
        self_out,
        *many(4, lambda i: (unpack_to(3, 2, 1) if i == 0 else None, project(E, 2, 0, K, i))),
        *many(4, lambda i: project(E, 2, 1, V, i)),
        lambda: (unpack_to(4, 3, 2), project(A2, 3, 0, Q2)),
        *many(6, lambda i: attend(Q2, K, V, O2, PC, ENC, cross_mask, i, i + 1)),
        cross_out,
        lambda: unpack_to(7, 4, 3),
        *many(2, lambda i: feed(i, 4)),
        lambda: in_grads(0),
        lambda: unpack_to(8, 7, 6),
        *many(2, lambda i: feed(2 + i, 7)),
        lambda: in_grads(1),
        *many(4, feed_grads),
        *many(4, lambda j: mix_back(j, 4 if j < 2 else 7)),
        norm_back_ffn,
        lambda: back_project([(C, 3, 1)], GO, low),
        *many(6, lambda i: attend_back(Q2, K, V, GO, PC, ENC, i, i + 1, nothing)),
        lambda: grad_pair(A2, Q2, O2, C, PLACE[4]),
        *many(3, lambda n: grad_pair(E, K, E, V, PLACE[5], tiles=(n,))),
        finish,
        lambda: back_project([(Q2, 3, 0)], F2, f32),
        norm_back_cross,
        lambda: back_project([(C, 1, 1)], GO, low),
        *many(3, lambda i: attend_back(Q1, K1, V1, GO, PS, DEC, 2 * i, 2 * i + 2, sum_bias)),
        lambda: grad_pair(A1, V1, O1, C, PLACE[6]),
        lambda: grad_pair(A1, Q1, A1, K1, PLACE[7]),
        *many(4, enc_grad),
        lambda: back_project([(Q1, 0, 0), (K1, 0, 1), (V1, 1, 0)], F2, f32),
        norm_back_self,
        small_grads,
    ]
    rows_g, rows_r, last = sem_rows([unit[0] - 1 for unit in GATHERED], [unit[0] for unit in REDUCED])
    g = Gather(me, BUF, ss, rs, rows_g)
    h = Gather(me, T, ss, rs, rows_g)
    r = Reduce(me, BUF, RC, gw, ss, rs, rows_r, ready, free, SLOTS, NP)
    rt = Reduce(me, GT, RCT, gt, ss, rs, rows_r, tready, tfree, 1, 1)
    na, nr = len(GATHERED), len(REDUCED)
    gathers = [g.steps(u, *unit) for u, unit in enumerate(GATHERED)] + [h.steps(na, 0, 0, 128, "zyx")]
    parts = [sum(unit[0] == p for unit in REDUCED) for p in range(NP)]
    reduces = [r.steps(u, p, PLACE[p], *cut, parts[p]) for u, (p, *cut) in enumerate(REDUCED)]
    reduces.append(rt.steps(nr, 0, 0, 0, 128, "xyz", 1))
    for code in PLAN:
        if code >= 2000:
            work[code - 2000]()
        else:
            (reduces if code >= 1000 else gathers)[code % 1000 // 10][code % 10]()
    g.drain()
    h.drain()
    r.drain()
    rt.drain()
    for cp in stores:
        cp.wait()


def layer_here(shards, dec_in, enc_out, dec_len, enc_len, cotangent):
    ns, sq, sk, sv, so, rel, nc, cq, ck, cv, co, nf, fi, fo = shards
    gains = jnp.pad(jnp.stack([ns, nc, nf]), ((0, 1), (0, 128 - OWN)))
    small = jnp.concatenate([gains, jnp.pad(rel, ((0, 8), (0, 128 - rel.shape[1])))], axis=0)
    b16, w32 = jnp.bfloat16, jnp.float32

    def vm(shape, dtype=b16):
        return pltpu.VMEM(shape, dtype)

    dec, enc = (RD, WIDTH), (RE, WIDTH)
    scratch = [
        vm((12, *CHUNKS, ROWS, COLS)),
        vm((1, *CHUNKS, TROWS, 128)),
        vm((1, *CHUNKS, TROWS, 128)),
        vm((1, 2, 4, 2, TROWS, 128)),
        vm((SLOTS, 2, 4, 2, ROWS, COLS)),
        vm(dec), vm(dec), vm(enc), vm(enc), vm(enc),
        *[vm(dec)] * 10,
        *[vm((RD, 4 * WIDTH))] * 2,
        *[vm(dec, w32)] * 4,
        vm((PAIRS, SEQS, 2 * DEC, DEC)),
        vm((PAIRS, SEQS, 2 * DEC, ENC)),
        vm((PAIRS, 2 * DEC, DEC), w32),
        vm((8, WIDTH), w32),
        vm((128, 128), w32),
        *[pltpu.SemaphoreType.DMA((sem_rows([u[0] - 1 for u in GATHERED], [u[0] for u in REDUCED])[2] + 1, 6))] * 2,
        pltpu.SemaphoreType.REGULAR((NP, 5)),
        pltpu.SemaphoreType.REGULAR((NP,)),
        pltpu.SemaphoreType.REGULAR((1, 5)),
        pltpu.SemaphoreType.REGULAR((1,)),
        pltpu.SemaphoreType.DMA((3,)),
    ]
    here, away = pl.BlockSpec(memory_space=pltpu.VMEM), pl.BlockSpec(memory_space=pl.ANY)
    scalars = pl.BlockSpec(memory_space=pltpu.SMEM)
    out, g_dec, g_enc, gw, gt = pl.pallas_call(
        layer_kernel,
        out_shape=(
            jax.ShapeDtypeStruct(dec, b16),
            jax.ShapeDtypeStruct(dec, b16),
            jax.ShapeDtypeStruct(enc, b16),
            jax.ShapeDtypeStruct((NP, ROWS, COLS), w32),
            jax.ShapeDtypeStruct((1, TROWS, 128), w32),
        ),
        in_specs=[scalars] * 2 + [away] * 3 + [here] * 12,
        out_specs=[away] * 3 + [here] * 2,
        scratch_shapes=scratch,
        compiler_params=pltpu.CompilerParams(
            collective_id=0, has_side_effects=True, vmem_limit_bytes=60 * 2**20
        ),
    )(
        dec_len.reshape(-1), enc_len.reshape(-1),
        dec_in.reshape(dec), enc_out.reshape(enc), cotangent.reshape(dec),
        small, bucket_rows(), sq, sk, sv, so, cq, ck, cv, co, fi, fo,
    )
    gt = gt[0]
    top, bottom = gw[:, :OWN], gw[:, OWN:]
    w_fi = jnp.concatenate([top[0], bottom[0], top[1], bottom[1]], axis=1)
    w_fo = gw[2:4].reshape(2 * ROWS, COLS)
    gains = [gt[n, :OWN] for n in range(3)]
    w_rel = gt[4 : 4 + rel.shape[0], : rel.shape[1]]
    return out, g_dec, g_enc, (
        gains[0], top[7], bottom[7], top[6], bottom[6], w_rel,
        gains[1], top[4], top[5], bottom[5], bottom[4], gains[2], w_fi, w_fo,
    )


EPSILON = 1e-06
MASKED = -1000000000.0
NB = 32
AT = ("dp", "fsdp")


def bucket_table(dec_slots, bucket_count):
    near = bucket_count // 2
    places = np.arange(dec_slots, dtype=np.int32)
    distance = np.maximum(places[:, None] - places[None, :], 0).astype(np.int32)
    edges = np.array(
        [math.ceil(near * (128 / near) ** (level / near) - 1e-09) for level in range(1, near)],
        dtype=np.int32,
    )
    far = near + np.sum(
        (distance[:, :, None] >= edges[None, None, :]).astype(np.int32), axis=-1, dtype=np.int32
    )
    return np.where(distance < near, distance, far).astype(np.int32)


def rms_norm(values, gain):
    return values * lax.rsqrt(jnp.mean(values * values, axis=-1, keepdims=True) + EPSILON) * gain


def smooth(values):
    return jax.nn.gelu(values, approximate=True)


def dot_nn(a, b):
    return jnp.dot(a, b, preferred_element_type=jnp.float32)


def dot_nt(a, b):
    return lax.dot_general(a, b, (((1,), (1,)), ((), ())), preferred_element_type=jnp.float32)


def dot_tn(a, b):
    return lax.dot_general(a, b, (((0,), (0,)), ((), ())), preferred_element_type=jnp.float32)


def low(v):
    return v.astype(jnp.bfloat16)


def layer_plain(weights, dec_rows, enc_rows, dec_len, enc_len, cot_rows):
    ns, sq, sk, sv, so, rel, nc, cq, ck, cv, co, nf, fi, fo = weights
    seqs, dec_slots, width = dec_rows.shape
    enc_slots = enc_rows.shape[1]
    heads = rel.shape[1]
    size = width // heads
    ns, nc, nf = (v.astype(jnp.float32) for v in (ns, nc, nf))
    places = jnp.arange(dec_slots, dtype=jnp.int32)
    causal = places[None, :] <= places[:, None]
    self_mask = causal[None, None] & (places[None, None, None, :] < dec_len[:, None, None, None])
    enc_places = jnp.arange(enc_slots, dtype=jnp.int32)
    cross_mask = enc_places[None, None, None, :] < enc_len[:, None, None, None]
    row_mask = (places[None, :] < dec_len[:, None]).astype(jnp.float32)
    table = bucket_table(dec_slots, NB).reshape(-1)
    onehot = jnp.asarray((table[:, None] == np.arange(NB)[None, :]).astype(np.float32), jnp.bfloat16)
    bias = lax.dot_general(rel, onehot, (((0,), (1,)), ((), ())), preferred_element_type=jnp.float32)
    bias = bias.reshape(heads, dec_slots, dec_slots)[None]

    def split(t):
        return t.reshape(seqs, -1, heads, size).transpose(0, 2, 1, 3)

    def join(t):
        return t.transpose(0, 2, 1, 3).reshape(-1, width)

    def many(a, b, ca, cb):
        return lax.dot_general(
            a, b, (((ca,), (cb,)), ((0, 1), (0, 1))), preferred_element_type=jnp.float32
        )

    def attend(q, k, v, add, mask):
        s = jnp.where(mask, many(q, k, 3, 3) + add, MASKED)
        top = jnp.max(s, axis=-1, keepdims=True)
        e = jnp.exp(s - top)
        p = e / jnp.sum(e, axis=-1, keepdims=True)
        return p, low(many(low(p), v, 3, 2))

    def back(q, k, v, p, g):
        gv = low(many(low(p), g, 2, 2))
        d = many(g, v, 3, 3)
        gs = low(p * (d - jnp.sum(p * d, axis=-1, keepdims=True)))
        return low(many(gs, k, 3, 2)), low(many(gs, q, 2, 2)), gv, gs

    x = dec_rows.reshape(-1, width).astype(jnp.float32)
    enc = enc_rows.reshape(-1, width)
    a1 = low(rms_norm(x, ns))
    q1, k1, v1 = (split(low(dot_nn(a1, w))) for w in (sq, sk, sv))
    p1, o1 = attend(q1, k1, v1, bias, self_mask)
    o1 = join(o1)
    y1 = x + dot_nn(o1, so)
    a2 = low(rms_norm(y1, nc))
    q2 = split(low(dot_nn(a2, cq)))
    k2, v2 = (split(low(dot_nn(enc, w))) for w in (ck, cv))
    p2, o2 = attend(q2, k2, v2, 0.0, cross_mask)
    o2 = join(o2)
    y2 = y1 + dot_nn(o2, co)
    a3 = low(rms_norm(y2, nf))
    pre = dot_nn(a3, fi)
    hidden = low(smooth(pre))
    out = y2 + dot_nn(hidden, fo)
    g = (cot_rows.astype(jnp.float32) * row_mask[:, :, None]).reshape(-1, width)
    gf = low(g)
    w_fo = dot_tn(hidden, gf)
    gp = low(jax.vjp(smooth, pre)[1](dot_nt(gf, fo))[0])
    w_fi = dot_tn(a3, gp)
    part, w_nf = jax.vjp(rms_norm, y2, nf)[1](dot_nt(gp, fi))
    gy = g + part
    gc = low(gy)
    w_co = dot_tn(o2, gc)
    gq, gk, gv, _ = back(q2, k2, v2, p2, split(low(dot_nt(gc, co))))
    gq, gk, gv = join(gq), join(gk), join(gv)
    w_cq, w_ck, w_cv = dot_tn(a2, gq), dot_tn(enc, gk), dot_tn(enc, gv)
    g_enc = dot_nt(gk, ck) + dot_nt(gv, cv)
    part, w_nc = jax.vjp(rms_norm, y1, nc)[1](dot_nt(gq, cq))
    gy = gy + part
    ga = low(gy)
    w_so = dot_tn(o1, ga)
    gq, gk, gv, gs = back(q1, k1, v1, p1, split(low(dot_nt(ga, so))))
    w_rel = lax.dot_general(
        onehot, gs.reshape(seqs, heads, -1), (((0,), (2,)), ((), ())), preferred_element_type=jnp.float32
    ).sum(axis=1)
    gq, gk, gv = join(gq), join(gk), join(gv)
    w_sq, w_sk, w_sv = dot_tn(a1, gq), dot_tn(a1, gk), dot_tn(a1, gv)
    part, w_ns = jax.vjp(rms_norm, x, ns)[1](dot_nt(gq, sq) + dot_nt(gk, sk) + dot_nt(gv, sv))
    grads = (w_ns, w_sq, w_sk, w_sv, w_so, w_rel, w_nc, w_cq, w_ck, w_cv, w_co, w_nf, w_fi, w_fo)
    return low(out), low(gy + part), low(g_enc), grads


REL = 5


def on_device(dec_in, enc_out, dec_len, enc_len, cotangent, *shards):
    micro, per, dec_slots, width = dec_in.shape
    seqs, enc_slots = micro * per, enc_out.shape[2]
    if (lax.axis_size("dp"), lax.axis_size("fsdp"), seqs, dec_slots, enc_slots, width) == HERE:
        out, g_dec, g_enc, grads = layer_here(shards, dec_in, enc_out, dec_len, enc_len, cotangent)
    else:
        whole = [lax.all_gather(w, AT[1] if i == REL else AT, axis=0, tiled=True) for i, w in enumerate(shards)]
        out, g_dec, g_enc, grads = layer_plain(
            whole,
            dec_in.reshape(seqs, dec_slots, width),
            enc_out.reshape(seqs, enc_slots, width),
            dec_len.reshape(-1),
            enc_len.reshape(-1),
            cotangent.reshape(seqs, dec_slots, width),
        )
        grads = [
            lax.psum_scatter(
                lax.psum(w, AT[0]) if i == REL else w,
                AT[1] if i == REL else AT,
                scatter_dimension=0,
                tiled=True,
            )
            for i, w in enumerate(grads)
        ]
    return (out.reshape(dec_in.shape), g_dec.reshape(dec_in.shape), g_enc.reshape(enc_out.shape), *grads)


def solution(mesh):
    rows, seq = P(AT, None), P(None, AT, None, None)
    gain, lens, rel = P(AT), P(None, AT), P(AT[1], None)
    placed = (gain, rows, rows, rows, rows, rel, gain, rows, rows, rows, rows, gain, rows, rows)
    return jax.shard_map(
        on_device,
        mesh=mesh,
        in_specs=(seq, seq, lens, lens, seq, *placed),
        out_specs=(seq, seq, seq, *placed),
        check_vma=False,
    )
```

```python
import functools
import math

import jax
import jax.numpy as jnp
import numpy as np
from jax import lax
from jax.experimental import pallas as pl
from jax.experimental.pallas import tpu as pltpu
from jax.sharding import PartitionSpec as P

MESH = pl.DeviceIdType.MESH
NP = 8
ROWS = 48
COLS = 768
ALL = slice(None)


class Place:
    def __init__(s):
        dp, f = lax.axis_index("dp"), lax.axis_index("fsdp")
        s.c, s.y, s.x, s.z = dp % 2, dp // 2, f % 2, f // 2
        s.pos = {"x": s.x, "y": s.y, "z": s.z}

    def dev(s, c=None, y=None, z=None, x=None):
        c = s.c if c is None else c
        y = s.y if y is None else y
        z = s.z if z is None else z
        x = s.x if x is None else x
        return (y * 2 + c, z * 2 + x)

    def core(s):
        return s.dev(c=1 - s.c)

    def over(s, axis, j=1):
        if axis == "x":
            return s.dev(x=1 - s.x)
        if axis == "y":
            return s.dev(y=1 - s.y)
        return s.dev(z=(s.z + j) % 4)

    def others(s):
        return [s.over("x"), s.over("y")] + [s.over("z", j) for j in (1, 2, 3)]


def signal(sem, dev):
    pl.semaphore_signal(sem, inc=1, device_id=dev, device_id_type=MESH)


def greet(me):
    for d in me.others() + [me.core()]:
        signal(pltpu.get_barrier_semaphore(), d)


def all_here():
    pl.semaphore_wait(pltpu.get_barrier_semaphore(), 6)


class Mover:
    def __init__(s, me, ss, rs, rows):
        s.me, s.ss, s.rs, s.rows, s.sent = me, ss, rs, rows, []

    def copy(s, u, slot, src, dst, dev):
        return pltpu.make_async_remote_copy(
            src_ref=src, dst_ref=dst, send_sem=s.ss.at[s.rows[u], slot], recv_sem=s.rs.at[s.rows[u], slot],
            device_id=dev, device_id_type=MESH,
        )

    def send(s, *what):
        cp = s.copy(*what)
        cp.start()
        s.sent.append((what[0], cp))

    def arrived(s, u, slot, dst):
        s.copy(u, slot, dst, dst, s.me.core()).wait_recv()

    def drain(s, us=None):
        for u, cp in s.sent:
            if us is None or u in us:
                cp.wait_send()
        s.sent = [] if us is None else [e for e in s.sent if e[0] not in us]


class Gather(Mover):
    def __init__(s, me, A, ss, rs, rows):
        super().__init__(me, ss, rs, rows)
        s.A = A

    def steps(s, u, b, c0, nc, order):
        me = s.me

        def region(done, c=me.c, **at):
            ix = {a: (at[a] if a in at else ALL if a in done else me.pos[a]) for a in "yzx"}
            return s.A.at[b, ix["y"], c, ix["z"], ix["x"], :, pl.ds(c0, nc)]

        def hop(a, done):
            if a == "z":
                for j in (3, 2, 1):
                    s.send(u, 2 + j, region(done), region(done), me.over(a, j))
            else:
                s.send(u, 1 if a == "x" else 2, region(done), region(done), me.over(a))

        def land(a, done):
            if a == "z":
                for j in (1, 2, 3):
                    s.arrived(u, 2 + j, region(done, z=(me.z + 4 - j) % 4))
            else:
                s.arrived(u, 1 if a == "x" else 2, region(done, **{a: 1 - me.pos[a]}))

        def step(k):
            if 0 < k < 4:
                land(order[k - 1], order[: k - 1])
            if k < 3:
                hop(order[k], order[:k])
            elif k == 3:
                s.send(u, 0, region(order), region(order), me.core())
            else:
                s.arrived(u, 0, region(order, c=1 - me.c))

        return [functools.partial(step, k) for k in range(5)]


class Reduce(Mover):
    def __init__(s, me, G, RC, out, ss, rs, rows, ready, free, slots, count):
        super().__init__(me, ss, rs, rows)
        s.G, s.RC, s.out, s.ready, s.free, s.slots, s.count = G, RC, out, ready, free, slots, count
        s.todo = {}

    def steps(s, u, p, g, c0, nc, order, units):
        me, G, oc = s.me, s.G, 1 - s.me.c
        cols = pl.ds(c0, nc)
        opened, added = s.todo.setdefault(p, ([], []))

        def region(done, **at):
            ix = {a: (at[a] if a in at else me.pos[a] if a in done else ALL) for a in "yzx"}
            return G.at[g, ix["y"], me.c, ix["z"], ix["x"], :, cols]

        def slot(k, z=None):
            i = {
                "xyz": ((ALL, ALL, 0), (0, ALL, 1), (1, z, 1)),
                "yxz": ((0, ALL, ALL), (1, ALL, 0), (1, z, 1)),
                "zyx": ((ALL, z, ALL), (0, me.z, ALL), (1, me.z, 0)),
                "zxy": ((ALL, z, ALL), (ALL, me.z, 0), (0, me.z, 1)),
            }[order][k]
            return G.at[g, i[0], oc, i[1], i[2], :, cols]

        def hop(k):
            a = order[k]
            if a == "z":
                for j in (3, 2, 1):
                    s.send(u, 2 + j, region(order[:k], z=(me.z + j) % 4), slot(k, me.z), me.over(a, j))
            else:
                s.send(u, 1 if a == "x" else 2, region(order[:k], **{a: 1 - me.pos[a]}), slot(k), me.over(a))

        def land(k):
            a = order[k]
            own = region(order[:k], **{a: me.pos[a]})
            if a == "z":
                got = [(2 + j, slot(k, (me.z + 4 - j) % 4)) for j in (1, 2, 3)]
            else:
                got = [(1 if a == "x" else 2, slot(k))]
            total = own[...].astype(jnp.float32)
            for n, ref in got:
                s.arrived(u, n, ref)
                total = total + ref[...].astype(jnp.float32)
            if k == 2:
                s.out[p, :, cols] = total
            else:
                own[...] = total.astype(jnp.bfloat16)

        def core():
            return s.copy(
                u, 0, G.at[g, :, oc, :, :, :, cols], s.RC.at[p % s.slots, :, :, :, :, cols], me.core()
            )

        def first():
            if p >= s.slots and p not in s.todo[-1]:
                pl.semaphore_wait(s.free.at[p], 1)
                s.todo[-1].add(p)
            core().start()

        def open_up():
            core().wait_send()
            opened.append(u)
            if len(opened) == units:
                for i, d in enumerate(me.others()):
                    signal(s.ready.at[p, i], d)

        def second():
            s.arrived(u, 0, s.RC.at[p % s.slots, :, :, :, :, cols])

            def add(i, carry):
                own = G.at[g, i // 4, me.c, i % 4, :, :, cols]
                got = s.RC.at[p % s.slots, i // 4, i % 4, :, :, cols]
                own[...] = (own[...].astype(jnp.float32) + got[...].astype(jnp.float32)).astype(jnp.bfloat16)
                return carry

            lax.fori_loop(0, 8, add, 0)
            if not added:
                for i in range(5):
                    pl.semaphore_wait(s.ready.at[p, i], 1)
            added.append(u)
            hop(0)
            if len(added) == units and p + s.slots < s.count:
                signal(s.free.at[p + s.slots], me.core())

        def later(k):
            land(k)
            if k < 2:
                hop(k + 1)

        s.todo.setdefault(-1, set())
        return [first, open_up, second] + [functools.partial(later, k) for k in range(3)]

WIDTH = 768
DEC = 128
ENC = 512
SEQS = 2
HERE = (4, 8, SEQS, DEC, ENC, WIDTH)
CHUNKS = (2, 2, 4, 2)
TROWS = 16
SLOTS = 4
OWN = WIDTH // 32
PAIRS = WIDTH // 128
HALF = WIDTH // 2
BLK = 256
RD = SEQS * DEC
RE = SEQS * ENC
GELU = math.sqrt(2.0 / math.pi)
PLACE = (9, 8, 10, 11, 4, 7, 5, 6)
GATHERED = (
    (1, 0, 128, "zyx"),
    (1, 128, 512, "zyx"),
    (1, 640, 128, "zyx"),
    (2, 0, 384, "zxy"),
    (2, 384, 256, "yzx"),
    (2, 640, 128, "zyx"),
    (3, 0, 256, "zxy"),
    (3, 256, 384, "zxy"),
    (3, 640, 128, "zyx"),
    (4, 0, 512, "xzy"),
    (4, 512, 128, "zyx"),
    (4, 640, 128, "zxy"),
    (5, 0, 384, "zyx"),
    (5, 384, 256, "xzy"),
    (5, 640, 128, "yxz"),
    (6, 0, 384, "yzx"),
    (6, 384, 256, "zyx"),
    (6, 640, 128, "xzy"),
    (7, 0, 512, "zxy"),
    (7, 512, 128, "xyz"),
    (7, 640, 128, "zyx"),
    (8, 0, 256, "zxy"),
    (8, 256, 256, "xyz"),
    (8, 512, 256, "zyx"),
)
REDUCED = (
    (0, 0, 384, "xyz"),
    (0, 384, 256, "yxz"),
    (0, 640, 128, "zxy"),
    (1, 0, 256, "xyz"),
    (1, 256, 384, "yxz"),
    (1, 640, 128, "zxy"),
    (2, 0, 640, "xyz"),
    (2, 640, 128, "zxy"),
    (3, 0, 640, "yxz"),
    (3, 640, 128, "zyx"),
    (4, 0, 384, "xyz"),
    (4, 384, 256, "yxz"),
    (4, 640, 128, "zyx"),
    (5, 0, 384, "xyz"),
    (5, 384, 256, "yxz"),
    (5, 640, 128, "zyx"),
    (6, 0, 256, "xyz"),
    (6, 256, 384, "yxz"),
    (6, 640, 128, "zyx"),
    (7, 0, 384, "xyz"),
    (7, 384, 384, "yxz"),
)
PLAN = (
    240, 2000, 90, 100, 110, 0, 10, 20, 60, 241, 70, 80, 91, 101, 242, 111,
    1, 102, 243, 112, 244, 2001, 11, 21, 2, 103, 2002, 61, 113, 104, 30, 40,
    50, 114, 71, 3, 81, 4, 12, 62, 22, 41, 82, 72, 150, 160, 170, 63,
    92, 64, 120, 130, 140, 31, 51, 13, 73, 180, 190, 200, 23, 14, 151, 74,
    24, 2003, 42, 83, 171, 131, 161, 2004, 84, 210, 220, 230, 32, 191, 121, 93,
    141, 52, 43, 94, 221, 181, 142, 162, 201, 44, 53, 54, 33, 182, 192, 152,
    34, 2005, 172, 2006, 122, 2007, 222, 163, 2008, 202, 2009, 132, 164, 2010, 2011, 2012,
    211, 2013, 2014, 2015, 231, 2016, 153, 2017, 2018, 2019, 154, 2020, 183, 2021, 143, 2022,
    173, 2023, 123, 144, 184, 2024, 174, 2025, 193, 124, 203, 133, 194, 212, 204, 134,
    2026, 232, 2027, 2028, 2029, 1000, 1010, 1020, 1001, 213, 1011, 1021, 223, 233, 1002, 214,
    1012, 1022, 224, 234, 2030, 2031, 2032, 2033, 1030, 1040, 1050, 2034, 1031, 2035, 2036, 1013,
    1041, 1051, 2037, 1060, 1070, 1080, 1090, 1003, 1032, 2038, 2039, 1061, 1023, 1071, 1042, 1052,
    1014, 1081, 1091, 2040, 1062, 1072, 1004, 1082, 1092, 1033, 1024, 2041, 2042, 2043, 2044, 2045,
    2046, 1043, 1053, 2047, 2048, 1015, 2049, 2050, 1100, 1110, 1120, 2051, 1101, 2052, 1063, 1073,
    1111, 1121, 2053, 1130, 1140, 1150, 1102, 1044, 1005, 1083, 1074, 1131, 1141, 1151, 1054, 1112,
    1122, 1034, 1025, 2054, 1132, 1142, 1152, 1093, 2055, 2056, 1075, 1064, 1045, 1055, 1103, 2057,
    2058, 2059, 2060, 2061, 1113, 1123, 1084, 1035, 1160, 1170, 1180, 2062, 1190, 1200, 1161, 2063,
    1171, 1181, 1143, 2064, 1094, 1191, 1162, 1153, 1201, 1172, 1182, 1133, 1192, 1104, 1202, 1154,
    1114, 1124, 2065, 2066, 1065, 1144, 1095, 2067, 2068, 2069, 1085, 1163, 1173, 1210, 1211, 1134,
    1183, 1212, 1193, 1155, 1125, 1105, 1115, 1203, 1174, 1213, 1145, 1164, 1184, 1135, 1194, 1204,
    1185, 1214, 1175, 1165, 1195, 1205, 1215,
)


def bucket_rows():
    table = bucket_table(DEC, NB)[:, 0]
    far = table[(-np.arange(DEC)) % DEC]
    rows = np.full((8, TROWS), -1)
    rows[:, 4:8] = np.arange(NB).reshape(8, 4)
    return jnp.asarray((rows.reshape(-1, 1) == far[None, :]).astype(np.float32), jnp.bfloat16)


def sem_rows(gathered, reduced):
    deep = [max(gathered.count(p), reduced.count(p)) for p in range(NP)]

    def rows(pieces):
        return [sum(deep[:p]) + pieces[:i].count(p) for i, p in enumerate(pieces)] + [sum(deep)]

    return rows(gathered), rows(reduced), sum(deep)


def loop(n, body):
    def step(i, carry):
        body(i)
        return carry

    lax.fori_loop(0, n, step, 0)


def tile(i, n):
    return pl.ds(pl.multiple_of(i * n, n), n)


def f32(v):
    return v.astype(jnp.float32)


def layer_kernel(
    dlen, elen, dec_hbm, enc_hbm, cot_hbm, small, bmap,
    sq, sk, sv, so, cq, ck, cv, co, fi, fo,
    out_hbm, gdec_hbm, genc_hbm, gw, gt,
    BUF, T, GT, RCT, RC,
    X, C, E, K, V, A1, Q1, K1, V1, O1, A2, Q2, O2, A3, GO, HID, GP,
    Y1, Y2, F2, GY, PS, PC, BIAS, NRM, DM,
    ss, rs, ready, free, tready, tfree, lsem,
):
    me = Place()
    greet(me)
    loads = [
        pltpu.make_async_copy(a, b, lsem.at[i])
        for i, (a, b) in enumerate(((dec_hbm, X), (cot_hbm, C), (enc_hbm, E)))
    ]
    for cp in loads:
        cp.start()

    def pack(p, top, bottom):
        both = jnp.concatenate([f32(top), f32(bottom)], axis=0)
        BUF[p + 1, me.y, me.c, me.z, me.x] = low(both)

    pack(0, sq[...], sk[...])
    pack(1, sv[...], so[...])
    pack(2, ck[...], cv[...])
    pack(3, cq[...], co[...])
    BUF[5, me.y, me.c, me.z, me.x] = fo[0:48]
    BUF[6, me.y, me.c, me.z, me.x] = fo[48:96]
    for h in range(2):
        pack(6 + h, fi[:, 1536 * h : 1536 * h + 768], fi[:, 1536 * h + 768 : 1536 * h + 1536])
    T[0, me.y, me.c, me.z, me.x] = small[...]
    all_here()

    def first_lanes(shape):
        return lax.broadcasted_iota(jnp.int32, shape, 1) < 64

    def two(v):
        keep = first_lanes(v.shape)
        w = f32(v)
        return low(jnp.concatenate([jnp.where(keep, w, 0.0), jnp.where(keep, 0.0, w)], axis=0))

    def one(v):
        return jnp.where(first_lanes((DEC, 128)), v[:DEC], v[DEC:])

    def unpack(src, dst):
        def body(i):
            for z in range(4):
                w = f32(BUF[src, i // 2, i % 2, z])
                for k in range(2):
                    rows = slice(OWN * k, OWN * k + OWN)
                    both = low(jnp.concatenate([w[0, rows], w[1, rows]], axis=0))
                    BUF[dst, k, i // 2, (i % 2) * 2 + z // 2, z % 2] = both

        loop(4, body)

    def whole(b, k):
        return BUF[b, k].reshape(WIDTH, WIDTH)

    def rows_of(i):
        return slice(i * RD, i * RD + RD) if isinstance(i, int) else tile(i, RD)

    def project(a, b, k, dst, i=0):
        r = rows_of(i)
        dst[r, :] = low(dot_nn(a[r, :], whole(b, k)))

    def project_add(a, b, k, base, dst):
        dst[...] = f32(base[...]) + dot_nn(a[...], whole(b, k))

    def norm(v, gain, dst):
        def body(i):
            r = tile(i, 128)
            x = f32(v[r, :])
            s = lax.rsqrt(jnp.mean(x * x, axis=-1, keepdims=True) + EPSILON)
            dst[r, :] = low(x * s * NRM[gain : gain + 1, :])

        loop(RD // 128, body)

    def norm_back(v, gain, G, base, dst):
        def body(i, total):
            r = tile(i, 64)
            x = f32(v[r, :])
            s = lax.rsqrt(jnp.mean(x * x, axis=-1, keepdims=True) + EPSILON)
            n = x * s
            w = G[r, :]
            u = w * NRM[gain : gain + 1, :]
            dst[r, :] = f32(base[r, :]) + s * (u - n * jnp.mean(u * n, axis=-1, keepdims=True))
            return total + jnp.sum((w * n).reshape(8, 8, WIDTH), axis=0)

        total = lax.fori_loop(0, RD // 64, body, jnp.zeros((8, WIDTH), jnp.float32))
        return jnp.sum(total, axis=0, keepdims=True)

    def softmax(s):
        e = jnp.exp(s - jnp.max(s, axis=-1, keepdims=True))
        return e * (1.0 / jnp.sum(e, axis=-1, keepdims=True))

    def attend(q, k, v, o, probs, slots, mask, lo, hi):
        def body(j):
            i = j + lo
            lanes = tile(i, 128)
            for at in range(SEQS):
                r, kr = slice(at * DEC, at * DEC + DEC), slice(at * slots, at * slots + slots)
                s = dot_nt(two(q[r, lanes]), k[kr, lanes])
                p = low(softmax(mask(s, at, i)))
                probs[i, at] = p
                o[r, lanes] = low(one(dot_nn(p, v[kr, lanes])))

        loop(hi - lo, body)

    def attend_back(q, k, v, go, probs, slots, lo, hi, extra):
        def body(j):
            i = j + lo
            lanes = tile(i, 128)
            for at in range(SEQS):
                r, kr = slice(at * DEC, at * DEC + DEC), slice(at * slots, at * slots + slots)
                q2, g2, p = two(q[r, lanes]), two(go[r, lanes]), probs[i, at]
                d = dot_nt(g2, v[kr, lanes])
                pf = f32(p)
                gs = low(pf * (d - jnp.sum(pf * d, axis=-1, keepdims=True)))
                v[kr, lanes] = low(dot_tn(p, g2))
                q[r, lanes] = low(one(dot_nn(gs, k[kr, lanes])))
                k[kr, lanes] = low(dot_tn(gs, q2))
                extra(gs, i)

        loop(hi - lo, body)

    def back_project(pairs, dst, cast, i=0):
        r = rows_of(i)
        v = None
        for a, b, k in pairs:
            d = dot_nt(a[r, :], whole(b, k))
            v = d if v is None else v + d
        dst[r, :] = cast(v)

    def grad_pair(aa, ga, ab, gb, place, oa=0, ob=0, tiles=(0, 1, 2)):
        for n in tiles:
            va = dot_tn(aa[...], ga[:, (n + oa) * BLK : (n + oa + 1) * BLK]).reshape(32, OWN, BLK)
            vb = dot_tn(ab[...], gb[:, (n + ob) * BLK : (n + ob + 1) * BLK]).reshape(32, OWN, BLK)
            both = low(jnp.concatenate([va, vb], axis=1))
            BUF[place, :, :, :, :, :, n * BLK : (n + 1) * BLK] = both.reshape(2, 2, 4, 2, ROWS, BLK)

    owner = jnp.floor((f32(lax.broadcasted_iota(jnp.int32, (1, WIDTH), 1)) + 0.5) * (1.0 / OWN))

    def spread():
        place = f32(lax.broadcasted_iota(jnp.int32, (128, WIDTH), 1)) - OWN * owner
        return low(jnp.where(place == f32(lax.broadcasted_iota(jnp.int32, (128, WIDTH), 0)), 1.0, 0.0))

    row = f32(lax.broadcasted_iota(jnp.int32, (32 * TROWS, 1), 0)) - TROWS * owner
    def self_mask(s, at, pair):
        k = lax.broadcasted_iota(jnp.int32, s.shape, 1)
        q = lax.broadcasted_iota(jnp.int32, s.shape, 0) % DEC
        return jnp.where((k <= q) & (k < dlen[at]), s + BIAS[pair], MASKED)

    def cross_mask(s, at, pair):
        return jnp.where(lax.broadcasted_iota(jnp.int32, s.shape, 1) < elen[at], s, MASKED)

    def out_rows(j):
        return jnp.concatenate([BUF[b, j // 2, j % 2] for b in (5, 6)], axis=2).reshape(WIDTH, WIDTH)

    def feed(j, b):
        k = j % 2
        pre = dot_nn(A3[...], whole(b, k))
        gh = dot_nt(C[...], out_rows(j))
        th = jnp.tanh(GELU * (pre + 0.044715 * (pre * pre * pre)))
        HID[:, j * WIDTH : (j + 1) * WIDTH] = low(0.5 * pre * (1.0 + th))
        slope = 0.5 * (1.0 + th) + 0.5 * pre * (1.0 - th * th) * (GELU * (1.0 + 0.134145 * (pre * pre)))
        GP[:, j * WIDTH : (j + 1) * WIDTH] = low(slope * gh)

    def feed_grads(j):
        for n in range(3):
            w = low(dot_tn(HID[:, j * WIDTH : (j + 1) * WIDTH], C[:, n * BLK : (n + 1) * BLK]))
            w = w.reshape(4, 2, 2 * ROWS, BLK)
            for e in range(2):
                part = w[:, :, ROWS * e : ROWS * e + ROWS]
                BUF[PLACE[2 + e], j // 2, j % 2, :, :, :, n * BLK : (n + 1) * BLK] = part

    def mix_back(j, b):
        d = dot_nt(GP[:, j * WIDTH : (j + 1) * WIDTH], whole(b, j % 2))
        F2[...] = d if j == 0 else F2[...] + d

    def mix():
        v = Y2[...]
        for j in range(4):
            v = v + dot_nn(HID[:, j * WIDTH : (j + 1) * WIDTH], out_rows(j))
        A3[...] = low(v)


    def cast_rows(src, dst):
        def body(i):
            q = tile(i, 64)
            dst[q, :] = low(src[q, :])

        loop(RD // 64, body)

    def nothing(gs, pair):
        pass

    def sum_bias(gs, pair):
        BIAS[pair] += f32(gs)

    def done(*pieces):
        g.drain([u for u, unit in enumerate(GATHERED) if unit[0] - 1 in pieces])

    stores, gains = [], {}

    def store(src, dst, i):
        stores.append(pltpu.make_async_copy(src, dst, lsem.at[i]))
        stores[-1].start()

    def init():
        for cp in loads:
            cp.wait()
        place = lax.broadcasted_iota(jnp.int32, (DEC, WIDTH), 0)
        for s in range(SEQS):
            r = slice(DEC * s, DEC * s + DEC)
            C[r, :] = low(jnp.where(place < dlen[s], f32(C[r, :]), 0.0))

    def tables():
        h.drain()
        table = T[0].reshape(32 * TROWS, 128)
        wide = dot_nn(table, spread())
        NRM[...] = jnp.concatenate(
            [jnp.sum(jnp.where(row == float(n), wide, 0.0), axis=0, keepdims=True) for n in range(3)]
            + [jnp.zeros((5, WIDTH), jnp.float32)],
            axis=0,
        )
        DM[...] = dot_tn(T[0, 0, 0].reshape(8 * TROWS, 128), bmap[...])
        for j in range(2 * PAIRS):
            v = jnp.broadcast_to(DM[j : j + 1, :], (DEC, DEC))
            BIAS[j // 2, DEC * (j % 2) : DEC * (j % 2) + DEC, :] = pltpu.roll(v, 0, 1, stride=1, stride_axis=0)

    def unpack_to(src, dst, *pieces):
        done(*pieces)
        unpack(src, dst)

    def self_out():
        project_add(O1, 1, 1, X, Y1)
        norm(Y1, 1, A2)

    def cross_out():
        project_add(O2, 3, 1, Y1, Y2)
        norm(Y2, 2, A3)

    def in_grads(h):
        if h:
            done(4, 5, 7)
        grad_pair(A3, GP, A3, GP, PLACE[h], 6 * h, 6 * h + 3)

    def finish():
        mix()
        store(A3, out_hbm, 0)

    def norm_back_ffn():
        gains[2] = norm_back(Y2, 2, F2, C, GY)
        cast_rows(GY, C)

    def norm_back_cross():
        gains[1] = norm_back(Y1, 1, F2, GY, GY)
        cast_rows(GY, C)
        BIAS[...] = jnp.zeros_like(BIAS)

    def norm_back_self():
        gains[0] = norm_back(X, 0, F2, GY, GY)
        cast_rows(GY, GO)
        store(GO, gdec_hbm, 1)

    def enc_grad(i):
        loop(2, lambda n: back_project([(K, 2, 0), (V, 2, 1)], E, low, n + 2 * i))
        if i:
            store(E, genc_hbm, 2)

    def small_grads():
        DM[...] = jnp.zeros_like(DM)
        flip = lax.broadcasted_iota(jnp.int32, (DEC, DEC), 0) + lax.broadcasted_iota(jnp.int32, (DEC, DEC), 1)
        flip = low(jnp.where(flip == DEC - 1, 1.0, 0.0))
        for j in range(2 * PAIRS):
            v = BIAS[j // 2, DEC * (j % 2) : DEC * (j % 2) + DEC, :]
            hi = low(v)
            v = dot_nn(flip, hi) + dot_nn(flip, low(v - f32(hi)))
            v = pltpu.roll(v, 0, 1, stride=1, stride_axis=0)
            DM[j : j + 1, :] = jnp.sum(v, axis=0, keepdims=True)
        DM[...] = pltpu.roll(DM[...], 1, 1)
        hi = low(DM[...])
        rel = dot_nt(bmap[...], hi) + dot_nt(bmap[...], low(DM[...] - f32(hi)))
        spots = sum(jnp.where(row == float(n), gains[n], 0.0) for n in range(3))
        spots = dot_nt(low(spots), spread()).reshape(4, 128, 128)
        for d in range(4):
            GT[0, d // 2, d % 2] = low(spots[d] + rel).reshape(4, 2, TROWS, 128)

    def many(n, fn, each=1):
        return [functools.partial(fn, i // each) if i % each == 0 else int for i in range(n)]

    work = [
        init,
        tables,
        lambda: norm(X, 0, A1),
        lambda: (unpack(1, 0), project(A1, 0, 0, Q1)),
        lambda: project(A1, 0, 1, K1),
        lambda: (unpack_to(2, 1, 0), project(A1, 1, 0, V1)),
        *many(3, lambda i: attend(Q1, K1, V1, O1, PS, DEC, self_mask, 0, 6), 3),
        self_out,
        *many(4, lambda i: (None if i else unpack_to(3, 2, 1), loop(2, lambda n: project(E, 2, 0, K, n + 2 * i))), 2),
        *many(4, lambda i: loop(2, lambda n: project(E, 2, 1, V, n + 2 * i)), 2),
        lambda: (unpack_to(4, 3, 2), project(A2, 3, 0, Q2)),
        *many(6, lambda i: attend(Q2, K, V, O2, PC, ENC, cross_mask, 3 * i, 3 * i + 3), 3),
        cross_out,
        lambda: unpack_to(7, 4, 3),
        *many(2, lambda i: feed(i, 4)),
        lambda: in_grads(0),
        lambda: unpack_to(8, 7, 6),
        *many(2, lambda i: feed(2 + i, 7)),
        lambda: in_grads(1),
        *many(4, feed_grads),
        *many(4, lambda j: mix_back(j, 4 if j < 2 else 7)),
        norm_back_ffn,
        lambda: back_project([(C, 3, 1)], GO, low),
        *many(6, lambda i: attend_back(Q2, K, V, GO, PC, ENC, 3 * i, 3 * i + 3, nothing), 3),
        lambda: grad_pair(A2, Q2, O2, C, PLACE[4]),
        *many(3, lambda n: grad_pair(E, K, E, V, PLACE[5], tiles=(n,))),
        finish,
        lambda: back_project([(Q2, 3, 0)], F2, f32),
        norm_back_cross,
        lambda: back_project([(C, 1, 1)], GO, low),
        *many(3, lambda i: attend_back(Q1, K1, V1, GO, PS, DEC, 0, 6, sum_bias), 3),
        lambda: grad_pair(A1, V1, O1, C, PLACE[6]),
        lambda: grad_pair(A1, Q1, A1, K1, PLACE[7]),
        *many(4, enc_grad, 2),
        lambda: back_project([(Q1, 0, 0), (K1, 0, 1), (V1, 1, 0)], F2, f32),
        norm_back_self,
        small_grads,
    ]
    rows_g, rows_r, last = sem_rows([unit[0] - 1 for unit in GATHERED], [unit[0] for unit in REDUCED])
    g = Gather(me, BUF, ss, rs, rows_g)
    h = Gather(me, T, ss, rs, rows_g)
    r = Reduce(me, BUF, RC, gw, ss, rs, rows_r, ready, free, SLOTS, NP)
    rt = Reduce(me, GT, RCT, gt, ss, rs, rows_r, tready, tfree, 1, 1)
    na, nr = len(GATHERED), len(REDUCED)
    gathers = [g.steps(u, *unit) for u, unit in enumerate(GATHERED)] + [h.steps(na, 0, 0, 128, "zyx")]
    parts = [sum(unit[0] == p for unit in REDUCED) for p in range(NP)]
    reduces = [r.steps(u, p, PLACE[p], *cut, parts[p]) for u, (p, *cut) in enumerate(REDUCED)]
    reduces.append(rt.steps(nr, 0, 0, 0, 128, "xyz", 1))
    for code in PLAN:
        if code >= 2000:
            work[code - 2000]()
        else:
            (reduces if code >= 1000 else gathers)[code % 1000 // 10][code % 10]()
    g.drain()
    h.drain()
    r.drain()
    rt.drain()
    for cp in stores:
        cp.wait()


def layer_here(shards, dec_in, enc_out, dec_len, enc_len, cotangent):
    ns, sq, sk, sv, so, rel, nc, cq, ck, cv, co, nf, fi, fo = shards
    gains = jnp.pad(jnp.stack([ns, nc, nf]), ((0, 1), (0, 128 - OWN)))
    small = jnp.concatenate([gains, jnp.pad(rel, ((0, 8), (0, 128 - rel.shape[1])))], axis=0)
    b16, w32 = jnp.bfloat16, jnp.float32

    def vm(shape, dtype=b16):
        return pltpu.VMEM(shape, dtype)

    dec, enc = (RD, WIDTH), (RE, WIDTH)
    scratch = [
        vm((12, *CHUNKS, ROWS, COLS)),
        vm((1, *CHUNKS, TROWS, 128)),
        vm((1, *CHUNKS, TROWS, 128)),
        vm((1, 2, 4, 2, TROWS, 128)),
        vm((SLOTS, 2, 4, 2, ROWS, COLS)),
        vm(dec), vm(dec), vm(enc), vm(enc), vm(enc),
        *[vm(dec)] * 10,
        *[vm((RD, 4 * WIDTH))] * 2,
        *[vm(dec, w32)] * 4,
        vm((PAIRS, SEQS, 2 * DEC, DEC)),
        vm((PAIRS, SEQS, 2 * DEC, ENC)),
        vm((PAIRS, 2 * DEC, DEC), w32),
        vm((8, WIDTH), w32),
        vm((128, 128), w32),
        *[pltpu.SemaphoreType.DMA((sem_rows([u[0] - 1 for u in GATHERED], [u[0] for u in REDUCED])[2] + 1, 6))] * 2,
        pltpu.SemaphoreType.REGULAR((NP, 5)),
        pltpu.SemaphoreType.REGULAR((NP,)),
        pltpu.SemaphoreType.REGULAR((1, 5)),
        pltpu.SemaphoreType.REGULAR((1,)),
        pltpu.SemaphoreType.DMA((3,)),
    ]
    here, away = pl.BlockSpec(memory_space=pltpu.VMEM), pl.BlockSpec(memory_space=pl.ANY)
    scalars = pl.BlockSpec(memory_space=pltpu.SMEM)
    out, g_dec, g_enc, gw, gt = pl.pallas_call(
        layer_kernel,
        out_shape=(
            jax.ShapeDtypeStruct(dec, b16),
            jax.ShapeDtypeStruct(dec, b16),
            jax.ShapeDtypeStruct(enc, b16),
            jax.ShapeDtypeStruct((NP, ROWS, COLS), w32),
            jax.ShapeDtypeStruct((1, TROWS, 128), w32),
        ),
        in_specs=[scalars] * 2 + [away] * 3 + [here] * 12,
        out_specs=[away] * 3 + [here] * 2,
        scratch_shapes=scratch,
        compiler_params=pltpu.CompilerParams(
            collective_id=0, has_side_effects=True, vmem_limit_bytes=60 * 2**20
        ),
    )(
        dec_len.reshape(-1), enc_len.reshape(-1),
        dec_in.reshape(dec), enc_out.reshape(enc), cotangent.reshape(dec),
        small, bucket_rows(), sq, sk, sv, so, cq, ck, cv, co, fi, fo,
    )
    return deliver(out, g_dec, g_enc, gw, gt, rel.shape)


def deliver_kernel(out, gdec, genc, gw, gt, o0, o1, o2, *outs):
    grads, (w_fi, w_fo, n1, n2, n3, rel, sem) = outs[:8], outs[8:]
    moves = [(out, o0), (gdec, o1), (genc, o2)]
    at = ((7, 0), (7, 1), (6, 0), (6, 1), (4, 0), (5, 0), (5, 1), (4, 1))
    moves += [(gw.at[p, pl.ds(OWN * h, OWN)], o) for (p, h), o in zip(at, grads)]
    for j in range(4):
        moves.append((gw.at[j // 2, pl.ds(OWN * (j % 2), OWN)], w_fi.at[:, pl.ds(WIDTH * j, WIDTH)]))
    moves += [(gw.at[2 + e], w_fo.at[pl.ds(ROWS * e, ROWS)]) for e in range(2)]
    copies = [pltpu.make_async_copy(a, b, sem.at[i]) for i, (a, b) in enumerate(moves)]
    for cp in copies:
        cp.start()
    for n, o in enumerate((n1, n2, n3)):
        o[...] = gt[0, n : n + 1, :OWN]
    rel[...] = gt[0, 4 : 4 + rel.shape[0], : rel.shape[1]]
    for cp in copies:
        cp.wait()


def deliver(out, g_dec, g_enc, gw, gt, rel):
    here, away = pl.BlockSpec(memory_space=pltpu.VMEM), pl.BlockSpec(memory_space=pl.ANY)
    w32 = [(OWN, WIDTH)] * 8 + [(OWN, 4 * WIDTH), (2 * ROWS, WIDTH)] + [(1, OWN)] * 3 + [rel]
    got = pl.pallas_call(
        deliver_kernel,
        out_shape=[jax.ShapeDtypeStruct(v.shape, v.dtype) for v in (out, g_dec, g_enc)]
        + [jax.ShapeDtypeStruct(v, jnp.float32) for v in w32],
        in_specs=[away] * 4 + [here],
        out_specs=[here] * 17,
        scratch_shapes=[pltpu.SemaphoreType.DMA((17,))],
    )(out, g_dec, g_enc, gw, gt)
    sq, sk, sv, so, cq, ck, cv, co, w_fi, w_fo, n1, n2, n3, w_rel = got[3:]
    n1, n2, n3 = (v.reshape(-1) for v in (n1, n2, n3))
    return got[0], got[1], got[2], (n1, sq, sk, sv, so, w_rel, n2, cq, ck, cv, co, n3, w_fi, w_fo)


EPSILON = 1e-06
MASKED = -1000000000.0
NB = 32
AT = ("dp", "fsdp")


def bucket_table(dec_slots, bucket_count):
    near = bucket_count // 2
    places = np.arange(dec_slots, dtype=np.int32)
    distance = np.maximum(places[:, None] - places[None, :], 0).astype(np.int32)
    edges = np.array(
        [math.ceil(near * (128 / near) ** (level / near) - 1e-09) for level in range(1, near)],
        dtype=np.int32,
    )
    far = near + np.sum(
        (distance[:, :, None] >= edges[None, None, :]).astype(np.int32), axis=-1, dtype=np.int32
    )
    return np.where(distance < near, distance, far).astype(np.int32)


def rms_norm(values, gain):
    return values * lax.rsqrt(jnp.mean(values * values, axis=-1, keepdims=True) + EPSILON) * gain


def smooth(values):
    return jax.nn.gelu(values, approximate=True)


def dot_nn(a, b):
    return jnp.dot(a, b, preferred_element_type=jnp.float32)


def dot_nt(a, b):
    return lax.dot_general(a, b, (((1,), (1,)), ((), ())), preferred_element_type=jnp.float32)


def dot_tn(a, b):
    return lax.dot_general(a, b, (((0,), (0,)), ((), ())), preferred_element_type=jnp.float32)


def low(v):
    return v.astype(jnp.bfloat16)


def layer_plain(weights, dec_rows, enc_rows, dec_len, enc_len, cot_rows):
    ns, sq, sk, sv, so, rel, nc, cq, ck, cv, co, nf, fi, fo = weights
    seqs, dec_slots, width = dec_rows.shape
    enc_slots = enc_rows.shape[1]
    heads = rel.shape[1]
    size = width // heads
    ns, nc, nf = (v.astype(jnp.float32) for v in (ns, nc, nf))
    places = jnp.arange(dec_slots, dtype=jnp.int32)
    causal = places[None, :] <= places[:, None]
    self_mask = causal[None, None] & (places[None, None, None, :] < dec_len[:, None, None, None])
    enc_places = jnp.arange(enc_slots, dtype=jnp.int32)
    cross_mask = enc_places[None, None, None, :] < enc_len[:, None, None, None]
    row_mask = (places[None, :] < dec_len[:, None]).astype(jnp.float32)
    table = bucket_table(dec_slots, NB).reshape(-1)
    onehot = jnp.asarray((table[:, None] == np.arange(NB)[None, :]).astype(np.float32), jnp.bfloat16)
    bias = lax.dot_general(rel, onehot, (((0,), (1,)), ((), ())), preferred_element_type=jnp.float32)
    bias = bias.reshape(heads, dec_slots, dec_slots)[None]

    def split(t):
        return t.reshape(seqs, -1, heads, size).transpose(0, 2, 1, 3)

    def join(t):
        return t.transpose(0, 2, 1, 3).reshape(-1, width)

    def many(a, b, ca, cb):
        return lax.dot_general(
            a, b, (((ca,), (cb,)), ((0, 1), (0, 1))), preferred_element_type=jnp.float32
        )

    def attend(q, k, v, add, mask):
        s = jnp.where(mask, many(q, k, 3, 3) + add, MASKED)
        top = jnp.max(s, axis=-1, keepdims=True)
        e = jnp.exp(s - top)
        p = e / jnp.sum(e, axis=-1, keepdims=True)
        return p, low(many(low(p), v, 3, 2))

    def back(q, k, v, p, g):
        gv = low(many(low(p), g, 2, 2))
        d = many(g, v, 3, 3)
        gs = low(p * (d - jnp.sum(p * d, axis=-1, keepdims=True)))
        return low(many(gs, k, 3, 2)), low(many(gs, q, 2, 2)), gv, gs

    x = dec_rows.reshape(-1, width).astype(jnp.float32)
    enc = enc_rows.reshape(-1, width)
    a1 = low(rms_norm(x, ns))
    q1, k1, v1 = (split(low(dot_nn(a1, w))) for w in (sq, sk, sv))
    p1, o1 = attend(q1, k1, v1, bias, self_mask)
    o1 = join(o1)
    y1 = x + dot_nn(o1, so)
    a2 = low(rms_norm(y1, nc))
    q2 = split(low(dot_nn(a2, cq)))
    k2, v2 = (split(low(dot_nn(enc, w))) for w in (ck, cv))
    p2, o2 = attend(q2, k2, v2, 0.0, cross_mask)
    o2 = join(o2)
    y2 = y1 + dot_nn(o2, co)
    a3 = low(rms_norm(y2, nf))
    pre = dot_nn(a3, fi)
    hidden = low(smooth(pre))
    out = y2 + dot_nn(hidden, fo)
    g = (cot_rows.astype(jnp.float32) * row_mask[:, :, None]).reshape(-1, width)
    gf = low(g)
    w_fo = dot_tn(hidden, gf)
    gp = low(jax.vjp(smooth, pre)[1](dot_nt(gf, fo))[0])
    w_fi = dot_tn(a3, gp)
    part, w_nf = jax.vjp(rms_norm, y2, nf)[1](dot_nt(gp, fi))
    gy = g + part
    gc = low(gy)
    w_co = dot_tn(o2, gc)
    gq, gk, gv, _ = back(q2, k2, v2, p2, split(low(dot_nt(gc, co))))
    gq, gk, gv = join(gq), join(gk), join(gv)
    w_cq, w_ck, w_cv = dot_tn(a2, gq), dot_tn(enc, gk), dot_tn(enc, gv)
    g_enc = dot_nt(gk, ck) + dot_nt(gv, cv)
    part, w_nc = jax.vjp(rms_norm, y1, nc)[1](dot_nt(gq, cq))
    gy = gy + part
    ga = low(gy)
    w_so = dot_tn(o1, ga)
    gq, gk, gv, gs = back(q1, k1, v1, p1, split(low(dot_nt(ga, so))))
    w_rel = lax.dot_general(
        onehot, gs.reshape(seqs, heads, -1), (((0,), (2,)), ((), ())), preferred_element_type=jnp.float32
    ).sum(axis=1)
    gq, gk, gv = join(gq), join(gk), join(gv)
    w_sq, w_sk, w_sv = dot_tn(a1, gq), dot_tn(a1, gk), dot_tn(a1, gv)
    part, w_ns = jax.vjp(rms_norm, x, ns)[1](dot_nt(gq, sq) + dot_nt(gk, sk) + dot_nt(gv, sv))
    grads = (w_ns, w_sq, w_sk, w_sv, w_so, w_rel, w_nc, w_cq, w_ck, w_cv, w_co, w_nf, w_fi, w_fo)
    return low(out), low(gy + part), low(g_enc), grads


REL = 5


def on_device(dec_in, enc_out, dec_len, enc_len, cotangent, *shards):
    micro, per, dec_slots, width = dec_in.shape
    seqs, enc_slots = micro * per, enc_out.shape[2]
    if (lax.axis_size("dp"), lax.axis_size("fsdp"), seqs, dec_slots, enc_slots, width) == HERE:
        out, g_dec, g_enc, grads = layer_here(shards, dec_in, enc_out, dec_len, enc_len, cotangent)
    else:
        whole = [lax.all_gather(w, AT[1] if i == REL else AT, axis=0, tiled=True) for i, w in enumerate(shards)]
        out, g_dec, g_enc, grads = layer_plain(
            whole,
            dec_in.reshape(seqs, dec_slots, width),
            enc_out.reshape(seqs, enc_slots, width),
            dec_len.reshape(-1),
            enc_len.reshape(-1),
            cotangent.reshape(seqs, dec_slots, width),
        )
        grads = [
            lax.psum_scatter(
                lax.psum(w, AT[0]) if i == REL else w,
                AT[1] if i == REL else AT,
                scatter_dimension=0,
                tiled=True,
            )
            for i, w in enumerate(grads)
        ]
    return (out.reshape(dec_in.shape), g_dec.reshape(dec_in.shape), g_enc.reshape(enc_out.shape), *grads)


def solution(mesh):
    rows, seq = P(AT, None), P(None, AT, None, None)
    gain, lens, rel = P(AT), P(None, AT), P(AT[1], None)
    placed = (gain, rows, rows, rows, rows, rel, gain, rows, rows, rows, rows, gain, rows, rows)
    return jax.shard_map(
        on_device,
        mesh=mesh,
        in_specs=(seq, seq, lens, lens, seq, *placed),
        out_specs=(seq, seq, seq, *placed),
        check_vma=False,
    )
```

```python
import functools
import math

import jax
import jax.numpy as jnp
import numpy as np
from jax import lax
from jax.experimental import pallas as pl
from jax.experimental.pallas import tpu as pltpu
from jax.sharding import PartitionSpec as P

MESH = pl.DeviceIdType.MESH
NP = 8
ROWS = 48
COLS = 768
ALL = slice(None)


class Place:
    def __init__(s):
        dp, f = lax.axis_index("dp"), lax.axis_index("fsdp")
        s.c, s.y, s.x, s.z = dp % 2, dp // 2, f % 2, f // 2
        s.pos = {"x": s.x, "y": s.y, "z": s.z}

    def dev(s, c=None, y=None, z=None, x=None):
        c = s.c if c is None else c
        y = s.y if y is None else y
        z = s.z if z is None else z
        x = s.x if x is None else x
        return (y * 2 + c, z * 2 + x)

    def core(s):
        return s.dev(c=1 - s.c)

    def over(s, axis, j=1):
        if axis == "x":
            return s.dev(x=1 - s.x)
        if axis == "y":
            return s.dev(y=1 - s.y)
        return s.dev(z=(s.z + j) % 4)

    def others(s):
        return [s.over("x"), s.over("y")] + [s.over("z", j) for j in (1, 2, 3)]


def signal(sem, dev):
    pl.semaphore_signal(sem, inc=1, device_id=dev, device_id_type=MESH)


def greet(me):
    for d in me.others() + [me.core()]:
        signal(pltpu.get_barrier_semaphore(), d)


def all_here():
    pl.semaphore_wait(pltpu.get_barrier_semaphore(), 6)


class Mover:
    def __init__(s, me, ss, rs, rows):
        s.me, s.ss, s.rs, s.rows, s.sent = me, ss, rs, rows, []

    def copy(s, u, slot, src, dst, dev):
        return pltpu.make_async_remote_copy(
            src_ref=src, dst_ref=dst, send_sem=s.ss.at[s.rows[u], slot], recv_sem=s.rs.at[s.rows[u], slot],
            device_id=dev, device_id_type=MESH,
        )

    def send(s, *what):
        cp = s.copy(*what)
        cp.start()
        s.sent.append((what[0], cp))

    def arrived(s, u, slot, dst):
        s.copy(u, slot, dst, dst, s.me.core()).wait_recv()

    def drain(s, us=None):
        for u, cp in s.sent:
            if us is None or u in us:
                cp.wait_send()
        s.sent = [] if us is None else [e for e in s.sent if e[0] not in us]


class Gather(Mover):
    def __init__(s, me, A, ss, rs, rows):
        super().__init__(me, ss, rs, rows)
        s.A = A

    def steps(s, u, b, c0, nc, order):
        me = s.me

        def region(done, c=me.c, **at):
            ix = {a: (at[a] if a in at else ALL if a in done else me.pos[a]) for a in "yzx"}
            return s.A.at[b, ix["y"], c, ix["z"], ix["x"], :, pl.ds(c0, nc)]

        def hop(a, done):
            if a == "z":
                for j in (3, 2, 1):
                    s.send(u, 2 + j, region(done), region(done), me.over(a, j))
            else:
                s.send(u, 1 if a == "x" else 2, region(done), region(done), me.over(a))

        def land(a, done):
            if a == "z":
                for j in (1, 2, 3):
                    s.arrived(u, 2 + j, region(done, z=(me.z + 4 - j) % 4))
            else:
                s.arrived(u, 1 if a == "x" else 2, region(done, **{a: 1 - me.pos[a]}))

        def step(k):
            if 0 < k < 4:
                land(order[k - 1], order[: k - 1])
            if k < 3:
                hop(order[k], order[:k])
            elif k == 3:
                s.send(u, 0, region(order), region(order), me.core())
            else:
                s.arrived(u, 0, region(order, c=1 - me.c))

        return [functools.partial(step, k) for k in range(5)]


class Reduce(Mover):
    def __init__(s, me, G, RC, out, ss, rs, rows, ready, free, slots, count):
        super().__init__(me, ss, rs, rows)
        s.G, s.RC, s.out, s.ready, s.free, s.slots, s.count = G, RC, out, ready, free, slots, count
        s.todo = {}

    def steps(s, u, p, g, c0, nc, order, units):
        me, G, oc = s.me, s.G, 1 - s.me.c
        cols = pl.ds(c0, nc)
        opened, added = s.todo.setdefault(p, ([], []))

        def region(done, **at):
            ix = {a: (at[a] if a in at else me.pos[a] if a in done else ALL) for a in "yzx"}
            return G.at[g, ix["y"], me.c, ix["z"], ix["x"], :, cols]

        def slot(k, z=None):
            i = {
                "xyz": ((ALL, ALL, 0), (0, ALL, 1), (1, z, 1)),
                "yxz": ((0, ALL, ALL), (1, ALL, 0), (1, z, 1)),
                "zyx": ((ALL, z, ALL), (0, me.z, ALL), (1, me.z, 0)),
                "zxy": ((ALL, z, ALL), (ALL, me.z, 0), (0, me.z, 1)),
            }[order][k]
            return G.at[g, i[0], oc, i[1], i[2], :, cols]

        def hop(k):
            a = order[k]
            if a == "z":
                for j in (3, 2, 1):
                    s.send(u, 2 + j, region(order[:k], z=(me.z + j) % 4), slot(k, me.z), me.over(a, j))
            else:
                s.send(u, 1 if a == "x" else 2, region(order[:k], **{a: 1 - me.pos[a]}), slot(k), me.over(a))

        def land(k):
            a = order[k]
            own = region(order[:k], **{a: me.pos[a]})
            if a == "z":
                got = [(2 + j, slot(k, (me.z + 4 - j) % 4)) for j in (1, 2, 3)]
            else:
                got = [(1 if a == "x" else 2, slot(k))]
            total = own[...].astype(jnp.float32)
            for n, ref in got:
                s.arrived(u, n, ref)
                total = total + ref[...].astype(jnp.float32)
            if k == 2:
                s.out[p, :, cols] = total
            else:
                own[...] = total.astype(jnp.bfloat16)

        def core():
            return s.copy(
                u, 0, G.at[g, :, oc, :, :, :, cols], s.RC.at[p % s.slots, :, :, :, :, cols], me.core()
            )

        def first():
            if p >= s.slots and p not in s.todo[-1]:
                pl.semaphore_wait(s.free.at[p], 1)
                s.todo[-1].add(p)
            core().start()

        def open_up():
            core().wait_send()
            opened.append(u)
            if len(opened) == units:
                for i, d in enumerate(me.others()):
                    signal(s.ready.at[p, i], d)

        def second():
            s.arrived(u, 0, s.RC.at[p % s.slots, :, :, :, :, cols])

            def add(i, carry):
                own = G.at[g, i // 4, me.c, i % 4, :, :, cols]
                got = s.RC.at[p % s.slots, i // 4, i % 4, :, :, cols]
                own[...] = (own[...].astype(jnp.float32) + got[...].astype(jnp.float32)).astype(jnp.bfloat16)
                return carry

            lax.fori_loop(0, 8, add, 0)
            if not added:
                for i in range(5):
                    pl.semaphore_wait(s.ready.at[p, i], 1)
            added.append(u)
            hop(0)
            if len(added) == units and p + s.slots < s.count:
                signal(s.free.at[p + s.slots], me.core())

        def later(k):
            land(k)
            if k < 2:
                hop(k + 1)

        s.todo.setdefault(-1, set())
        return [first, open_up, second] + [functools.partial(later, k) for k in range(3)]

WIDTH = 768
DEC = 128
ENC = 512
SEQS = 2
HERE = (4, 8, SEQS, DEC, ENC, WIDTH)
CHUNKS = (2, 2, 4, 2)
TROWS = 16
SLOTS = 4
OWN = WIDTH // 32
PAIRS = WIDTH // 128
HALF = WIDTH // 2
BLK = 256
RD = SEQS * DEC
RE = SEQS * ENC
GELU = math.sqrt(2.0 / math.pi)
PLACE = (9, 8, 10, 11, 4, 7, 5, 6)
GATHERED = (
    (1, 0, 128, "zxy"),
    (1, 128, 512, "zyx"),
    (1, 640, 128, "zyx"),
    (2, 0, 384, "zxy"),
    (2, 384, 256, "yzx"),
    (2, 640, 128, "zyx"),
    (3, 0, 128, "zxy"),
    (3, 128, 384, "zxy"),
    (3, 512, 256, "zyx"),
    (4, 0, 512, "xzy"),
    (4, 512, 128, "zxy"),
    (4, 640, 128, "zyx"),
    (5, 0, 256, "zyx"),
    (5, 256, 256, "xzy"),
    (5, 512, 256, "xzy"),
    (6, 0, 384, "yzx"),
    (6, 384, 256, "zyx"),
    (6, 640, 128, "xzy"),
    (7, 0, 256, "zxy"),
    (7, 256, 128, "yxz"),
    (7, 384, 384, "zyx"),
    (8, 0, 256, "zxy"),
    (8, 256, 256, "xyz"),
    (8, 512, 256, "zyx"),
)
REDUCED = (
    (0, 0, 512, "xyz"),
    (0, 512, 256, "yxz"),
    (1, 0, 512, "xyz"),
    (1, 512, 128, "yxz"),
    (1, 640, 128, "zxy"),
    (2, 0, 384, "xyz"),
    (2, 384, 256, "yxz"),
    (2, 640, 128, "zxy"),
    (3, 0, 640, "yxz"),
    (3, 640, 128, "zxy"),
    (4, 0, 384, "xyz"),
    (4, 384, 256, "yxz"),
    (4, 640, 128, "zyx"),
    (5, 0, 384, "xyz"),
    (5, 384, 256, "yxz"),
    (5, 640, 128, "zyx"),
    (6, 0, 256, "xyz"),
    (6, 256, 384, "yxz"),
    (6, 640, 128, "zxy"),
    (7, 0, 512, "xyz"),
    (7, 512, 256, "yxz"),
)
PLAN = (
    240, 90, 100, 110, 2000, 0, 10, 20, 60, 70, 80, 241, 91, 101, 111, 242,
    1, 102, 30, 243, 40, 50, 112, 2, 244, 2001, 11, 21, 41, 61, 103, 113,
    2002, 3, 104, 114, 71, 4, 62, 81, 12, 22, 72, 63, 64, 82, 150, 160,
    170, 92, 31, 180, 13, 51, 73, 190, 200, 120, 130, 140, 151, 23, 14, 74,
    24, 2003, 42, 2004, 161, 83, 171, 84, 181, 32, 93, 131, 141, 52, 191, 201,
    94, 162, 121, 210, 220, 230, 43, 44, 182, 53, 33, 192, 54, 152, 34, 2005,
    172, 202, 2006, 221, 122, 163, 2007, 2008, 2009, 2010, 132, 164, 2011, 2012, 2013, 2014,
    183, 2015, 2016, 142, 153, 173, 2017, 2018, 222, 211, 184, 2019, 231, 154, 174, 2020,
    2021, 2022, 133, 203, 2023, 2024, 2025, 193, 134, 143, 204, 123, 194, 144, 232, 124,
    2026, 212, 2027, 2028, 2029, 1000, 1010, 1001, 223, 1011, 233, 213, 224, 1002, 234, 1012,
    214, 2030, 2031, 2032, 2033, 1020, 1030, 1040, 2034, 2035, 2036, 1021, 1031, 2037, 1013, 1050,
    1060, 1070, 1080, 1090, 1041, 2038, 1051, 2039, 1061, 1022, 1071, 1032, 1042, 1003, 1052, 1062,
    1072, 1014, 1081, 1091, 2040, 2041, 2042, 1033, 2043, 1082, 1092, 2044, 1004, 1043, 2045, 2046,
    2047, 1063, 1023, 2048, 2049, 2050, 1073, 1100, 1110, 1120, 2051, 1015, 1101, 2052, 1053, 1111,
    1121, 2053, 1034, 1044, 1102, 1130, 1140, 1150, 1112, 1064, 1093, 1074, 1131, 1141, 1122, 1151,
    2054, 1083, 1005, 1132, 1035, 1142, 1152, 2055, 1065, 2056, 1024, 1103, 2057, 1094, 2058, 1054,
    1045, 1123, 2059, 2060, 2061, 1160, 1170, 1180, 2062, 1084, 1075, 1113, 1190, 1200, 1161, 1153,
    1171, 1181, 2063, 1191, 1201, 1162, 1172, 1143, 1182, 1025, 1133, 1192, 1202, 2064, 2065, 1055,
    1095, 1154, 1104, 1114, 1124, 2066, 2067, 2068, 1163, 2069, 1085, 1144, 1173, 1210, 1211, 1183,
    1134, 1212, 1105, 1193, 1155, 1203, 1115, 1125, 1145, 1164, 1174, 1184, 1213, 1135, 1194, 1204,
    1185, 1214, 1165, 1175, 1195, 1205, 1215,
)


def bucket_rows():
    table = bucket_table(DEC, NB)[:, 0]
    far = table[(-np.arange(DEC)) % DEC]
    rows = np.full((8, TROWS), -1)
    rows[:, 4:8] = np.arange(NB).reshape(8, 4)
    return jnp.asarray((rows.reshape(-1, 1) == far[None, :]).astype(np.float32), jnp.bfloat16)


def sem_rows(gathered, reduced):
    deep = [max(gathered.count(p), reduced.count(p)) for p in range(NP)]

    def rows(pieces):
        return [sum(deep[:p]) + pieces[:i].count(p) for i, p in enumerate(pieces)] + [sum(deep)]

    return rows(gathered), rows(reduced), sum(deep)


def loop(n, body):
    def step(i, carry):
        body(i)
        return carry

    lax.fori_loop(0, n, step, 0)


def tile(i, n):
    return pl.ds(pl.multiple_of(i * n, n), n)


def f32(v):
    return v.astype(jnp.float32)


def layer_kernel(
    dlen, elen, dec_hbm, enc_hbm, cot_hbm, small, bmap,
    sq, sk, sv, so, cq, ck, cv, co, fi, fo,
    out_hbm, gdec_hbm, genc_hbm, gw, gt,
    BUF, T, GT, RCT, RC,
    X, C, E, K, V, A1, Q1, K1, V1, O1, A2, Q2, O2, A3, GO, HID, GP,
    Y1, Y2, F2, GY, PS, PC, BIAS, NRM, DM,
    ss, rs, ready, free, tready, tfree, lsem,
):
    me = Place()
    greet(me)
    loads = [
        pltpu.make_async_copy(a, b, lsem.at[i])
        for i, (a, b) in enumerate(((dec_hbm, X), (cot_hbm, C), (enc_hbm, E)))
    ]
    for cp in loads:
        cp.start()

    def pack(p, top, bottom):
        both = jnp.concatenate([f32(top), f32(bottom)], axis=0)
        BUF[p + 1, me.y, me.c, me.z, me.x] = low(both)

    pack(0, sq[...], sk[...])
    pack(1, sv[...], so[...])
    pack(2, ck[...], cv[...])
    pack(3, cq[...], co[...])
    BUF[5, me.y, me.c, me.z, me.x] = fo[0:48]
    BUF[6, me.y, me.c, me.z, me.x] = fo[48:96]
    for h in range(2):
        pack(6 + h, fi[:, 1536 * h : 1536 * h + 768], fi[:, 1536 * h + 768 : 1536 * h + 1536])
    T[0, me.y, me.c, me.z, me.x] = small[...]
    all_here()

    def first_lanes(shape):
        return lax.broadcasted_iota(jnp.int32, shape, 1) < 64

    def two(v):
        keep = first_lanes(v.shape)
        w = f32(v)
        return low(jnp.concatenate([jnp.where(keep, w, 0.0), jnp.where(keep, 0.0, w)], axis=0))

    def one(v):
        return jnp.where(first_lanes((DEC, 128)), v[:DEC], v[DEC:])

    def unpack(src, dst):
        def body(i):
            for z in range(4):
                w = f32(BUF[src, i // 2, i % 2, z])
                for k in range(2):
                    rows = slice(OWN * k, OWN * k + OWN)
                    both = low(jnp.concatenate([w[0, rows], w[1, rows]], axis=0))
                    BUF[dst, k, i // 2, (i % 2) * 2 + z // 2, z % 2] = both

        loop(4, body)

    def whole(b, k):
        return BUF[b, k].reshape(WIDTH, WIDTH)

    def rows_of(i):
        return slice(i * RD, i * RD + RD) if isinstance(i, int) else tile(i, RD)

    def project(a, b, k, dst, i=0):
        r = rows_of(i)
        dst[r, :] = low(dot_nn(a[r, :], whole(b, k)))

    def project_add(a, b, k, base, dst):
        dst[...] = f32(base[...]) + dot_nn(a[...], whole(b, k))

    def norm(v, gain, dst):
        def body(i):
            r = tile(i, 128)
            x = f32(v[r, :])
            s = lax.rsqrt(jnp.mean(x * x, axis=-1, keepdims=True) + EPSILON)
            dst[r, :] = low(x * s * NRM[gain : gain + 1, :])

        loop(RD // 128, body)

    def norm_back(v, gain, G, base, dst):
        def body(i, total):
            r = tile(i, 64)
            x = f32(v[r, :])
            s = lax.rsqrt(jnp.mean(x * x, axis=-1, keepdims=True) + EPSILON)
            n = x * s
            w = G[r, :]
            u = w * NRM[gain : gain + 1, :]
            dst[r, :] = f32(base[r, :]) + s * (u - n * jnp.mean(u * n, axis=-1, keepdims=True))
            return total + jnp.sum((w * n).reshape(8, 8, WIDTH), axis=0)

        total = lax.fori_loop(0, RD // 64, body, jnp.zeros((8, WIDTH), jnp.float32))
        return jnp.sum(total, axis=0, keepdims=True)

    def softmax(s):
        e = jnp.exp(s - jnp.max(s, axis=-1, keepdims=True))
        return e * (1.0 / jnp.sum(e, axis=-1, keepdims=True))

    def attend(q, k, v, o, probs, slots, mask, lo, hi):
        def body(j):
            i = j + lo
            lanes = tile(i, 128)
            for at in range(SEQS):
                r, kr = slice(at * DEC, at * DEC + DEC), slice(at * slots, at * slots + slots)
                s = dot_nt(two(q[r, lanes]), k[kr, lanes])
                p = low(softmax(mask(s, at, i)))
                probs[i, at] = p
                o[r, lanes] = low(one(dot_nn(p, v[kr, lanes])))

        loop(hi - lo, body)

    def attend_back(q, k, v, go, probs, slots, lo, hi, extra):
        def body(j):
            i = j + lo
            lanes = tile(i, 128)
            for at in range(SEQS):
                r, kr = slice(at * DEC, at * DEC + DEC), slice(at * slots, at * slots + slots)
                q2, g2, p = two(q[r, lanes]), two(go[r, lanes]), probs[i, at]
                d = dot_nt(g2, v[kr, lanes])
                pf = f32(p)
                gs = low(pf * (d - jnp.sum(pf * d, axis=-1, keepdims=True)))
                v[kr, lanes] = low(dot_tn(p, g2))
                q[r, lanes] = low(one(dot_nn(gs, k[kr, lanes])))
                k[kr, lanes] = low(dot_tn(gs, q2))
                extra(gs, i)

        loop(hi - lo, body)

    def back_project(pairs, dst, cast, i=0):
        r = rows_of(i)
        v = None
        for a, b, k in pairs:
            d = dot_nt(a[r, :], whole(b, k))
            v = d if v is None else v + d
        dst[r, :] = cast(v)

    def grad_pair(aa, ga, ab, gb, place, oa=0, ob=0, tiles=(0, 1, 2)):
        for n in tiles:
            va = dot_tn(aa[...], ga[:, (n + oa) * BLK : (n + oa + 1) * BLK]).reshape(32, OWN, BLK)
            vb = dot_tn(ab[...], gb[:, (n + ob) * BLK : (n + ob + 1) * BLK]).reshape(32, OWN, BLK)
            both = low(jnp.concatenate([va, vb], axis=1))
            BUF[place, :, :, :, :, :, n * BLK : (n + 1) * BLK] = both.reshape(2, 2, 4, 2, ROWS, BLK)

    owner = jnp.floor((f32(lax.broadcasted_iota(jnp.int32, (1, WIDTH), 1)) + 0.5) * (1.0 / OWN))

    def spread():
        place = f32(lax.broadcasted_iota(jnp.int32, (128, WIDTH), 1)) - OWN * owner
        return low(jnp.where(place == f32(lax.broadcasted_iota(jnp.int32, (128, WIDTH), 0)), 1.0, 0.0))

    row = f32(lax.broadcasted_iota(jnp.int32, (32 * TROWS, 1), 0)) - TROWS * owner
    def self_mask(s, at, pair):
        k = lax.broadcasted_iota(jnp.int32, s.shape, 1)
        q = lax.broadcasted_iota(jnp.int32, s.shape, 0) % DEC
        return jnp.where((k <= q) & (k < dlen[at]), s + BIAS[pair], MASKED)

    def cross_mask(s, at, pair):
        return jnp.where(lax.broadcasted_iota(jnp.int32, s.shape, 1) < elen[at], s, MASKED)

    def out_rows(j):
        return jnp.concatenate([BUF[b, j // 2, j % 2] for b in (5, 6)], axis=2).reshape(WIDTH, WIDTH)

    def feed(j, b):
        k = j % 2
        pre = dot_nn(A3[...], whole(b, k))
        gh = dot_nt(C[...], out_rows(j))
        th = jnp.tanh(GELU * (pre + 0.044715 * (pre * pre * pre)))
        HID[:, j * WIDTH : (j + 1) * WIDTH] = low(0.5 * pre * (1.0 + th))
        slope = 0.5 * (1.0 + th) + 0.5 * pre * (1.0 - th * th) * (GELU * (1.0 + 0.134145 * (pre * pre)))
        GP[:, j * WIDTH : (j + 1) * WIDTH] = low(slope * gh)

    def feed_grads(j):
        for n in range(3):
            w = low(dot_tn(HID[:, j * WIDTH : (j + 1) * WIDTH], C[:, n * BLK : (n + 1) * BLK]))
            w = w.reshape(4, 2, 2 * ROWS, BLK)
            for e in range(2):
                part = w[:, :, ROWS * e : ROWS * e + ROWS]
                BUF[PLACE[2 + e], j // 2, j % 2, :, :, :, n * BLK : (n + 1) * BLK] = part

    def mix_back(j, b):
        d = dot_nt(GP[:, j * WIDTH : (j + 1) * WIDTH], whole(b, j % 2))
        F2[...] = d if j == 0 else F2[...] + d

    def mix():
        v = Y2[...]
        for j in range(4):
            v = v + dot_nn(HID[:, j * WIDTH : (j + 1) * WIDTH], out_rows(j))
        A3[...] = low(v)


    def cast_rows(src, dst):
        def body(i):
            q = tile(i, 64)
            dst[q, :] = low(src[q, :])

        loop(RD // 64, body)

    def nothing(gs, pair):
        pass

    def sum_bias(gs, pair):
        BIAS[pair] += f32(gs)

    def done(*pieces):
        g.drain([u for u, unit in enumerate(GATHERED) if unit[0] - 1 in pieces])

    stores, gains = [], {}

    def store(src, dst, i):
        stores.append(pltpu.make_async_copy(src, dst, lsem.at[i]))
        stores[-1].start()

    def init():
        for cp in loads:
            cp.wait()
        place = lax.broadcasted_iota(jnp.int32, (DEC, WIDTH), 0)
        for s in range(SEQS):
            r = slice(DEC * s, DEC * s + DEC)
            C[r, :] = low(jnp.where(place < dlen[s], f32(C[r, :]), 0.0))

    def tables():
        h.drain()
        table = T[0].reshape(32 * TROWS, 128)
        wide = dot_nn(table, spread())
        NRM[...] = jnp.concatenate(
            [jnp.sum(jnp.where(row == float(n), wide, 0.0), axis=0, keepdims=True) for n in range(3)]
            + [jnp.zeros((5, WIDTH), jnp.float32)],
            axis=0,
        )
        DM[...] = dot_tn(T[0, 0, 0].reshape(8 * TROWS, 128), bmap[...])
        for j in range(2 * PAIRS):
            v = jnp.broadcast_to(DM[j : j + 1, :], (DEC, DEC))
            BIAS[j // 2, DEC * (j % 2) : DEC * (j % 2) + DEC, :] = pltpu.roll(v, 0, 1, stride=1, stride_axis=0)

    def unpack_to(src, dst, *pieces):
        done(*pieces)
        unpack(src, dst)

    def self_out():
        project_add(O1, 1, 1, X, Y1)
        norm(Y1, 1, A2)

    def cross_out():
        project_add(O2, 3, 1, Y1, Y2)
        norm(Y2, 2, A3)

    def in_grads(h):
        if h:
            done(4, 5, 7)
        grad_pair(A3, GP, A3, GP, PLACE[h], 6 * h, 6 * h + 3)

    def finish():
        mix()
        store(A3, out_hbm, 0)

    def norm_back_ffn():
        gains[2] = norm_back(Y2, 2, F2, C, GY)
        cast_rows(GY, C)

    def norm_back_cross():
        gains[1] = norm_back(Y1, 1, F2, GY, GY)
        cast_rows(GY, C)
        BIAS[...] = jnp.zeros_like(BIAS)

    def norm_back_self():
        gains[0] = norm_back(X, 0, F2, GY, GY)
        cast_rows(GY, GO)
        store(GO, gdec_hbm, 1)

    def enc_grad(i):
        loop(2, lambda n: back_project([(K, 2, 0), (V, 2, 1)], E, low, n + 2 * i))
        if i:
            store(E, genc_hbm, 2)

    def small_grads():
        DM[...] = jnp.zeros_like(DM)
        flip = lax.broadcasted_iota(jnp.int32, (DEC, DEC), 0) + lax.broadcasted_iota(jnp.int32, (DEC, DEC), 1)
        flip = low(jnp.where(flip == DEC - 1, 1.0, 0.0))
        for j in range(2 * PAIRS):
            v = BIAS[j // 2, DEC * (j % 2) : DEC * (j % 2) + DEC, :]
            hi = low(v)
            v = dot_nn(flip, hi) + dot_nn(flip, low(v - f32(hi)))
            v = pltpu.roll(v, 0, 1, stride=1, stride_axis=0)
            DM[j : j + 1, :] = jnp.sum(v, axis=0, keepdims=True)
        DM[...] = pltpu.roll(DM[...], 1, 1)
        hi = low(DM[...])
        rel = dot_nt(bmap[...], hi) + dot_nt(bmap[...], low(DM[...] - f32(hi)))
        spots = sum(jnp.where(row == float(n), gains[n], 0.0) for n in range(3))
        spots = dot_nt(low(spots), spread()).reshape(4, 128, 128)
        for d in range(4):
            GT[0, d // 2, d % 2] = low(spots[d] + rel).reshape(4, 2, TROWS, 128)

    def many(n, fn, each=1):
        return [functools.partial(fn, i // each) if i % each == 0 else int for i in range(n)]

    work = [
        init,
        tables,
        lambda: norm(X, 0, A1),
        lambda: (unpack(1, 0), project(A1, 0, 0, Q1)),
        lambda: project(A1, 0, 1, K1),
        lambda: (unpack_to(2, 1, 0), project(A1, 1, 0, V1)),
        *many(3, lambda i: attend(Q1, K1, V1, O1, PS, DEC, self_mask, 0, 6), 3),
        self_out,
        *many(4, lambda i: (None if i else unpack_to(3, 2, 1), loop(2, lambda n: project(E, 2, 0, K, n + 2 * i))), 2),
        *many(4, lambda i: loop(2, lambda n: project(E, 2, 1, V, n + 2 * i)), 2),
        lambda: (unpack_to(4, 3, 2), project(A2, 3, 0, Q2)),
        *many(6, lambda i: attend(Q2, K, V, O2, PC, ENC, cross_mask, 3 * i, 3 * i + 3), 3),
        cross_out,
        lambda: unpack_to(7, 4, 3),
        *many(2, lambda i: feed(i, 4)),
        lambda: in_grads(0),
        lambda: unpack_to(8, 7, 6),
        *many(2, lambda i: feed(2 + i, 7)),
        lambda: in_grads(1),
        *many(4, feed_grads),
        *many(4, lambda j: mix_back(j, 4 if j < 2 else 7)),
        norm_back_ffn,
        lambda: back_project([(C, 3, 1)], GO, low),
        *many(6, lambda i: attend_back(Q2, K, V, GO, PC, ENC, 3 * i, 3 * i + 3, nothing), 3),
        lambda: grad_pair(A2, Q2, O2, C, PLACE[4]),
        *many(3, lambda n: grad_pair(E, K, E, V, PLACE[5], tiles=(n,))),
        finish,
        lambda: back_project([(Q2, 3, 0)], F2, f32),
        norm_back_cross,
        lambda: back_project([(C, 1, 1)], GO, low),
        *many(3, lambda i: attend_back(Q1, K1, V1, GO, PS, DEC, 0, 6, sum_bias), 3),
        lambda: grad_pair(A1, V1, O1, C, PLACE[6]),
        lambda: grad_pair(A1, Q1, A1, K1, PLACE[7]),
        *many(4, enc_grad, 2),
        lambda: back_project([(Q1, 0, 0), (K1, 0, 1), (V1, 1, 0)], F2, f32),
        norm_back_self,
        small_grads,
    ]
    rows_g, rows_r, last = sem_rows([unit[0] - 1 for unit in GATHERED], [unit[0] for unit in REDUCED])
    g = Gather(me, BUF, ss, rs, rows_g)
    h = Gather(me, T, ss, rs, rows_g)
    r = Reduce(me, BUF, RC, gw, ss, rs, rows_r, ready, free, SLOTS, NP)
    rt = Reduce(me, GT, RCT, gt, ss, rs, rows_r, tready, tfree, 1, 1)
    na, nr = len(GATHERED), len(REDUCED)
    gathers = [g.steps(u, *unit) for u, unit in enumerate(GATHERED)] + [h.steps(na, 0, 0, 128, "zyx")]
    parts = [sum(unit[0] == p for unit in REDUCED) for p in range(NP)]
    reduces = [r.steps(u, p, PLACE[p], *cut, parts[p]) for u, (p, *cut) in enumerate(REDUCED)]
    reduces.append(rt.steps(nr, 0, 0, 0, 128, "xyz", 1))
    for code in PLAN:
        if code >= 2000:
            work[code - 2000]()
        else:
            (reduces if code >= 1000 else gathers)[code % 1000 // 10][code % 10]()
    g.drain()
    h.drain()
    r.drain()
    rt.drain()
    for cp in stores:
        cp.wait()


def layer_here(shards, dec_in, enc_out, dec_len, enc_len, cotangent):
    ns, sq, sk, sv, so, rel, nc, cq, ck, cv, co, nf, fi, fo = shards
    gains = jnp.pad(jnp.stack([ns, nc, nf]), ((0, 1), (0, 128 - OWN)))
    small = jnp.concatenate([gains, jnp.pad(rel, ((0, 8), (0, 128 - rel.shape[1])))], axis=0)
    b16, w32 = jnp.bfloat16, jnp.float32

    def vm(shape, dtype=b16):
        return pltpu.VMEM(shape, dtype)

    dec, enc = (RD, WIDTH), (RE, WIDTH)
    scratch = [
        vm((12, *CHUNKS, ROWS, COLS)),
        vm((1, *CHUNKS, TROWS, 128)),
        vm((1, *CHUNKS, TROWS, 128)),
        vm((1, 2, 4, 2, TROWS, 128)),
        vm((SLOTS, 2, 4, 2, ROWS, COLS)),
        vm(dec), vm(dec), vm(enc), vm(enc), vm(enc),
        *[vm(dec)] * 10,
        *[vm((RD, 4 * WIDTH))] * 2,
        *[vm(dec, w32)] * 4,
        vm((PAIRS, SEQS, 2 * DEC, DEC)),
        vm((PAIRS, SEQS, 2 * DEC, ENC)),
        vm((PAIRS, 2 * DEC, DEC), w32),
        vm((8, WIDTH), w32),
        vm((128, 128), w32),
        *[pltpu.SemaphoreType.DMA((sem_rows([u[0] - 1 for u in GATHERED], [u[0] for u in REDUCED])[2] + 1, 6))] * 2,
        pltpu.SemaphoreType.REGULAR((NP, 5)),
        pltpu.SemaphoreType.REGULAR((NP,)),
        pltpu.SemaphoreType.REGULAR((1, 5)),
        pltpu.SemaphoreType.REGULAR((1,)),
        pltpu.SemaphoreType.DMA((3,)),
    ]
    here, away = pl.BlockSpec(memory_space=pltpu.VMEM), pl.BlockSpec(memory_space=pl.ANY)
    scalars = pl.BlockSpec(memory_space=pltpu.SMEM)
    out, g_dec, g_enc, gw, gt = pl.pallas_call(
        layer_kernel,
        out_shape=(
            jax.ShapeDtypeStruct(dec, b16),
            jax.ShapeDtypeStruct(dec, b16),
            jax.ShapeDtypeStruct(enc, b16),
            jax.ShapeDtypeStruct((NP, ROWS, COLS), w32),
            jax.ShapeDtypeStruct((1, TROWS, 128), w32),
        ),
        in_specs=[scalars] * 2 + [away] * 3 + [here] * 12,
        out_specs=[away] * 3 + [here] * 2,
        scratch_shapes=scratch,
        compiler_params=pltpu.CompilerParams(
            collective_id=0, has_side_effects=True, vmem_limit_bytes=60 * 2**20
        ),
    )(
        dec_len.reshape(-1), enc_len.reshape(-1),
        dec_in.reshape(dec), enc_out.reshape(enc), cotangent.reshape(dec),
        small, bucket_rows(), sq, sk, sv, so, cq, ck, cv, co, fi, fo,
    )
    return deliver(out, g_dec, g_enc, gw, gt, rel.shape)


def deliver_kernel(out, gdec, genc, gw, gt, o0, o1, o2, *outs):
    grads, (w_fi, w_fo, n1, n2, n3, rel, sem) = outs[:8], outs[8:]
    moves = [(out, o0), (gdec, o1), (genc, o2)]
    at = ((7, 0), (7, 1), (6, 0), (6, 1), (4, 0), (5, 0), (5, 1), (4, 1))
    moves += [(gw.at[p, pl.ds(OWN * h, OWN)], o) for (p, h), o in zip(at, grads)]
    for j in range(4):
        moves.append((gw.at[j // 2, pl.ds(OWN * (j % 2), OWN)], w_fi.at[:, pl.ds(WIDTH * j, WIDTH)]))
    moves += [(gw.at[2 + e], w_fo.at[pl.ds(ROWS * e, ROWS)]) for e in range(2)]
    copies = [pltpu.make_async_copy(a, b, sem.at[i]) for i, (a, b) in enumerate(moves)]
    for cp in copies:
        cp.start()
    for n, o in enumerate((n1, n2, n3)):
        o[...] = gt[0, n : n + 1, :OWN]
    rel[...] = gt[0, 4 : 4 + rel.shape[0], : rel.shape[1]]
    for cp in copies:
        cp.wait()


def deliver(out, g_dec, g_enc, gw, gt, rel):
    here, away = pl.BlockSpec(memory_space=pltpu.VMEM), pl.BlockSpec(memory_space=pl.ANY)
    w32 = [(OWN, WIDTH)] * 8 + [(OWN, 4 * WIDTH), (2 * ROWS, WIDTH)] + [(1, OWN)] * 3 + [rel]
    got = pl.pallas_call(
        deliver_kernel,
        out_shape=[jax.ShapeDtypeStruct(v.shape, v.dtype) for v in (out, g_dec, g_enc)]
        + [jax.ShapeDtypeStruct(v, jnp.float32) for v in w32],
        in_specs=[away] * 4 + [here],
        out_specs=[here] * 17,
        scratch_shapes=[pltpu.SemaphoreType.DMA((17,))],
    )(out, g_dec, g_enc, gw, gt)
    sq, sk, sv, so, cq, ck, cv, co, w_fi, w_fo, n1, n2, n3, w_rel = got[3:]
    n1, n2, n3 = (v.reshape(-1) for v in (n1, n2, n3))
    return got[0], got[1], got[2], (n1, sq, sk, sv, so, w_rel, n2, cq, ck, cv, co, n3, w_fi, w_fo)


EPSILON = 1e-06
MASKED = -1000000000.0
NB = 32
AT = ("dp", "fsdp")


def bucket_table(dec_slots, bucket_count):
    near = bucket_count // 2
    places = np.arange(dec_slots, dtype=np.int32)
    distance = np.maximum(places[:, None] - places[None, :], 0).astype(np.int32)
    edges = np.array(
        [math.ceil(near * (128 / near) ** (level / near) - 1e-09) for level in range(1, near)],
        dtype=np.int32,
    )
    far = near + np.sum(
        (distance[:, :, None] >= edges[None, None, :]).astype(np.int32), axis=-1, dtype=np.int32
    )
    return np.where(distance < near, distance, far).astype(np.int32)


def rms_norm(values, gain):
    return values * lax.rsqrt(jnp.mean(values * values, axis=-1, keepdims=True) + EPSILON) * gain


def smooth(values):
    return jax.nn.gelu(values, approximate=True)


def dot_nn(a, b):
    return jnp.dot(a, b, preferred_element_type=jnp.float32)


def dot_nt(a, b):
    return lax.dot_general(a, b, (((1,), (1,)), ((), ())), preferred_element_type=jnp.float32)


def dot_tn(a, b):
    return lax.dot_general(a, b, (((0,), (0,)), ((), ())), preferred_element_type=jnp.float32)


def low(v):
    return v.astype(jnp.bfloat16)


def layer_plain(weights, dec_rows, enc_rows, dec_len, enc_len, cot_rows):
    ns, sq, sk, sv, so, rel, nc, cq, ck, cv, co, nf, fi, fo = weights
    seqs, dec_slots, width = dec_rows.shape
    enc_slots = enc_rows.shape[1]
    heads = rel.shape[1]
    size = width // heads
    ns, nc, nf = (v.astype(jnp.float32) for v in (ns, nc, nf))
    places = jnp.arange(dec_slots, dtype=jnp.int32)
    causal = places[None, :] <= places[:, None]
    self_mask = causal[None, None] & (places[None, None, None, :] < dec_len[:, None, None, None])
    enc_places = jnp.arange(enc_slots, dtype=jnp.int32)
    cross_mask = enc_places[None, None, None, :] < enc_len[:, None, None, None]
    row_mask = (places[None, :] < dec_len[:, None]).astype(jnp.float32)
    table = bucket_table(dec_slots, NB).reshape(-1)
    onehot = jnp.asarray((table[:, None] == np.arange(NB)[None, :]).astype(np.float32), jnp.bfloat16)
    bias = lax.dot_general(rel, onehot, (((0,), (1,)), ((), ())), preferred_element_type=jnp.float32)
    bias = bias.reshape(heads, dec_slots, dec_slots)[None]

    def split(t):
        return t.reshape(seqs, -1, heads, size).transpose(0, 2, 1, 3)

    def join(t):
        return t.transpose(0, 2, 1, 3).reshape(-1, width)

    def many(a, b, ca, cb):
        return lax.dot_general(
            a, b, (((ca,), (cb,)), ((0, 1), (0, 1))), preferred_element_type=jnp.float32
        )

    def attend(q, k, v, add, mask):
        s = jnp.where(mask, many(q, k, 3, 3) + add, MASKED)
        top = jnp.max(s, axis=-1, keepdims=True)
        e = jnp.exp(s - top)
        p = e / jnp.sum(e, axis=-1, keepdims=True)
        return p, low(many(low(p), v, 3, 2))

    def back(q, k, v, p, g):
        gv = low(many(low(p), g, 2, 2))
        d = many(g, v, 3, 3)
        gs = low(p * (d - jnp.sum(p * d, axis=-1, keepdims=True)))
        return low(many(gs, k, 3, 2)), low(many(gs, q, 2, 2)), gv, gs

    x = dec_rows.reshape(-1, width).astype(jnp.float32)
    enc = enc_rows.reshape(-1, width)
    a1 = low(rms_norm(x, ns))
    q1, k1, v1 = (split(low(dot_nn(a1, w))) for w in (sq, sk, sv))
    p1, o1 = attend(q1, k1, v1, bias, self_mask)
    o1 = join(o1)
    y1 = x + dot_nn(o1, so)
    a2 = low(rms_norm(y1, nc))
    q2 = split(low(dot_nn(a2, cq)))
    k2, v2 = (split(low(dot_nn(enc, w))) for w in (ck, cv))
    p2, o2 = attend(q2, k2, v2, 0.0, cross_mask)
    o2 = join(o2)
    y2 = y1 + dot_nn(o2, co)
    a3 = low(rms_norm(y2, nf))
    pre = dot_nn(a3, fi)
    hidden = low(smooth(pre))
    out = y2 + dot_nn(hidden, fo)
    g = (cot_rows.astype(jnp.float32) * row_mask[:, :, None]).reshape(-1, width)
    gf = low(g)
    w_fo = dot_tn(hidden, gf)
    gp = low(jax.vjp(smooth, pre)[1](dot_nt(gf, fo))[0])
    w_fi = dot_tn(a3, gp)
    part, w_nf = jax.vjp(rms_norm, y2, nf)[1](dot_nt(gp, fi))
    gy = g + part
    gc = low(gy)
    w_co = dot_tn(o2, gc)
    gq, gk, gv, _ = back(q2, k2, v2, p2, split(low(dot_nt(gc, co))))
    gq, gk, gv = join(gq), join(gk), join(gv)
    w_cq, w_ck, w_cv = dot_tn(a2, gq), dot_tn(enc, gk), dot_tn(enc, gv)
    g_enc = dot_nt(gk, ck) + dot_nt(gv, cv)
    part, w_nc = jax.vjp(rms_norm, y1, nc)[1](dot_nt(gq, cq))
    gy = gy + part
    ga = low(gy)
    w_so = dot_tn(o1, ga)
    gq, gk, gv, gs = back(q1, k1, v1, p1, split(low(dot_nt(ga, so))))
    w_rel = lax.dot_general(
        onehot, gs.reshape(seqs, heads, -1), (((0,), (2,)), ((), ())), preferred_element_type=jnp.float32
    ).sum(axis=1)
    gq, gk, gv = join(gq), join(gk), join(gv)
    w_sq, w_sk, w_sv = dot_tn(a1, gq), dot_tn(a1, gk), dot_tn(a1, gv)
    part, w_ns = jax.vjp(rms_norm, x, ns)[1](dot_nt(gq, sq) + dot_nt(gk, sk) + dot_nt(gv, sv))
    grads = (w_ns, w_sq, w_sk, w_sv, w_so, w_rel, w_nc, w_cq, w_ck, w_cv, w_co, w_nf, w_fi, w_fo)
    return low(out), low(gy + part), low(g_enc), grads


REL = 5


def on_device(dec_in, enc_out, dec_len, enc_len, cotangent, *shards):
    micro, per, dec_slots, width = dec_in.shape
    seqs, enc_slots = micro * per, enc_out.shape[2]
    if (lax.axis_size("dp"), lax.axis_size("fsdp"), seqs, dec_slots, enc_slots, width) == HERE:
        out, g_dec, g_enc, grads = layer_here(shards, dec_in, enc_out, dec_len, enc_len, cotangent)
    else:
        whole = [lax.all_gather(w, AT[1] if i == REL else AT, axis=0, tiled=True) for i, w in enumerate(shards)]
        out, g_dec, g_enc, grads = layer_plain(
            whole,
            dec_in.reshape(seqs, dec_slots, width),
            enc_out.reshape(seqs, enc_slots, width),
            dec_len.reshape(-1),
            enc_len.reshape(-1),
            cotangent.reshape(seqs, dec_slots, width),
        )
        grads = [
            lax.psum_scatter(
                lax.psum(w, AT[0]) if i == REL else w,
                AT[1] if i == REL else AT,
                scatter_dimension=0,
                tiled=True,
            )
            for i, w in enumerate(grads)
        ]
    return (out.reshape(dec_in.shape), g_dec.reshape(dec_in.shape), g_enc.reshape(enc_out.shape), *grads)


def solution(mesh):
    rows, seq = P(AT, None), P(None, AT, None, None)
    gain, lens, rel = P(AT), P(None, AT), P(AT[1], None)
    placed = (gain, rows, rows, rows, rows, rel, gain, rows, rows, rows, rows, gain, rows, rows)
    return jax.shard_map(
        on_device,
        mesh=mesh,
        in_specs=(seq, seq, lens, lens, seq, *placed),
        out_specs=(seq, seq, seq, *placed),
        check_vma=False,
    )
```
